32 devices in a mesh: ctx: 8 (over z, x), wt: 4 (over y, core).
Axes of the slice: x: 2, y: 2, z: 4, core: 2. Of those that a mesh axis runs over, the one named last changes fastest.
Arguments:
- tokens: bfloat16 [8192, 1024], P('ctx'), may hold values from -6 to 6
- flags: int32 [8192], P('ctx'), may hold values from 0 to 1, as said below
- w_query: bfloat16 [1024, 1024], P(None, 'wt'), may hold values from -0.1875 to 0.1875
- w_key: bfloat16 [1024, 1024], P(None, 'wt'), may hold values from -0.1875 to 0.1875
- w_value: bfloat16 [1024, 1024], P(None, 'wt'), may hold values from -0.1875 to 0.1875
- w_out: bfloat16 [1024, 1024], P(None, 'wt'), may hold values from -2 to 2
- w_up: bfloat16 [1024, 4096], P(None, 'wt'), may hold values from -0.1875 to 0.1875
- w_down: bfloat16 [1024, 4096], P(None, 'wt'), may hold values from -0.09375 to 0.09375
- bias_query: float32 [1024], P('wt'), may hold values from -3 to 3
- bias_value: float32 [1024], P('wt'), may hold values from -3 to 3
- bias_out: float32 [1024], replicated, may hold values from -3 to 3
- mid_gain: float32 [1024], replicated, may hold values from 0.25 to 1.75
- mid_bias: float32 [1024], replicated, may hold values from -3 to 3
- bias_up: float32 [4096], P('wt'), may hold values from -3 to 3
- bias_down: float32 [1024], replicated, may hold values from -3 to 3
- end_gain: float32 [1024], replicated, may hold values from 0.25 to 1.75
- end_bias: float32 [1024], replicated, may hold values from -3 to 3
- cotangent: bfloat16 [8192, 1024], P('ctx'), may hold values from -6 to 6
Outputs:
- layer_out: bfloat16 [8192, 1024], P(('ctx', 'wt'))
- input_grad: float32 [8192, 1024], P(('ctx', 'wt'))
- grad_w_query: float32 [1024, 1024], P('ctx', 'wt')
- grad_w_key: float32 [1024, 1024], P('ctx', 'wt')
- grad_w_value: float32 [1024, 1024], P('ctx', 'wt')
- grad_w_out: float32 [1024, 1024], P('ctx', 'wt')
- grad_w_up: float32 [1024, 4096], P('ctx', 'wt')
- grad_w_down: float32 [1024, 4096], P('ctx', 'wt')
- grad_bias_query: float32 [1024], P('wt')
- grad_bias_value: float32 [1024], P('wt')
- grad_bias_out: float32 [1024], replicated
- grad_mid_gain: float32 [1024], replicated
- grad_mid_bias: float32 [1024], replicated
- grad_bias_up: float32 [4096], P('wt')
- grad_bias_down: float32 [1024], replicated
- grad_end_gain: float32 [1024], replicated
- grad_end_bias: float32 [1024], replicated
The draws below stay inside these ranges and needn't reach their ends.
Inputs may be any that keep to these rules, and one draw needn't show every extreme that they name: flags is 1 at the first token; consecutive document starts lie at most 512 apart and the last document has at most 512 tokens; some document has exactly 512 tokens.
All inputs are finite; a program needn't handle non-finite values.
Results may differ from the reference program's by a relative error of at most 0.014.
Values may be sent and summed in bfloat16 or wider, within the bound.
No kernel may reach another device: no remote copies, remote signals or barrier semaphores. Data moves between devices by JAX's collectives and lax.ppermute only.
A program may use at most 192 MiB of HBM per device.

```python
import math
import jax
import jax.numpy as jnp
from jax import lax

D = 1024
HEADS = 16
HEAD_DIM = 64
FF = 4096
MAXDOC = 512
BQ = 512
TOKENS = 8192


def draw_flags(key, part):
    key = jax.random.fold_in(key, 11)
    first_key, second_key = jax.random.split(key)
    lengths = jax.random.randint(first_key, (TOKENS,), 1, MAXDOC + 1)
    chosen = jax.random.randint(second_key, (), 0, TOKENS // MAXDOC - 2)
    lengths = jnp.where(jnp.arange(TOKENS) == chosen, MAXDOC, lengths)
    starts = jnp.cumsum(lengths) - lengths
    return jnp.zeros((TOKENS,), jnp.int32).at[starts].set(1, mode='drop')


def block_scale(rng, shape, cuts, low, top_value):
    def one(axis_at, blocks):
        steps = jax.random.uniform(jax.random.fold_in(jax.random.fold_in(rng, 6), axis_at), (blocks,), jnp.float32, low / len(cuts), top_value / len(cuts))
        return jnp.repeat(jnp.exp(steps), shape[axis_at] // blocks).reshape((-1,) + (1,) * (len(shape) - axis_at - 1))

    level = one(*cuts[0])
    for cut in cuts[1:]:
        level = level * one(*cut)
    return level


def scatter_about(stream_key, dims, width, most, cuts=(), kind=jnp.bfloat16):
    drawn = width * jax.random.normal(stream_key, dims, jnp.float32)
    if cuts:
        drawn = drawn * block_scale(stream_key, dims, cuts, -0.22, 0.18)
    return jnp.clip(drawn, -most, most).astype(kind)


def setup_inputs(seed: int = 0) -> dict:
    splits = jax.random.split(jax.random.key(seed), 19)
    tokens = scatter_about(splits[0], (TOKENS, D), 1.0, 6.0, ((0, 8),))
    flags = draw_flags(jax.random.fold_in(splits[18], 71), 0)
    w_query = scatter_about(splits[2], (D, HEADS * HEAD_DIM), D ** -0.5, 0.1875, ((1, 4),))
    w_key = scatter_about(splits[3], (D, HEADS * HEAD_DIM), D ** -0.5, 0.1875, ((1, 4),))
    w_value = scatter_about(splits[4], (D, HEADS * HEAD_DIM), D ** -0.5, 0.1875, ((1, 4),))
    w_out = scatter_about(splits[5], (D, HEADS * HEAD_DIM), (max(1, HEADS * HEAD_DIM * 4 // MAXDOC)) ** -0.5, 2.0, ((1, 4),))
    w_up = scatter_about(splits[6], (D, FF), D ** -0.5, 0.1875, ((1, 4),))
    w_down = scatter_about(splits[7], (D, FF), FF ** -0.5, 0.09375, ((1, 4),))
    bias_query = scatter_about(splits[8], (HEADS * HEAD_DIM,), 0.5, 3.0, ((0, 4),), jnp.float32)
    bias_value = scatter_about(splits[9], (HEADS * HEAD_DIM,), 0.5, 3.0, ((0, 4),), jnp.float32)
    bias_out = scatter_about(splits[10], (D,), 0.5, 3.0, (), jnp.float32)
    mid_gain = jnp.clip(1.0 + 0.15 * jax.random.normal(splits[11], (D,), jnp.float32), 0.25, 1.75)
    mid_bias = scatter_about(splits[12], (D,), 0.5, 3.0, (), jnp.float32)
    bias_up = scatter_about(splits[13], (FF,), 0.5, 3.0, ((0, 4),), jnp.float32)
    bias_down = scatter_about(splits[14], (D,), 0.5, 3.0, (), jnp.float32)
    end_gain = jnp.clip(1.0 + 0.15 * jax.random.normal(splits[15], (D,), jnp.float32), 0.25, 1.75)
    end_bias = scatter_about(splits[16], (D,), 0.5, 3.0, (), jnp.float32)
    cotangent = scatter_about(splits[17], (TOKENS, D), 1.0, 6.0, ((0, 8),))
    return dict(tokens=tokens, flags=flags, w_query=w_query, w_key=w_key, w_value=w_value, w_out=w_out, w_up=w_up, w_down=w_down, bias_query=bias_query, bias_value=bias_value, bias_out=bias_out, mid_gain=mid_gain, mid_bias=mid_bias, bias_up=bias_up, bias_down=bias_down, end_gain=end_gain, end_bias=end_bias, cotangent=cotangent)


@jax.custom_vjp
def low(v):
    return lax.optimization_barrier(v.astype(jnp.bfloat16)).astype(jnp.float32)

@jax.custom_vjp
def low_back(v):
    return v

def low_keep(v):
    return (low(v), None)

def low_pass(kept, grad):
    return (grad,)

def back_keep(v):
    return (v, None)

def back_low(kept, grad):
    return (low(grad),)
low.defvjp(low_keep, low_pass)
low_back.defvjp(back_keep, back_low)

def product(left, right):
    return jnp.dot(left, right, precision=lax.Precision.HIGHEST)

def right_transposed(left, right):
    return lax.dot_general(left, right, (((1,), (1,)), ((), ())), precision=lax.Precision.HIGHEST)

def normalized(value):
    average = lax.optimization_barrier(jnp.mean(value, axis=-1, keepdims=True))
    centred = value - average
    variance = lax.optimization_barrier(jnp.mean(centred * centred, axis=-1, keepdims=True))
    return centred * lax.rsqrt(variance + 1e-12)

def gelu_exact(value):
    return 0.5 * value * (1.0 + jax.scipy.special.erf(value * 0.7071067811865476))

def attention(queries, key_rows, value_rows, segments):
    row_total = queries.shape[0]
    head_width = queries.shape[1]
    head_count = head_width // HEAD_DIM
    scaling = HEAD_DIM ** (-0.5)
    window = BQ + 2 * MAXDOC
    wide_keys = jnp.pad(key_rows, ((MAXDOC, MAXDOC), (0, 0)))
    wide_values = jnp.pad(value_rows, ((MAXDOC, MAXDOC), (0, 0)))
    wide_segs = jnp.pad(segments, (MAXDOC, MAXDOC), constant_values=-1)

    def block(block_index):
        start = block_index * BQ
        query_block = lax.dynamic_slice_in_dim(queries, start, BQ, 0).reshape(BQ, head_count, HEAD_DIM)
        near_keys = lax.dynamic_slice_in_dim(wide_keys, start, window, 0).reshape(window, head_count, HEAD_DIM)
        near_values = lax.dynamic_slice_in_dim(wide_values, start, window, 0).reshape(window, head_count, HEAD_DIM)
        own_segs = lax.dynamic_slice_in_dim(segments, start, BQ, 0)
        near_segs = lax.dynamic_slice_in_dim(wide_segs, start, window, 0)
        raw = jnp.einsum('qhd,khd->hqk', query_block, near_keys, precision=lax.Precision.HIGHEST) * scaling
        scores = low_back(raw)
        allowed = (own_segs[:, None] == near_segs[None, :])[None]
        masked = jnp.where(allowed, scores, -1e+30)
        peak = lax.optimization_barrier(jnp.max(masked, axis=-1, keepdims=True))
        weights = jnp.exp(masked - peak)
        probs = weights / lax.optimization_barrier(jnp.sum(weights, axis=-1, keepdims=True))
        mixed = jnp.einsum('hqk,khd->qhd', low(probs), near_values, precision=lax.Precision.HIGHEST)
        return mixed.reshape(BQ, head_width)
    blocks = lax.map(jax.checkpoint(block), jnp.arange(row_total // BQ, dtype=jnp.int32))
    return blocks.reshape(row_total, head_width)

def reference(tokens, flags, w_query, w_key, w_value, w_out, w_up, w_down, bias_query, bias_value, bias_out, mid_gain, mid_bias, bias_up, bias_down, end_gain, end_bias, cotangent):
    segments = jnp.cumsum(flags).astype(jnp.int32)
    row_total = tokens.shape[0]
    rows_each = math.gcd(row_total, 4096)
    pieces = row_total // rows_each

    def forward(inputs, wq_f, wk_f, wv_f, wo_f, wu_f, wd_f, bq_f, bv_f, bo_f, gain_one, shift_one, bu_f, bd_f, gain_two, shift_two):
        queries = low_back(low(product(inputs, wq_f) + bq_f))
        key_rows = low_back(low(product(inputs, wk_f)))
        value_rows = low_back(low(product(inputs, wv_f) + bv_f))
        attended = attention(queries, key_rows, value_rows, segments)

        def rows_part(pair):
            rows_in, rows_att = pair
            mixed = low_back(right_transposed(low_back(low(rows_att)), wo_f) + bo_f)
            first_out = normalized(rows_in + mixed) * gain_one + shift_one
            inner = low_back(product(low(first_out), wu_f) + bu_f)
            hidden = low(gelu_exact(inner))
            second = low_back(right_transposed(hidden, wd_f) + bd_f)
            return normalized(first_out + second) * gain_two + shift_two
        outs = lax.map(jax.checkpoint(rows_part), (inputs.reshape(pieces, rows_each, -1), attended.reshape(pieces, rows_each, -1)))
        return outs.reshape(row_total, -1)
    floats = (tokens.astype(jnp.float32), w_query.astype(jnp.float32), w_key.astype(jnp.float32), w_value.astype(jnp.float32), w_out.astype(jnp.float32), w_up.astype(jnp.float32), w_down.astype(jnp.float32), bias_query.astype(jnp.float32), bias_value.astype(jnp.float32), bias_out.astype(jnp.float32), mid_gain.astype(jnp.float32), mid_bias.astype(jnp.float32), bias_up.astype(jnp.float32), bias_down.astype(jnp.float32), end_gain.astype(jnp.float32), end_bias.astype(jnp.float32))
    layer, pullback = jax.vjp(forward, *floats)
    grads = pullback(cotangent.astype(jnp.float32))
    return (layer.astype(jnp.bfloat16), grads[0], grads[1], grads[2], grads[3], grads[4], grads[5], grads[6], grads[7], grads[8], grads[9], grads[10], grads[11], grads[12], grads[13], grads[14], grads[15])
```

```python
import functools
import jax
import jax.numpy as jnp
from jax import lax
from jax.experimental import pallas as pl
from jax.experimental.pallas import tpu as pltpu

HEAD_DIM = 64
MAXDOC = 512
TILE = 256
HALO = MAXDOC // TILE
SCALE = HEAD_DIM ** -0.5
LOG2E = 1.4426950408889634
NEG = -1e30
F32 = jnp.float32
BF16 = jnp.bfloat16
VMEM_LIMIT = 56 * 1024 * 1024


def dot_nt(left, right):
    return lax.dot_general(left, right, (((1,), (1,)), ((), ())), preferred_element_type=F32)


def dot_nn(left, right):
    return lax.dot_general(left, right, (((1,), (0,)), ((), ())), preferred_element_type=F32)


def rows_of(index):
    return pl.ds(pl.multiple_of(index * TILE, TILE), TILE)


def meet(seg_sm, a, b):
    return jnp.logical_and(
        seg_sm[a * TILE] <= seg_sm[b * TILE + TILE - 1],
        seg_sm[a * TILE + TILE - 1] >= seg_sm[b * TILE],
    )


def fill(scratch, low, own, high):
    rows = own.shape[0]
    scratch[0:MAXDOC, :] = low[...]
    scratch[MAXDOC : MAXDOC + rows, :] = own[...]
    scratch[MAXDOC + rows :, :] = high[...]


def spread_segments(seg_row, seg_col, blocks):
    for b in range(blocks):
        piece = seg_row[:, b * TILE : (b + 1) * TILE]
        seg_col[b * TILE : (b + 1) * TILE, :] = jnp.broadcast_to(piece, (128, TILE)).T


def head_mask(value, head):
    lane = lax.broadcasted_iota(jnp.int32, value.shape, 1)
    mine = (lane < HEAD_DIM) if head % 2 == 0 else (lane >= HEAD_DIM)
    return jnp.where(mine, value, jnp.zeros_like(value))


def pair_cols(head):
    return slice((head // 2) * 128, (head // 2) * 128 + 128)


def attn_fwd_kernel(
    heads, blocks,
    seg_sm, seg_row, q_ref, kl_ref, k_ref, kr_ref, vl_ref, v_ref, vr_ref,
    att_ref, lse_ref,
    kx, vt, seg_col, m_ref, l_ref, acc_ref,
):
    step = pl.program_id(0)

    @pl.when(step == 0)
    def _():
        fill(kx, kl_ref, k_ref, kr_ref)
        rows = v_ref.shape[0]
        vt[:, 0:MAXDOC] = vl_ref[...].T
        vt[:, MAXDOC : MAXDOC + rows] = v_ref[...].T
        vt[:, MAXDOC + rows :] = vr_ref[...].T
        spread_segments(seg_row, seg_col, blocks + 2 * HALO)

    own = step + HALO
    seg_q = seg_row[:, rows_of(own)]

    def tile(kb, first):
        ks = rows_of(kb)
        seg_k = seg_col[ks, :]
        allowed = jnp.concatenate([seg_k, seg_k], axis=1) == seg_q
        for head in range(heads):
            q_masked = head_mask(q_ref[:, pair_cols(head)], head)
            s = dot_nt(kx[ks, pair_cols(head)], q_masked) * (SCALE * LOG2E)
            s = jnp.where(allowed, s, NEG)
            peak = jnp.max(s, axis=0, keepdims=True)
            hrow = slice(head, head + 1)
            hd = slice(head * HEAD_DIM, (head + 1) * HEAD_DIM)
            if first:
                p = jnp.exp2(s - peak)
                m_ref[hrow, :] = peak
                l_ref[hrow, :] = jnp.sum(p, axis=0, keepdims=True)
                acc_ref[hd, :] = dot_nn(vt[hd, ks], p.astype(BF16))
            else:
                before = m_ref[hrow, :]
                top = jnp.maximum(before, peak)
                p = jnp.exp2(s - top)
                keep = jnp.exp2(before - top)
                m_ref[hrow, :] = top
                l_ref[hrow, :] = l_ref[hrow, :] * keep + jnp.sum(p, axis=0, keepdims=True)
                acc_ref[hd, :] = acc_ref[hd, :] * keep + dot_nn(vt[hd, ks], p.astype(BF16))

    tile(own, True)

    def other(i, _):
        kb = step + i

        @pl.when(jnp.logical_and(i != HALO, meet(seg_sm, kb, own)))
        def _():
            tile(kb, False)

        return 0

    lax.fori_loop(0, 2 * HALO + 1, other, 0)
    for head in range(heads):
        hrow = slice(head, head + 1)
        hd = slice(head * HEAD_DIM, (head + 1) * HEAD_DIM)
        total = l_ref[hrow, :]
        acc_ref[hd, :] = acc_ref[hd, :] * (1.0 / total)
        lse_ref[hrow, :] = m_ref[hrow, :] + jnp.log2(total)
    att_ref[...] = acc_ref[...].T.astype(BF16)


def whole(shape):
    return pl.BlockSpec(shape, lambda i: (0,) * len(shape))


def attention_forward(seg, q, k_parts, v_parts):
    rows, width = q.shape
    heads = width // HEAD_DIM
    blocks = rows // TILE
    ext = rows + 2 * MAXDOC
    kv_specs = [whole((MAXDOC, width)), whole((rows, width)), whole((MAXDOC, width))]
    return pl.pallas_call(
        functools.partial(attn_fwd_kernel, heads, blocks),
        grid=(blocks,),
        in_specs=[
            pl.BlockSpec(memory_space=pltpu.SMEM),
            whole((1, ext)),
            pl.BlockSpec((TILE, width), lambda i: (i, 0)),
            *kv_specs,
            *kv_specs,
        ],
        out_specs=[
            pl.BlockSpec((TILE, width), lambda i: (i, 0)),
            pl.BlockSpec((heads, TILE), lambda i: (0, i)),
        ],
        out_shape=[
            jax.ShapeDtypeStruct((rows, width), BF16),
            jax.ShapeDtypeStruct((heads, rows), F32),
        ],
        scratch_shapes=[
            pltpu.VMEM((ext, width), BF16),
            pltpu.VMEM((width, ext), BF16),
            pltpu.VMEM((ext, 128), jnp.int32),
            pltpu.VMEM((heads, TILE), F32),
            pltpu.VMEM((heads, TILE), F32),
            pltpu.VMEM((width, TILE), F32),
        ],
        compiler_params=pltpu.CompilerParams(vmem_limit_bytes=VMEM_LIMIT),
        cost_estimate=pl.CostEstimate(
            flops=4 * rows * 3 * TILE * width, bytes_accessed=8 * rows * width * 2, transcendentals=0
        ),
        name="attention_forward",
    )(seg, seg[None, :], q, *k_parts, *v_parts)


def attn_bwd_kernel(
    heads, blocks,
    seg_sm, seg_row,
    ql_ref, q_ref, qr_ref, dl_ref, d_ref, dr_ref, al_ref, a_ref, ar_ref, ll_ref, l_ref, lr_ref,
    kl_ref, k_ref, kr_ref, vl_ref, v_ref, vr_ref,
    dq_ref, dk_ref, dv_ref,
    qx, dx, lx, delta, kx, vx, seg_col, dqt, dk_acc, dv_acc,
):
    step = pl.program_id(0)
    ext_blocks = blocks + 2 * HALO

    @pl.when(step == 0)
    def _():
        fill(qx, ql_ref, q_ref, qr_ref)
        fill(dx, dl_ref, d_ref, dr_ref)
        fill(kx, kl_ref, k_ref, kr_ref)
        fill(vx, vl_ref, v_ref, vr_ref)
        rows = q_ref.shape[0]
        lx[:, 0:MAXDOC] = ll_ref[...]
        lx[:, MAXDOC : MAXDOC + rows] = l_ref[...]
        lx[:, MAXDOC + rows :] = lr_ref[...]
        spread_segments(seg_row, seg_col, ext_blocks)
        width = q_ref.shape[1]
        col = lax.broadcasted_iota(jnp.int32, (8, width), 1) // HEAD_DIM
        row = lax.broadcasted_iota(jnp.int32, (8, width), 0)
        pick = (col == row).astype(F32)

        def per_head(d, a):
            product = d[...].astype(F32) * a[...].astype(F32)
            return lax.dot_general(
                pick, product, (((1,), (1,)), ((), ())),
                preferred_element_type=F32, precision=lax.Precision.HIGHEST,
            )

        delta[:, 0:MAXDOC] = per_head(dl_ref, al_ref)
        delta[:, MAXDOC : MAXDOC + rows] = per_head(d_ref, a_ref)
        delta[:, MAXDOC + rows :] = per_head(dr_ref, ar_ref)
        dqt[...] = jnp.zeros_like(dqt)

    dk_acc[...] = jnp.zeros_like(dk_acc)
    dv_acc[...] = jnp.zeros_like(dv_acc)
    ks = rows_of(step)
    seg_k = seg_col[ks, :]
    k_own = jnp.logical_and(step >= HALO, step < HALO + blocks)
    kt = kx[ks, :].T

    def tile(qb):
        qs = rows_of(qb)
        allowed = jnp.concatenate([seg_k, seg_k], axis=1) == seg_row[:, qs]
        for head in range(heads):
            pair = pair_cols(head)
            hd = slice(head * HEAD_DIM, (head + 1) * HEAD_DIM)
            s = dot_nt(head_mask(kx[ks, pair], head), qx[qs, pair])
            p = jnp.exp2(s * (SCALE * LOG2E) - lx[head : head + 1, qs])
            p = jnp.where(allowed, p, 0.0)
            dp = dot_nt(head_mask(vx[ks, pair], head), dx[qs, pair])
            ds = (p * (dp - delta[head : head + 1, qs])).astype(BF16)
            dv_acc[head] += dot_nn(p.astype(BF16), dx[qs, pair])
            dk_acc[head] += dot_nn(ds, qx[qs, pair])
            dqt[hd, qs] += dot_nn(kt[hd, :], ds)

    def other(i, _):
        qb = step + i - HALO
        inside = jnp.logical_and(qb >= 0, qb < ext_blocks)
        q_own = jnp.logical_and(qb >= HALO, qb < HALO + blocks)
        safe = jnp.clip(qb, 0, ext_blocks - 1)
        wanted = jnp.logical_and(inside, jnp.logical_or(q_own, k_own))

        @pl.when(jnp.logical_and(wanted, meet(seg_sm, safe, step)))
        def _():
            tile(safe)

        return 0

    lax.fori_loop(0, 2 * HALO + 1, other, 0)

    @pl.when(k_own)
    def _():
        lane = lax.broadcasted_iota(jnp.int32, (TILE, 128), 1)
        for pair in range(heads // 2):
            cols = slice(pair * 128, pair * 128 + 128)
            low = lane < HEAD_DIM
            dk = jnp.where(low, dk_acc[2 * pair], dk_acc[2 * pair + 1]) * SCALE
            dk_ref[:, cols] = dk.astype(BF16)
            dv_ref[:, cols] = jnp.where(low, dv_acc[2 * pair], dv_acc[2 * pair + 1]).astype(BF16)

    @pl.when(step == ext_blocks - 1)
    def _():
        for b in range(blocks):
            piece = dqt[:, MAXDOC + b * TILE : MAXDOC + (b + 1) * TILE]
            dq_ref[b * TILE : (b + 1) * TILE, :] = (piece * SCALE).T.astype(BF16)


def attention_backward(seg, q_parts, d_parts, a_parts, lse_parts, k_parts, v_parts):
    rows, width = q_parts[1].shape
    heads = width // HEAD_DIM
    blocks = rows // TILE
    ext = rows + 2 * MAXDOC
    specs = [whole((MAXDOC, width)), whole((rows, width)), whole((MAXDOC, width))]
    lse_specs = [whole((heads, MAXDOC)), whole((heads, rows)), whole((heads, MAXDOC))]
    own_block = pl.BlockSpec((TILE, width), lambda i: (jnp.clip(i - HALO, 0, blocks - 1), 0))
    return pl.pallas_call(
        functools.partial(attn_bwd_kernel, heads, blocks),
        grid=(blocks + 2 * HALO,),
        in_specs=[
            pl.BlockSpec(memory_space=pltpu.SMEM),
            whole((1, ext)),
            *specs, *specs, *specs, *lse_specs, *specs, *specs,
        ],
        out_specs=[whole((rows, width)), own_block, own_block],
        out_shape=[jax.ShapeDtypeStruct((rows, width), BF16)] * 3,
        scratch_shapes=[
            pltpu.VMEM((ext, width), BF16),
            pltpu.VMEM((ext, width), BF16),
            pltpu.VMEM((heads, ext), F32),
            pltpu.VMEM((8, ext), F32),
            pltpu.VMEM((ext, width), BF16),
            pltpu.VMEM((ext, width), BF16),
            pltpu.VMEM((ext, 128), jnp.int32),
            pltpu.VMEM((width, ext), F32),
            pltpu.VMEM((heads, TILE, 128), F32),
            pltpu.VMEM((heads, TILE, 128), F32),
        ],
        compiler_params=pltpu.CompilerParams(vmem_limit_bytes=VMEM_LIMIT),
        cost_estimate=pl.CostEstimate(
            flops=10 * rows * 3 * TILE * width, bytes_accessed=16 * rows * width * 2, transcendentals=0
        ),
        name="attention_backward",
    )(seg, seg[None, :], *q_parts, *d_parts, *a_parts, *lse_parts, *k_parts, *v_parts)


from jax.sharding import PartitionSpec as P


def swap(value, axis, mask):
    return lax.ppermute(value, axis, [(i, i ^ mask) for i in range(lax.axis_size(axis))])


def neighbours(value_low, value_high, axis):
    count = lax.axis_size(axis)
    forward = [(i, i + 1) for i in range(count - 1)]
    backward = [(i + 1, i) for i in range(count - 1)]
    return lax.ppermute(value_high, axis, forward), lax.ppermute(value_low, axis, backward)


def halo(value, axis):
    return neighbours(value[:MAXDOC], value[value.shape[0] - MAXDOC :], axis)


def dot_tn(left, right):
    return lax.dot_general(left, right, (((0,), (0,)), ((), ())), preferred_element_type=F32)


def scatter_sum(part, axis, order):
    count = lax.axis_size(axis)
    bits = count.bit_length() - 1
    index = lax.axis_index(axis)
    rows = part.shape[0] // count
    value = part.reshape((2,) * bits + (rows, part.shape[1]))
    left = list(range(bits - 1, -1, -1))
    for bit in order:
        dim = left.index(bit)
        mine = (index >> bit) & 1
        keep = lax.dynamic_index_in_dim(value, mine, dim, keepdims=False)
        give = lax.dynamic_index_in_dim(value, 1 - mine, dim, keepdims=False)
        got = swap(give.astype(BF16), axis, 1 << bit)
        value = keep.astype(F32) + got.astype(F32)
        left.pop(dim)
    return value


def everywhere_sum(value, axis):
    count = lax.axis_size(axis)
    for bit in range(count.bit_length() - 1):
        value = value + swap(value, axis, 1 << bit)
    return value


def moments(value):
    average = jnp.mean(value, axis=-1, keepdims=True)
    centred = value - average
    variance = jnp.mean(centred * centred, axis=-1, keepdims=True)
    scale = lax.rsqrt(variance + 1e-12)
    return centred * scale, scale


def norm_back(grad, normal, scale):
    return scale * (
        grad
        - jnp.mean(grad, axis=-1, keepdims=True)
        - normal * jnp.mean(grad * normal, axis=-1, keepdims=True)
    )


def gelu_both(value):
    half = 0.5 * (1.0 + lax.erf(value * 0.7071067811865476))
    slope = half + value * jnp.exp(-0.5 * value * value) * 0.3989422804014327
    return value * half, slope


def body(
    tokens, flags, w_query, w_key, w_value, w_out, w_up, w_down, bias_query, bias_value, bias_out,
    mid_gain, mid_bias, bias_up, bias_down, end_gain, end_bias, cotangent,
):
    rows, width = tokens.shape
    quarter = rows // 4
    slot = lax.axis_index("wt")
    core = slot & 1
    side = slot >> 1
    ctx_count = lax.axis_size("ctx")
    ctx = lax.axis_index("ctx")
    bits = list(range(ctx_count.bit_length() - 1))

    def split(value):
        parts = value.reshape((2, 2, quarter) + value.shape[1:])
        shape = (2 * quarter,) + value.shape[1:]
        mine = lax.dynamic_index_in_dim(parts, core, 1, keepdims=False).reshape(shape)
        other = lax.dynamic_index_in_dim(parts, 1 - core, 1, keepdims=False).reshape(shape)
        return mine, other

    def mine_of(value):
        return split(value)[0]

    def join(mine, other):
        shape = (2, 1, quarter) + mine.shape[1:]
        a, b = mine.reshape(shape), other.reshape(shape)
        first = jnp.where(core == 0, a, b)
        second = jnp.where(core == 0, b, a)
        return jnp.concatenate([first, second], axis=1).reshape((rows,) + mine.shape[1:])

    def in_order(place, own, far):
        return jnp.concatenate(
            [jnp.where(place == 0, own, far), jnp.where(place == 0, far, own)], axis=1
        )

    def final(mine):
        return lax.dynamic_slice_in_dim(mine, side * quarter, quarter, 0)

    def core_gather(value):
        return swap(value, "wt", 1)

    def across(value):
        return swap(value, "wt", 2)

    def both_sides(mine_part, other_part):
        got = swap(other_part.astype(BF16), "wt", 1)
        chip = (mine_part + got.astype(F32)).astype(BF16)
        return chip.astype(F32) + across(chip).astype(F32)

    flags_low, flags_high = halo(flags, "ctx")
    after = jnp.arange(MAXDOC) == 0
    flags_high = jnp.where(jnp.logical_and(ctx == ctx_count - 1, after), 1, flags_high)
    seg = jnp.cumsum(jnp.concatenate([flags_low, flags, flags_high])).astype(jnp.int32)

    queries = (dot_nn(tokens, w_query) + bias_query).astype(BF16)
    key_rows = dot_nn(tokens, w_key).astype(BF16)
    value_rows = (dot_nn(tokens, w_value) + bias_value).astype(BF16)
    pairs = jnp.concatenate([key_rows, value_rows], axis=1)
    pairs_low, pairs_high = halo(pairs, "ctx")
    head_width = queries.shape[1]
    k_parts = (pairs_low[:, :head_width], key_rows, pairs_high[:, :head_width])
    v_parts = (pairs_low[:, head_width:], value_rows, pairs_high[:, head_width:])

    w_chip = in_order(core, w_out, core_gather(w_out))
    w_out_whole = in_order(side, w_chip, across(w_chip))

    attended, peaks = attention_forward(seg, queries, k_parts, v_parts)
    att_mine, att_other = split(attended)
    att_chip = in_order(core, att_mine, core_gather(att_other))
    att_whole = in_order(side, att_chip, across(att_chip))
    q_att_low, q_att_high = halo(jnp.concatenate([queries, attended], axis=1), "ctx")
    peaks_low, peaks_high = neighbours(peaks[:, :MAXDOC], peaks[:, rows - MAXDOC :], "ctx")

    first_sum = mine_of(tokens).astype(F32) + dot_nt(att_whole, w_out_whole) + bias_out
    first_norm, first_scale = moments(first_sum)
    first_out = first_norm * mid_gain + mid_bias
    low_mine = first_out.astype(BF16)
    low_other = core_gather(low_mine)
    first_low = jnp.concatenate([low_mine, low_other], axis=0)
    activated, slope = gelu_both(dot_nn(first_low, w_up) + bias_up)
    hidden = activated.astype(BF16)
    slope = slope.astype(BF16)
    half = 2 * quarter
    second_sum = first_out + both_sides(
        dot_nt(hidden[:half], w_down), dot_nt(hidden[half:], w_down)
    ) + bias_down

    second_norm, second_scale = moments(second_sum)
    layer_out = final(second_norm * end_gain + end_bias).astype(BF16)
    upstream = mine_of(cotangent).astype(F32)
    grad_end_gain = jnp.sum(upstream * second_norm, axis=0)
    grad_end_bias = jnp.sum(upstream, axis=0)
    d_second = norm_back(upstream * end_gain, second_norm, second_scale)
    down_mine = d_second.astype(BF16)
    grad_bias_down = jnp.sum(down_mine.astype(F32), axis=0)
    d_down = jnp.concatenate([down_mine, core_gather(down_mine)], axis=0)
    grad_w_down = dot_tn(d_down, hidden).astype(BF16)
    d_inner = (dot_nn(d_down, w_down) * slope.astype(F32)).astype(BF16)
    grad_bias_up = jnp.sum(d_inner.astype(F32), axis=0)
    grad_w_up = dot_tn(first_low, d_inner).astype(BF16)
    d_first = d_second + both_sides(dot_nt(d_inner[:half], w_up), dot_nt(d_inner[half:], w_up))
    summed_down = scatter_sum(grad_w_down, "ctx", bits)
    summed_up = scatter_sum(grad_w_up, "ctx", bits[1:] + bits[:1])

    grad_mid_gain = jnp.sum(d_first * first_norm, axis=0)
    grad_mid_bias = jnp.sum(d_first, axis=0)
    d_first_sum = norm_back(d_first * mid_gain, first_norm, first_scale)
    mixed_mine = d_first_sum.astype(BF16)
    grad_bias_out = jnp.sum(mixed_mine.astype(F32), axis=0)
    mixed_other = core_gather(mixed_mine)
    d_mixed = join(mixed_mine, mixed_other)
    d_attended = dot_nn(d_mixed, w_out).astype(BF16)
    grad_w_out = dot_tn(d_mixed, attended).astype(BF16)

    d_low, d_high = halo(d_attended, "ctx")
    d_queries, d_keys, d_values = attention_backward(
        seg,
        (q_att_low[:, :head_width], queries, q_att_high[:, :head_width]),
        (d_low, d_attended, d_high),
        (q_att_low[:, head_width:], attended, q_att_high[:, head_width:]),
        (peaks_low, peaks, peaks_high),
        k_parts,
        v_parts,
    )
    summed_out = scatter_sum(grad_w_out, "ctx", bits)
    summed_query = scatter_sum(dot_tn(tokens, d_queries).astype(BF16), "ctx", bits)
    summed_key = scatter_sum(dot_tn(tokens, d_keys).astype(BF16), "ctx", bits[1:] + bits[:1])
    summed_value = scatter_sum(dot_tn(tokens, d_values).astype(BF16), "ctx", bits[1:] + bits[:1])

    input_part = (
        dot_nt(d_queries, w_query) + dot_nt(d_keys, w_key) + dot_nt(d_values, w_value)
    )
    part_mine, part_other = split(input_part)
    chip = part_mine + swap(part_other.astype(BF16), "wt", 1).astype(F32)
    far = lax.dynamic_slice_in_dim(chip, (1 - side) * quarter, quarter, 0).astype(BF16)
    input_grad = final(chip) + across(far).astype(F32) + final(d_first_sum)

    shared = jnp.stack(
        [grad_end_gain, grad_end_bias, grad_bias_down, grad_mid_gain, grad_mid_bias, grad_bias_out]
    )
    shared = shared + core_gather(shared)
    early = everywhere_sum(jnp.concatenate([shared, grad_bias_up.reshape(-1, width)]), "ctx")
    late = everywhere_sum(
        jnp.stack(
            [jnp.sum(d_queries.astype(F32), axis=0), jnp.sum(d_values.astype(F32), axis=0)]
        ),
        "ctx",
    )
    return (
        layer_out,
        input_grad,
        summed_query,
        summed_key,
        summed_value,
        summed_out,
        summed_up,
        summed_down,
        late[0],
        late[1],
        early[5],
        early[3],
        early[4],
        early[6:].reshape(-1),
        early[2],
        early[0],
        early[1],
    )


def solution(mesh):
    wt = P(None, "wt")
    in_specs = (
        P("ctx", None), P("ctx"), wt, wt, wt, wt, wt, wt, P("wt"), P("wt"),
        P(), P(), P(), P("wt"), P(), P(), P(), P("ctx", None),
    )
    rows = P(("ctx", "wt"), None)
    both = P("ctx", "wt")
    out_specs = (
        rows, rows, both, both, both, both, both, both, P("wt"), P("wt"),
        P(), P(), P(), P("wt"), P(), P(), P(),
    )
    return jax.shard_map(body, mesh=mesh, in_specs=in_specs, out_specs=out_specs, check_vma=False)
```

```python
import functools

import jax
import jax.numpy as jnp
from jax import lax
from jax.experimental import pallas as pl
from jax.experimental.pallas import tpu as pltpu
from jax.sharding import PartitionSpec as P

HEAD_DIM = 64
MAXDOC = 512
TILE = 256
HALO = MAXDOC // TILE
SCALE = HEAD_DIM ** -0.5
SCORE = SCALE * 1.4426950408889634
NEG = -1e30
F32 = jnp.float32
BF16 = jnp.bfloat16
MIB = 1024 * 1024
EXTRA = 16


def dot_nt(left, right):
    return lax.dot_general(left, right, (((1,), (1,)), ((), ())), preferred_element_type=F32)


def dot_nn(left, right):
    return lax.dot_general(left, right, (((1,), (0,)), ((), ())), preferred_element_type=F32)


VMEM = pl.BlockSpec(memory_space=pltpu.VMEM)
SMEM = pl.BlockSpec(memory_space=pltpu.SMEM)
HBM = pl.BlockSpec(memory_space=pltpu.HBM)
HBM_OR_VMEM = pl.BlockSpec(memory_space=pl.ANY)


class Order:
    def __init__(self):
        self.last = ()
        self.held = []

    def hold(self, *arrays):
        self.held += arrays

    def free(self, *arrays):
        self.held = [h for h in self.held if not any(h is a for a in arrays)]


def call(order, name, fn, outs, args, scratch=(), specs=None, limit=16, waits=()):
    held = [h for h in order.held if not any(h is a for a in args)]
    tokens = (*order.last, *waits, *held)
    count = len(tokens) + len(args) + len(outs)

    def kernel(*refs):
        refs[count][...] = jnp.zeros((8, 128), F32)
        fn(*refs[len(tokens) : count], *refs[count + 1 :])

    results = pl.pallas_call(
        kernel,
        in_specs=[HBM_OR_VMEM] * len(tokens) + ([VMEM] * len(args) if specs is None else specs),
        out_specs=[o[2] if len(o) > 2 else VMEM for o in outs] + [VMEM],
        out_shape=[jax.ShapeDtypeStruct(o[0], o[1]) for o in outs] + [jax.ShapeDtypeStruct((8, 128), F32)],
        scratch_shapes=list(scratch),
        compiler_params=pltpu.CompilerParams(vmem_limit_bytes=limit * MIB),
        cost_estimate=pl.CostEstimate(flops=1, bytes_accessed=1, transcendentals=0),
        name=name,
    )(*tokens, *args)
    order.last = (results[-1],)
    return results[:-1]


def position():
    slot, ctx = lax.axis_index("wt"), lax.axis_index("ctx")
    return slot & 1, slot >> 1, ctx, ctx == lax.axis_size("ctx") - 1


def running_count(marks):
    lane = lax.broadcasted_iota(jnp.int32, marks.shape, 1)
    reach = 1
    while reach < marks.shape[1]:
        marks = marks + jnp.where(lane >= reach, pltpu.roll(marks, reach, 1), 0)
        reach *= 2
    return marks


def keys_kernel(tok_hbm, wk_hbm, wv_hbm, bv_hbm, fl_hbm, tok, kv_ref, low_ref, high_ref, seg_ref, bound_sm,
                wk, wv, bv, fl, sems):
    blocks, width = tok.shape[0] // TILE, wk.shape[1]
    pairs = [(fl_hbm, fl), (bv_hbm, bv), (wk_hbm, wk), (wv_hbm, wv)]
    pairs += [(tok_hbm.at[b * TILE : (b + 1) * TILE], tok.at[b * TILE : (b + 1) * TILE]) for b in range(blocks)]
    copies = [pltpu.make_async_copy(a, b, sems.at[n]) for n, (a, b) in enumerate(pairs)]
    for copy in copies:
        copy.start()
    copies[0].wait()
    seg = running_count(jnp.broadcast_to(fl[...], (8, fl.shape[1])))[0:1, :]
    seg_ref[...] = seg
    for b in range(blocks):
        bound_sm[2 * b] = jnp.min(seg[:, b * TILE : (b + 1) * TILE])
        bound_sm[2 * b + 1] = jnp.max(seg[:, b * TILE : (b + 1) * TILE])
    for ref, number in (
        (low_ref, seg[:, :MAXDOC]),
        (high_ref, jnp.max(seg) - seg[:, seg.shape[1] - MAXDOC :]),
    ):
        upper = lax.shift_right_logical(number, 8)
        row = lax.broadcasted_iota(jnp.int32, (EXTRA, MAXDOC), 0)
        digits = jnp.where(row == 0, upper, number - upper * 256)
        ref[MAXDOC:, :] = digits.astype(F32).astype(BF16)
    for copy in copies[1:4]:
        copy.wait()
    for b in range(blocks):
        copies[4 + b].wait()
        rows = slice(b * TILE, (b + 1) * TILE)
        keys = dot_nn(tok[rows, :], wk[...]).astype(BF16)
        values = (dot_nn(tok[rows, :], wv[...]) + bv[...]).astype(BF16)
        places = [(kv_ref, b)]
        if b < HALO:
            places.append((low_ref, b))
        if b >= blocks - HALO:
            places.append((high_ref, b - blocks + HALO))
        for ref, at in places:
            ref[at * TILE : (at + 1) * TILE, :width] = keys
            ref[at * TILE : (at + 1) * TILE, width:] = values


def in_hbm(arrays):
    return [pltpu.with_memory_space_constraint(a, pltpu.HBM) for a in arrays]


def project_keys(order, tokens, w_key, w_value, bias_value, flags):
    rows, width = tokens.shape
    cols = w_key.shape[1]
    edge = ((MAXDOC + EXTRA, 2 * cols), BF16)
    blocks = rows // TILE
    params = (tokens, w_key, w_value, bias_value, flags)
    return call(
        order, "project_keys", keys_kernel,
        [(tokens.shape, BF16), ((rows, 2 * cols), BF16), edge, edge, ((1, rows), jnp.int32),
         ((2 * blocks,), jnp.int32, SMEM)],
        in_hbm(params),
        scratch=[pltpu.VMEM(p.shape, p.dtype) for p in params[1:]] + [pltpu.SemaphoreType.DMA((4 + blocks,))],
        specs=[HBM] * len(params),
    )


def queries_kernel(count, *refs):
    tok, wq_hbm, bq_hbm, sources = refs[0], refs[1], refs[2], refs[3 : 3 + count]
    q_ref, held = refs[3 + count], refs[4 + count : 4 + 2 * count]
    wq, bq, sems = refs[4 + 2 * count :]
    pairs = [(wq_hbm, wq), (bq_hbm, bq), *zip(sources, held)]
    copies = [pltpu.make_async_copy(a, b, sems.at[n]) for n, (a, b) in enumerate(pairs)]
    for copy in copies:
        copy.start()
    copies[0].wait()
    copies[1].wait()
    for b in range(tok.shape[0] // TILE):
        rows = slice(b * TILE, (b + 1) * TILE)
        q_ref[rows, :] = (dot_nn(tok[rows, :], wq[...]) + bq[...]).astype(BF16)
    for copy in copies[2:]:
        copy.wait()


def project_queries(order, tokens, w_query, bias_query, others):
    shape = (tokens.shape[0], w_query.shape[1])
    return call(
        order, "project_queries", functools.partial(queries_kernel, len(others)),
        [(shape, BF16)] + [(p.shape, p.dtype) for p in others],
        (tokens, *in_hbm((w_query, bias_query, *others))),
        scratch=[
            pltpu.VMEM(w_query.shape, BF16), pltpu.VMEM(bias_query.shape, F32),
            pltpu.SemaphoreType.DMA((2 + len(others),)),
        ],
        specs=[VMEM] + [HBM] * (2 + len(others)),
    )


def rows_of(index):
    if isinstance(index, int):
        return pl.ds(index * TILE, TILE)
    return pl.ds(pl.multiple_of(index * TILE, TILE), TILE)


def meet(first_a, last_a, first_b, last_b):
    return jnp.logical_and(first_a <= last_b, last_a >= first_b)


def blocks_meet(bound_sm, a, b):
    return meet(bound_sm[2 * a], bound_sm[2 * a + 1], bound_sm[2 * b], bound_sm[2 * b + 1])


def seg_column(seg_row, index):
    return jnp.broadcast_to(seg_row[:, rows_of(index)], (128, TILE)).T


def edge_segments(seg_row, ref, left):
    digits = ref[MAXDOC : MAXDOC + EXTRA, :].astype(F32)
    segs = (digits[0:1, :] * 256.0 + digits[1:2, :]).astype(jnp.int32)
    if left:
        segs = -segs
    else:
        segs = segs + jnp.max(seg_row[...]) + jnp.where(position()[3], 1, 0)
    pieces = [segs[:, b * TILE : (b + 1) * TILE] for b in range(HALO)]
    return [(piece, jnp.min(piece), jnp.max(piece)) for piece in pieces]


def allowed_of(column, row):
    return jnp.concatenate([column, column], axis=1) == row


def head_mask(value, head):
    lane = lax.broadcasted_iota(jnp.int32, value.shape, 1)
    mine = (lane < HEAD_DIM) if head % 2 == 0 else (lane >= HEAD_DIM)
    return jnp.where(mine, value, jnp.zeros_like(value))


def pair_cols(head, base=0):
    return slice(base + (head // 2) * 128, base + (head // 2) * 128 + 128)


def head_rows(head):
    return slice(head * HEAD_DIM, (head + 1) * HEAD_DIM)


def forward_tile(heads, first, allowed, keys, values_t, q_ref, m_ref, l_ref, acc_ref):
    for head in range(heads):
        q_masked = head_mask(q_ref[:, pair_cols(head)], head)
        s = jnp.where(allowed, dot_nt(keys(head), q_masked) * SCORE, NEG)
        peak = jnp.max(s, axis=0, keepdims=True)
        row, hd = slice(head, head + 1), head_rows(head)
        if first:
            p = jnp.exp2(s - peak)
            m_ref[row, :] = peak
            l_ref[row, :] = jnp.sum(p, axis=0, keepdims=True)
            acc_ref[hd, :] = dot_nn(values_t(hd), p.astype(BF16))
        else:
            before = m_ref[row, :]
            top = jnp.maximum(before, peak)
            p = jnp.exp2(s - top)
            keep = jnp.exp2(before - top)
            m_ref[row, :] = top
            l_ref[row, :] = l_ref[row, :] * keep + jnp.sum(p, axis=0, keepdims=True)
            acc_ref[hd, :] = acc_ref[hd, :] * keep + dot_nn(values_t(hd), p.astype(BF16))


def attn_local_kernel(heads, blocks, bound_sm, seg_row, q_ref, kv_ref, m_ref, l_ref, acc_0, acc_1, vt, seg_col, acc_ref):
    width = heads * HEAD_DIM
    vt[...] = kv_ref[:, width:].T
    for b in range(blocks):
        seg_col[b * TILE : (b + 1) * TILE, :] = seg_column(seg_row, b)

    def block(qb, carry):
        qs = rows_of(qb)
        seg_q = seg_row[:, qs]

        def tile(kb, first):
            ks = rows_of(kb)
            forward_tile(
                heads, first, allowed_of(seg_col[ks, :], seg_q),
                lambda head: kv_ref[ks, pair_cols(head)], lambda hd: vt[hd, ks],
                q_ref.at[qs, :], m_ref.at[:, qs], l_ref.at[:, qs], acc_ref.at[:, qs],
            )

        tile(qb, True)

        def other(i, inner):
            kb = qb + i - HALO
            safe = jnp.clip(kb, 0, blocks - 1)

            @pl.when(jnp.logical_and(jnp.logical_and(kb == safe, i != HALO), blocks_meet(bound_sm, safe, qb)))
            def _():
                tile(safe, False)

            return inner

        lax.fori_loop(0, 2 * HALO + 1, other, 0)
        return carry

    lax.fori_loop(0, blocks, block, 0)
    acc_0[...] = acc_ref[:, :MAXDOC]
    acc_1[...] = acc_ref[:, MAXDOC:]


def attention_local(order, bounds, seg, q, kv):
    rows, width = q.shape
    heads, blocks = width // HEAD_DIM, rows // TILE
    stat = ((heads, rows), F32)
    return call(
        order, "attention_local",
        functools.partial(attn_local_kernel, heads, blocks),
        [stat, stat, ((width, MAXDOC), F32), ((width, MAXDOC), F32)],
        (bounds, seg, q, kv),
        scratch=[
            pltpu.VMEM((width, rows), BF16), pltpu.VMEM((rows, 128), jnp.int32), pltpu.VMEM((width, rows), F32)
        ],
        specs=[SMEM, VMEM, VMEM, VMEM],
    )


def attn_edge_kernel(
    heads, blocks, base, count,
    bound_sm, seg_row, q_ref, m_in, l_in, acc_in, far_ref, *refs,
):
    sources, (att_ref, lse_ref, edge_ref), refs = refs[:count], refs[count : count + 3], refs[count + 3 :]
    held, (m_ref, l_ref, acc_ref, sems) = refs[:count], refs[count:]
    copies = [pltpu.make_async_copy(a, b, sems.at[n]) for n, (a, b) in enumerate(zip(sources, held))]
    for copy in copies:
        copy.start()
    width = heads * HEAD_DIM
    left = base == 0
    edge_segs = edge_segments(seg_row, far_ref, left)
    for step in range(HALO):
        block = step + base
        own = block + HALO
        from_q = slice(block * TILE, (block + 1) * TILE)
        here = slice(step * TILE, (step + 1) * TILE)
        m_ref[...] = m_in[:, from_q]
        l_ref[...] = l_in[:, from_q]
        acc_ref[...] = acc_in[:, here]
        seg_q = seg_row[:, from_q]
        for h in range(HALO):
            segs, first, last = edge_segs[h]
            if abs((h if left else h + blocks + HALO) - own) > HALO:
                continue

            @pl.when(meet(first, last, bound_sm[2 * block], bound_sm[2 * block + 1]))
            def _():
                ks = rows_of(h)
                values_t = far_ref[ks, width:].T
                forward_tile(
                    heads, False, allowed_of(seg_column(segs, 0), seg_q),
                    lambda head: far_ref[ks, pair_cols(head)], lambda hd: values_t[hd, :],
                    q_ref.at[from_q, :], m_ref, l_ref, acc_ref,
                )

        for head in range(heads):
            row, hd = slice(head, head + 1), head_rows(head)
            total = l_ref[row, :]
            acc_ref[hd, :] = acc_ref[hd, :] * (1.0 / total)
            lse = m_ref[row, :] + jnp.log2(total)
            lse_ref[row, here] = lse
            for piece in range(3):
                part = lse.astype(BF16)
                at = MAXDOC + piece * heads + head
                edge_ref[at : at + 1, here] = part
                lse = lse - part.astype(F32)
        att = acc_ref[...].T.astype(BF16)
        att_ref[here, :] = att
        edge_ref[here, :width] = q_ref[from_q, :]
        edge_ref[here, width:] = att

    edge_ref[MAXDOC + 3 * heads :, :] = jnp.zeros((EXTRA - 3 * heads, 2 * width), BF16)
    for copy in copies:
        copy.wait()


def attention_edge(order, chunk, bounds, seg, q, m, l, acc, far, others=()):
    rows, width = q.shape
    heads, blocks = width // HEAD_DIM, rows // TILE
    (acc,) = in_hbm((acc,))
    att, lse, edge, *held = call(
        order, f"attention_edge_{chunk}",
        functools.partial(attn_edge_kernel, heads, blocks, chunk * HALO, len(others)),
        [((MAXDOC, width), BF16), ((heads, MAXDOC), F32), ((MAXDOC + EXTRA, 2 * width), BF16)]
        + [(p.shape, p.dtype) for p in others],
        (bounds, seg, q, m, l, acc, far, *in_hbm(others)),
        scratch=[
            pltpu.VMEM((heads, TILE), F32), pltpu.VMEM((heads, TILE), F32), pltpu.VMEM((width, TILE), F32),
            pltpu.SemaphoreType.DMA((max(1, len(others)),)),
        ],
        specs=[SMEM] + [VMEM] * 6 + [HBM] * len(others),
    )
    return att, lse, edge, held


def per_head_sums(heads, d, a):
    width = heads * HEAD_DIM
    col = lax.broadcasted_iota(jnp.int32, (8, width), 1) // HEAD_DIM
    row = lax.broadcasted_iota(jnp.int32, (8, width), 0)
    return lax.dot_general(
        (col == row).astype(F32), d.astype(F32) * a.astype(F32), (((1,), (1,)), ((), ())),
        preferred_element_type=F32, precision=lax.Precision.HIGHEST,
    )


def backward_tile(heads, allowed, k_of, v_of, kt, q_of, d_of, lse, delta, dq_add, dkv_add):
    for head in range(heads):
        row = slice(head, head + 1)
        q_pair, d_pair = q_of(head), d_of(head)
        s = dot_nt(head_mask(k_of(head), head), q_pair)
        p = jnp.where(allowed, jnp.exp2(s * SCORE - lse[row, :]), 0.0)
        dp = dot_nt(head_mask(v_of(head), head), d_pair)
        ds = (p * (dp - delta[row, :])).astype(BF16)
        if dkv_add is not None:
            dkv_add(head, dot_nn(ds, q_pair), dot_nn(p.astype(BF16), d_pair))
        if dq_add is not None:
            dq_add(head, dot_nn(kt[head_rows(head), :], ds))


def merge_pairs(heads, acc):
    lane = lax.broadcasted_iota(jnp.int32, (TILE, 128), 1)
    pieces = [jnp.where(lane < HEAD_DIM, acc[h], acc[h + 1]) for h in range(0, heads, 2)]
    return jnp.concatenate(pieces, axis=1)


def back_local_kernel(
    heads, blocks,
    bound_sm, seg_row, q_ref, kv_ref, a0, a1, lse0, lse1, d0, d1,
    dqt_ref, dk_ref, dv_ref, delta,
    dx, lx, dk_acc, dv_acc,
):
    width = heads * HEAD_DIM
    for i, (d, a, lse) in enumerate(((d0, a0, lse0), (d1, a1, lse1))):
        part = slice(i * MAXDOC, (i + 1) * MAXDOC)
        dx[part, :] = d[...]
        lx[:, part] = lse[...]
        delta[:, part] = per_head_sums(heads, d[...], a[...])
    dqt_ref[...] = jnp.zeros_like(dqt_ref)

    def block(kb, carry):
        dk_acc[...] = jnp.zeros_like(dk_acc)
        dv_acc[...] = jnp.zeros_like(dv_acc)
        ks = rows_of(kb)
        seg_k = seg_column(seg_row, kb)
        kt = kv_ref[ks, :width].T

        def tile(qb):
            qs = rows_of(qb)

            def dq_add(head, value):
                dqt_ref[head_rows(head), qs] += value

            def dkv_add(head, dk, dv):
                dk_acc[head] += dk
                dv_acc[head] += dv

            backward_tile(
                heads, allowed_of(seg_k, seg_row[:, qs]),
                lambda h: kv_ref[ks, pair_cols(h)], lambda h: kv_ref[ks, pair_cols(h, width)], kt,
                lambda h: q_ref[qs, pair_cols(h)], lambda h: dx[qs, pair_cols(h)],
                lx[:, qs], delta[:, qs], dq_add, dkv_add,
            )

        def other(i, inner):
            qb = kb + i - HALO
            safe = jnp.clip(qb, 0, blocks - 1)

            @pl.when(jnp.logical_and(qb == safe, blocks_meet(bound_sm, safe, kb)))
            def _():
                tile(safe)

            return inner

        lax.fori_loop(0, 2 * HALO + 1, other, 0)
        dk_ref[ks, :] = merge_pairs(heads, dk_acc)
        dv_ref[ks, :] = merge_pairs(heads, dv_acc)
        return carry

    lax.fori_loop(0, blocks, block, 0)


def attention_back_local(order, bounds, seg, q, kv, d_parts, a_parts, lse_parts):
    rows, width = q.shape
    heads, blocks = width // HEAD_DIM, rows // TILE
    out = ((rows, width), F32)
    return call(
        order, "attention_back_local",
        functools.partial(back_local_kernel, heads, blocks),
        [((width, rows), F32), out, out, ((8, rows), F32)],
        (bounds, seg, q, kv, *a_parts, *lse_parts, *d_parts),
        scratch=[
            pltpu.VMEM((rows, width), BF16),
            pltpu.VMEM((heads, rows), F32),
            pltpu.VMEM((heads, TILE, 128), F32),
            pltpu.VMEM((heads, TILE, 128), F32),
        ],
        specs=[SMEM] + [VMEM] * 9,
    )


def back_edge_kernel(
    heads, blocks,
    bound_sm, seg_row, q_ref, kv_ref, lse0, lse1, d0, d1,
    kv_low, kv_high, qa_low, qa_high, dqt_in, dk_in, dv_in, delta_own, d_low, d_high,
    dq_ref, dk_ref, dv_ref,
    dqt, dk_acc, dv_acc, stats,
):
    width = heads * HEAD_DIM
    edge_segs = edge_segments(seg_row, kv_low, True) + edge_segments(seg_row, kv_high, False)
    low_meets = edge_segs[HALO - 1][2] >= bound_sm[0]
    high_meets = edge_segs[HALO][1] <= bound_sm[2 * blocks - 1]
    for n, (meets, qa, d) in enumerate(((low_meets, qa_low, d_low), (high_meets, qa_high, d_high))):

        @pl.when(meets)
        def _():
            pieces = qa[MAXDOC : MAXDOC + EXTRA, :].astype(F32)
            stats[n, :heads, :] = pieces[:heads] + pieces[heads : 2 * heads] + pieces[2 * heads : 3 * heads]
            stats[n, 8:, :] = per_head_sums(heads, d[...], qa[:MAXDOC, width:])

    for step in range(blocks):
        here = slice(step * TILE, (step + 1) * TILE)
        inner = slice((step % HALO) * TILE, (step % HALO + 1) * TILE)
        lse_own, d_own = (lse0, d0) if step < HALO else (lse1, d1)
        dqt[...] = dqt_in[:, here]
        dk_acc[...] = jnp.zeros_like(dk_acc)
        dv_acc[...] = jnp.zeros_like(dv_acc)

        def dq_add(head, value):
            dqt[head_rows(head), :] += value

        def dkv_add(head, dk, dv):
            dk_acc[head] += dk
            dv_acc[head] += dv

        for h in range(2 * HALO):
            far = h if h < HALO else blocks + h
            if abs(far - step - HALO) > HALO:
                continue
            kv_far, qa_far, d_far = (kv_low, qa_low, d_low) if h < HALO else (kv_high, qa_high, d_high)
            at = slice((h % HALO) * TILE, (h % HALO + 1) * TILE)
            segs, first, last = edge_segs[h]

            @pl.when(meet(first, last, bound_sm[2 * step], bound_sm[2 * step + 1]))
            def _():
                backward_tile(
                    heads, allowed_of(seg_column(segs, 0), seg_row[:, here]),
                    lambda hd: kv_far[at, pair_cols(hd)], lambda hd: kv_far[at, pair_cols(hd, width)],
                    kv_far[at, :width].T,
                    lambda hd: q_ref[here, pair_cols(hd)], lambda hd: d_own[inner, pair_cols(hd)],
                    lse_own[:, inner], delta_own[:, here], dq_add, None,
                )
                side = h // HALO
                backward_tile(
                    heads, allowed_of(seg_column(seg_row, step), segs),
                    lambda hd: kv_ref[here, pair_cols(hd)], lambda hd: kv_ref[here, pair_cols(hd, width)], None,
                    lambda hd: qa_far[at, pair_cols(hd)], lambda hd: d_far[at, pair_cols(hd)],
                    stats[side, :heads, at], stats[side, 8:, at], None, dkv_add,
                )

        dq_ref[here, :] = (dqt[...] * SCALE).T.astype(BF16)
        dk_ref[here, :] = ((dk_in[here, :] + merge_pairs(heads, dk_acc)) * SCALE).astype(BF16)
        dv_ref[here, :] = (dv_in[here, :] + merge_pairs(heads, dv_acc)).astype(BF16)


def attention_back_edge(order, bounds, seg, q, kv, d_parts, lse_parts, kv_far, qa_far, d_far, local):
    rows, width = q.shape
    heads, blocks = width // HEAD_DIM, rows // TILE
    return call(
        order, "attention_back_edge",
        functools.partial(back_edge_kernel, heads, blocks),
        [((rows, width), BF16)] * 3,
        (bounds, seg, q, kv, *lse_parts, *d_parts, *kv_far, *qa_far, *local, *d_far),
        scratch=[
            pltpu.VMEM((width, TILE), F32),
            pltpu.VMEM((heads, TILE, 128), F32),
            pltpu.VMEM((heads, TILE, 128), F32),
            pltpu.VMEM((2, 16, MAXDOC), F32),
        ],
        specs=[SMEM] + [VMEM] * 17,
    )


def moments(value):
    average = jnp.mean(value, axis=-1, keepdims=True)
    centred = value - average
    variance = jnp.mean(centred * centred, axis=-1, keepdims=True)
    scale = lax.rsqrt(variance + 1e-12)
    return centred * scale, scale


def norm_back(grad, normal, scale):
    return scale * (
        grad
        - jnp.mean(grad, axis=-1, keepdims=True)
        - normal * jnp.mean(grad * normal, axis=-1, keepdims=True)
    )


def gelu_both(value):
    half = 0.5 * (1.0 + lax.erf(value * 0.7071067811865476))
    slope = half + value * jnp.exp(-0.5 * value * value) * 0.3989422804014327
    return value * half, slope


PIECE = 64
PIECES = TILE // PIECE


def swap_pieces(pieces):
    return tuple(swap(piece, "wt", 1) for piece in pieces)


def gather(rows, refs):
    for i, ref in enumerate(refs):
        rows[i * PIECE : (i + 1) * PIECE, :] = ref[...]


def scatter(refs, value):
    for i, ref in enumerate(refs):
        ref[...] = value[i * PIECE : (i + 1) * PIECE, :].astype(ref.dtype)


def by_pieces(one):
    for i in range(PIECES):
        one(i, slice(i * PIECE, (i + 1) * PIECE))


def add_sums(ref, rows):
    for i, value in enumerate(rows):
        ref[i : i + 1, :] += jnp.sum(value, axis=0, keepdims=True)


def mix_kernel(chunk, tok, w_own, w_core, w_far, w_diag, bias, gain, shift, a_own, a_core, a_far, a_diag,
               normal_ref, scale_ref, *rest):
    low_refs, total = rest[:PIECES], rest[PIECES]
    core, side = position()[:2]
    rows = pl.ds(pl.multiple_of(core * TILE, TILE), TILE)
    chip = ((a_own, w_own), (a_core, w_core))
    far = ((a_far, w_far), (a_diag, w_diag))

    def add_up(pairs):
        total[...] = dot_nt(pairs[0][0][rows, :], pairs[0][1][...])
        for left, right in pairs[1:]:
            total[...] += dot_nt(left[rows, :], right[...])

    @pl.when(side == 0)
    def _():
        add_up(chip + far)

    @pl.when(side != 0)
    def _():
        add_up(far + chip)

    first = (2 * chunk + core) * TILE

    def one(i, here):
        there = pl.ds(pl.multiple_of(first + i * PIECE, PIECE), PIECE)
        normal, scale = moments(tok[there, :].astype(F32) + total[here, :] + bias[...])
        normal_ref[here, :] = normal
        scale_ref[here, :] = jnp.broadcast_to(scale, (PIECE, 128))
        low_refs[i][...] = (normal * gain[...] + shift[...]).astype(BF16)

    by_pieces(one)


def mix(order, chunk, tokens, att, weights, bias, gain, shift):
    rows, width = tokens.shape
    normal, scale, *low = call(
        order, f"mix_{chunk}",
        functools.partial(mix_kernel, chunk),
        [((TILE, width), F32), ((TILE, 128), F32)] + [((PIECE, width), BF16)] * PIECES,
        (tokens, *weights, bias, gain, shift, *att),
        scratch=[pltpu.VMEM((TILE, width), F32)],
    )
    return normal, scale, low


STRIP = 256


def strips(width, one):
    def step(i, carry):
        one(i, pl.ds(pl.multiple_of(i * STRIP, STRIP), STRIP))
        return carry

    lax.fori_loop(0, width // STRIP, step, 0)


def up_down_kernel(w_up, w_down, bias, *refs):
    mine, other, refs = refs[:PIECES], refs[PIECES : 2 * PIECES], refs[2 * PIECES :]
    hidden_ref, slope_ref, rows, part_mine = refs[:4]
    gather(rows.at[:TILE, :], mine)
    gather(rows.at[TILE:, :], other)

    def one(i, cols):
        active, slope = gelu_both(dot_nn(rows[...], w_up[:, cols]) + bias[:, cols])
        hidden_ref[:, cols] = active.astype(BF16)
        slope_ref[:, cols] = slope.astype(BF16)

    strips(w_up.shape[1], one)
    scatter(refs[4:], dot_nt(hidden_ref[TILE:, :], w_down[...]))
    part_mine[...] = dot_nt(hidden_ref[:TILE, :], w_down[...])


def up_down(order, chunk, mine, other, w_up, w_down, bias):
    width, hidden = w_up.shape
    both = ((2 * TILE, hidden), BF16)
    hidden, slope, rows, part, *parts = call(
        order, f"up_down_{chunk}", up_down_kernel,
        [both, both, ((2 * TILE, width), BF16), ((TILE, width), F32)] + [((PIECE, width), BF16)] * PIECES,
        (w_up, w_down, bias, *mine, *other),
    )
    return hidden, slope, rows, part, parts


def down_up_kernel(w_down, w_up, slope_ref, *refs):
    mine, other, refs = refs[:PIECES], refs[PIECES : 2 * PIECES], refs[2 * PIECES :]
    inner_ref, sums, rows, part_mine = refs[:4]
    gather(rows.at[:TILE, :], mine)
    gather(rows.at[TILE:, :], other)

    def one(i, cols):
        d_inner = (dot_nn(rows[...], w_down[:, cols]) * slope_ref[:, cols].astype(F32)).astype(BF16)
        inner_ref[:, cols] = d_inner
        sums[:, cols] = jnp.sum(d_inner.astype(F32), axis=0, keepdims=True)

    strips(w_down.shape[1], one)
    scatter(refs[4:], dot_nt(inner_ref[TILE:, :], w_up[...]))
    part_mine[...] = dot_nt(inner_ref[:TILE, :], w_up[...])


def down_up(order, chunk, mine, other, w_down, w_up, slope):
    width, hidden = w_up.shape
    inner, sums, rows, part, *parts = call(
        order, f"down_up_{chunk}", down_up_kernel,
        [((2 * TILE, hidden), BF16), ((1, hidden), F32), ((2 * TILE, width), BF16), ((TILE, width), F32)]
        + [((PIECE, width), BF16)] * PIECES,
        (w_down, w_up, slope, *mine, *other),
    )
    return inner, sums, rows, part, parts


def chip_sum_kernel(mine, *refs):
    out = refs[-1]
    for i, ref in enumerate(refs[:-1]):
        here = slice(i * PIECE, (i + 1) * PIECE)
        out[here, :] = (mine[here, :] + ref[...].astype(F32)).astype(BF16)


def chip_sum(order, name, mine, parts):
    return call(order, name, chip_sum_kernel, [(mine.shape, BF16)], (mine, *swap_pieces(parts)))[0]


def end_kernel(chunk, normal, chip, cot, mid_gain, mid_bias, bias, gain, shift, *refs):
    before, refs = (refs[:2], refs[2:]) if chunk else ((), refs)
    far, out_ref, d_ref, sums = refs[:4]
    low_refs = refs[4:]
    core, side = position()[:2]
    sums[...] = before[1][...] if before else jnp.zeros_like(sums)
    first = (2 * chunk + core) * TILE

    def one(i, here):
        there = pl.ds(pl.multiple_of(first + i * PIECE, PIECE), PIECE)
        both = chip[here, :].astype(F32) + far[here, :].astype(F32)
        second = (normal[here, :] * mid_gain[...] + mid_bias[...]) + both + bias[...]
        unit, scale = moments(second)
        value = (unit * gain[...] + shift[...]).astype(BF16)
        if before:
            value = jnp.where(side == chunk, value, before[0][here, :])
        out_ref[here, :] = value
        upstream = cot[there, :].astype(F32)
        d_second = norm_back(upstream * gain[...], unit, scale)
        low = d_second.astype(BF16)
        d_ref[here, :] = d_second
        low_refs[i][...] = low
        add_sums(sums, (upstream * unit, upstream, low.astype(F32)))

    by_pieces(one)


def end(order, chunk, normal, chip, far, cotangent, vectors, before, waits=()):
    rows, width = normal.shape
    out, d, sums, *low = call(
        order, f"end_{chunk}",
        functools.partial(end_kernel, chunk),
        [((rows, width), BF16), ((rows, width), F32), ((8, width), F32)] + [((PIECE, width), BF16)] * PIECES,
        (normal, chip, cotangent, *vectors, *before, far),
        waits=waits,
    )
    return out, d, sums, low


def mid_kernel(count, d_second, chip, normal, scale, gain, far, *refs):
    before, (d_ref, sums), low_refs = refs[:count], refs[count : count + 2], refs[count + 2 :]
    sums[...] = before[0][...] if before else jnp.zeros_like(sums)

    def one(i, here):
        d_first = d_second[here, :] + (chip[here, :].astype(F32) + far[here, :].astype(F32))
        unit = normal[here, :]
        d_sum = norm_back(d_first * gain[...], unit, scale[here, 0:1])
        low = d_sum.astype(BF16)
        d_ref[here, :] = d_sum
        low_refs[i][...] = low
        add_sums(sums, (d_first * unit, d_first, low.astype(F32)))

    by_pieces(one)


def mid(order, chunk, d_second, chip, far, normal, scale, gain, before):
    rows, width = normal.shape
    d, sums, *low = call(
        order, f"mid_{chunk}", functools.partial(mid_kernel, len(before)),
        [((rows, width), F32), ((8, width), F32)] + [((PIECE, width), BF16)] * PIECES,
        (d_second, chip, normal, scale, gain, far, *before),
    )
    return d, sums, low


def d_att_kernel(w_out, *refs):
    mine, other, out, rows = refs[:PIECES], refs[PIECES : 2 * PIECES], refs[2 * PIECES], refs[2 * PIECES + 1]
    core = position()[0]
    here = pl.ds(pl.multiple_of(core * TILE, TILE), TILE)
    there = pl.ds(pl.multiple_of((1 - core) * TILE, TILE), TILE)
    gather(rows.at[here, :], mine)
    gather(rows.at[there, :], other)
    out[...] = dot_nn(rows[...], w_out[...]).astype(BF16)


def d_att(order, chunk, mine, other, w_out):
    width, cols = w_out.shape
    return call(
        order, f"d_attended_{chunk}", d_att_kernel, [((2 * TILE, cols), BF16), ((2 * TILE, width), BF16)],
        (w_out, *mine, *other),
    )


def part_of(refs, weights, block):
    rows = pl.ds(pl.multiple_of(block * TILE, TILE), TILE)
    total = None
    for ref, weight in zip(refs, weights):
        part = dot_nt(ref[rows, :], weight[...])
        total = part if total is None else total + part
    return total


def input_other_kernel(wq, wk, wv, dq, dk, dv, other_0, other_1):
    for j, other in enumerate((other_0, other_1)):
        block = 2 * j + 1 - position()[0]
        other[...] = part_of((dq, dk, dv), (wq, wk, wv), block).astype(BF16)


def input_mine_kernel(wq, wk, wv, dq, dk, dv, d0, d1, got_0, got_1, here, away):
    core, side = position()[:2]
    weights = (wq, wk, wv)

    def chip(j):
        return part_of((dq, dk, dv), weights, 2 * j + core)

    for mine, got, d in ((0, got_0, d0), (1, got_1, d1)):

        @pl.when(side == mine)
        def _():
            here[...] = chip(mine) + got[...].astype(F32) + d[...]

        @pl.when(side != mine)
        def _():
            away[...] = (chip(mine) + got[...].astype(F32)).astype(BF16)


def input_sum_kernel(here, got, out):
    out[...] = here[...] + got[...].astype(F32)


def halves(value, bit, rows):
    low = (1 << bit) * rows
    split = value.reshape(value.shape[0] // (2 * low), 2, low, value.shape[1])
    flat = (value.shape[0] // 2, value.shape[1])
    return split[:, 0].reshape(flat), split[:, 1].reshape(flat)


def put_halves(value, bit, rows, mine, keep_ref, give_ref):
    zero, one = halves(value, bit, rows)

    @pl.when(mine == 0)
    def _():
        keep_ref[...] = zero.astype(keep_ref.dtype)
        give_ref[...] = one.astype(give_ref.dtype)

    @pl.when(mine != 0)
    def _():
        keep_ref[...] = one.astype(keep_ref.dtype)
        give_ref[...] = zero.astype(give_ref.dtype)


def weight_grad_kernel(cuts, rows, count, *refs):
    lefts, rights = refs[:count], refs[count : 2 * count]
    outs, left_t = refs[2 * count : -1], refs[-1]
    at = 0
    for ref in lefts:
        left_t[:, at : at + ref.shape[0]] = ref[...].T
        at += ref.shape[0]
    for n, (cols, bit) in enumerate(cuts):
        keep_ref, give_ref = outs[2 * n], outs[2 * n + 1]
        mine = (position()[2] >> bit) & 1
        for first in range(0, cols.stop - cols.start, 128 if (cols.stop - cols.start) % 256 else 256):
            size = 128 if (cols.stop - cols.start) % 256 else 256
            there = slice(cols.start + first, cols.start + first + size)
            total, at = None, 0
            for ref in rights:
                part = dot_nn(left_t[:, at : at + ref.shape[0]], ref[:, there])
                total = part if total is None else total + part
                at += ref.shape[0]
            put_halves(
                total, bit, rows, mine, keep_ref.at[:, first : first + size], give_ref.at[:, first : first + size]
            )


def out_grad_kernel(att0, att1, m0, m1, out, left_t):
    half = att0.shape[0]
    left_t[:, :half] = m0[...].T
    left_t[:, half:] = m1[...].T
    out[...] = (dot_nn(left_t[:, :half], att0[...]) + dot_nn(left_t[:, half:], att1[...])).astype(BF16)


def weight_grad(order, name, lefts, rights, cuts, ctx_count):
    width = lefts[0].shape[1]
    tall = sum(left.shape[0] for left in lefts)
    outs = []
    for cols, _ in cuts:
        outs += [((width // 2, cols.stop - cols.start), BF16)] * 2
    return call(
        order, name,
        functools.partial(weight_grad_kernel, cuts, width // ctx_count, len(lefts)),
        outs, (*lefts, *rights),
        scratch=[pltpu.VMEM((width, tall), BF16)],
    )


SMALL = 8


def two_digits(small, width):
    flat = [small[:, at : at + width] for at in range(0, small.shape[1], width)]
    value = jnp.concatenate(flat, axis=0)
    upper = value.astype(BF16)
    return jnp.concatenate([upper, (value - upper.astype(F32)).astype(BF16)], axis=0)


def from_digits(rows, width):
    half = rows.shape[0] // 2
    value = rows[:half].astype(F32) + rows[half:].astype(F32)
    return jnp.concatenate([value[at : at + SMALL] for at in range(0, half, SMALL)], axis=1)


def put_given(total, bit, rows, mine, keep_ref, give_ref):
    tall = keep_ref.shape[0]
    put_halves(total, bit, rows, mine, keep_ref, give_ref.at[:tall, :])


def qkv_grad_kernel(
    bit_a, bit_b, rows, tokens, out_grad, sums_end, sums_mid, sums_up0, sums_up1,
    dq, dk, dv, keep_a, give_a, keep_b, give_b, small_ref, tok_t,
):
    tok_t[...] = tokens[...].T
    width = dq.shape[1]
    mine = (position()[2] >> bit_a) & 1
    for n, ref in enumerate((dq, dk)):
        cols = slice(n * width, (n + 1) * width)
        put_given(dot_nn(tok_t[...], ref[...]), bit_a, rows, mine, keep_a.at[:, cols], give_a.at[:, cols])
    mine = (position()[2] >> bit_b) & 1
    put_given(dot_nn(tok_t[...], dv[...]), bit_b, rows, mine, keep_b.at[:, :width], give_b.at[:, :width])
    put_given(out_grad[...], bit_b, rows, mine, keep_b.at[:, width:], give_b.at[:, width:])
    small_ref[0:3, :] = sums_end[0:3, :]
    small_ref[3:6, :] = sums_mid[0:3, :]
    small_ref[6:7, :] = sums_up0[...] + sums_up1[...]
    small_ref[7:8, :] = jnp.zeros_like(small_ref[7:8, :])
    small_ref[7:8, :width] = jnp.sum(dq[...].astype(F32), axis=0, keepdims=True)
    small_ref[7:8, width : 2 * width] = jnp.sum(dv[...].astype(F32), axis=0, keepdims=True)
    give_a[keep_a.shape[0] :, :] = two_digits(small_ref[...], give_a.shape[1])


def small_rows(width, cols):
    return 2 * SMALL * (width // cols)


def qkv_grad(order, tokens, out_grad, sums, dq, dk, dv, bits, ctx_count):
    width = tokens.shape[1]
    cols = 2 * dq.shape[1]
    extra = small_rows(width, cols)
    return call(
        order, "grad_w_qkv",
        functools.partial(qkv_grad_kernel, *bits, width // ctx_count),
        [((width // 2, cols), BF16), ((width // 2 + extra, cols), BF16),
         ((width // 2, cols), BF16), ((width // 2, cols), BF16), ((SMALL, width), F32)],
        (tokens, out_grad, *sums, dq, dk, dv),
        scratch=[pltpu.VMEM(tokens.shape[::-1], BF16)],
    )


def fold_small_kernel(axis_bit, bit, rows, keep, small, got, keep_ref, give_ref, small_ref):
    tall = keep.shape[0]
    total = keep[...].astype(F32) + got[:tall, :].astype(F32)
    put_given(total, bit, rows, (position()[2] >> axis_bit) & 1, keep_ref, give_ref)
    cols = keep.shape[1]
    own = from_digits(two_digits(small[...], cols), cols)
    value = own + from_digits(got[tall:, :], cols)
    small_ref[...] = value
    give_ref[keep_ref.shape[0] :, :] = two_digits(value, cols)


def last_small_kernel(keep_a, keep_b, small, got_a, got_b, q, k, v, out, small_ref):
    width = q.shape[1]
    tall, cols = keep_a.shape
    a = keep_a[...].astype(F32) + got_a[:tall, :].astype(F32)
    b = keep_b[...].astype(F32) + got_b[...].astype(F32)
    q[...] = a[:, :width]
    k[...] = a[:, width:]
    v[...] = b[:, :width]
    out[...] = b[:, width:]
    small_ref[...] = from_digits(two_digits(small[...], cols), cols) + from_digits(got_a[tall:, :], cols)


def fold_kernel(axis_bit, bit, rows, keep, got, keep_ref, give_ref):
    total = keep[...].astype(F32) + got[...].astype(F32)
    put_halves(total, bit, rows, (position()[2] >> axis_bit) & 1, keep_ref, give_ref)


def last_kernel(keep, got, out):
    out[...] = keep[...].astype(F32) + got[...].astype(F32)


class ScatterSum:
    def __init__(self, order, name, keep, give, bits, ctx_count, small=None):
        self.order, self.name, self.bits, self.small = order, name, bits, small
        self.left = list(range(ctx_count.bit_length() - 1))
        self.keep, self.give, self.done = keep, give, 0
        self.rows = keep.shape[0] * 2 // ctx_count

    def send(self):
        self.got = swap(self.give, "ctx", 1 << self.bits[self.done])
        return self

    def fold(self):
        self.left.remove(self.bits[self.done])
        self.done += 1
        tall, width = self.keep.shape
        bit = self.bits[self.done]
        half = ((tall // 2, width), BF16)
        if self.small is not None:
            extra = small_rows(self.small.shape[1], width)
            self.keep, self.give, self.small = call(
                self.order, f"{self.name}_fold_{self.done}",
                functools.partial(fold_small_kernel, bit, self.left.index(bit), self.rows),
                [half, ((tall // 2 + extra, width), BF16), (self.small.shape, F32)],
                (self.keep, self.small, self.got),
            )
            return self.send()
        self.keep, self.give = call(
            self.order, f"{self.name}_fold_{self.done}",
            functools.partial(fold_kernel, bit, self.left.index(bit), self.rows),
            [half, half], (self.keep, self.got),
        )
        return self.send()

    def last(self):
        return call(
            self.order, f"{self.name}_sum", last_kernel, [(self.keep.shape, F32)], (self.keep, self.got)
        )[0]


def swap(value, axis, mask):
    return lax.ppermute(value, axis, [(i, i ^ mask) for i in range(lax.axis_size(axis))])


def neighbours(to_left, to_right, axis):
    count = lax.axis_size(axis)
    forward = [(i, i + 1) for i in range(count - 1)]
    backward = [(i + 1, i) for i in range(count - 1)]
    return lax.ppermute(to_right, axis, forward), lax.ppermute(to_left, axis, backward)


def after(value, *earlier):
    return lax.optimization_barrier((value, *earlier))[0]


def everywhere_sum(value, axis):
    for bit in range(lax.axis_size(axis).bit_length() - 1):
        value = value + swap(value, axis, 1 << bit)
    return value


def body(
    tokens, flags, w_query, w_key, w_value, w_out, w_up, w_down, bias_query, bias_value, bias_out,
    mid_gain, mid_bias, bias_up, bias_down, end_gain, end_bias, cotangent,
):
    rows, width = tokens.shape
    assert rows == 4 * TILE == 2 * MAXDOC
    ctx_count = lax.axis_size("ctx")
    bits = list(range(ctx_count.bit_length() - 1))
    turned = bits[1:] + bits[:1]
    order = Order()
    biases = [v[None] for v in (bias_out, mid_gain, mid_bias, bias_up, bias_down, end_gain, end_bias)]

    w_far = swap(w_out, "wt", 2)
    tokens, kv, kv_to_left, kv_to_right, seg, bounds = project_keys(
        order, tokens, w_key, w_value, bias_value[None], flags[None]
    )
    kv_low, kv_high = neighbours(kv_to_left, kv_to_right, "ctx")
    order.hold(tokens, kv)
    (queries,) = project_queries(order, tokens, w_query, bias_query[None], ())
    order.hold(queries)
    m, l, *acc = attention_local(order, bounds, seg, queries, kv)
    w_diag = swap(w_far, "wt", 1)

    att_0, lse_0, edge_0, held = attention_edge(
        order, 0, bounds, seg, queries, m, l, acc[0], kv_low, (w_out, w_up, w_down, cotangent, *biases)
    )
    w_out, w_up, w_down, cotangent, bias_out, mid_gain, mid_bias, bias_up, bias_down, end_gain, end_bias = held
    w_core = swap(w_out, "wt", 1)
    weights = (w_out, w_core, w_far, w_diag)
    order.hold(w_out, w_up, w_down, cotangent, att_0)
    att_1, lse_1, edge_1, _ = attention_edge(order, 1, bounds, seg, queries, m, l, acc[1], kv_high)
    order.hold(att_1)
    att, lse = (att_0, att_1), (lse_0, lse_1)
    qa_low, qa_high = neighbours(edge_0, edge_1, "ctx")

    normal, scale, low, hidden, slope, chip, far = [], [], [], [], [], [], []
    for j in range(2):
        att_far = swap(att[j], "wt", 2)
        pieces = (att[j], swap(att[j], "wt", 1), att_far, swap(att_far, "wt", 1))
        n, s, lo = mix(order, j, tokens, pieces, weights, bias_out, mid_gain, mid_bias)
        normal.append(n)
        scale.append(s)
        h, sl, rows_j, part, parts = up_down(order, j, lo, swap_pieces(lo), w_up, w_down, bias_up)
        low.append(rows_j)
        hidden.append(h)
        slope.append(sl)
        chip.append(chip_sum(order, f"second_{j}", part, parts))
        far.append(swap(chip[j], "wt", 2))
        order.hold(n, s, rows_j, h, sl)

    before, d_second, down = (), [], []
    d_inner, up_sums, d_chip, d_far = [], [], [], []
    vectors = (mid_gain, mid_bias, bias_down, end_gain, end_bias)
    for j in range(2):
        out, d, sums, lo = end(
            order, j, normal[j], chip[j], far[j], cotangent, vectors, before, (qa_low, qa_high) if j else ()
        )
        before = (out, sums)
        d_second.append(d)
        di, sums, rows_j, part, parts = down_up(order, j, lo, swap_pieces(lo), w_down, w_up, slope[j])
        down.append(rows_j)
        d_inner.append(di)
        up_sums.append(sums)
        d_chip.append(chip_sum(order, f"first_{j}", part, parts))
        d_far.append(swap(d_chip[j], "wt", 2))
        order.hold(d, rows_j, di)
    order.free(cotangent, w_up, w_down, *slope)
    layer_out, end_sums = before
    end_sums = end_sums + swap(end_sums, "wt", 1)

    full = slice(0, hidden[0].shape[1])
    keep, give = weight_grad(order, "grad_w_down", down, hidden, ((full, turned[0]),), ctx_count)
    order.free(*down, *hidden)
    sum_down = ScatterSum(order, "grad_w_down", keep, give, turned, ctx_count).send()
    keep, give = weight_grad(order, "grad_w_up", low, d_inner, ((full, bits[0]),), ctx_count)
    order.free(*low, *d_inner)
    sum_up = ScatterSum(order, "grad_w_up", keep, give, bits, ctx_count).send()
    order.hold(end_sums, *up_sums)

    d_first_sum, d_attended, mixed, before = [], [], [], ()
    for j in range(2):
        d, sums, lo = mid(order, j, d_second[j], d_chip[j], d_far[j], normal[j], scale[j], mid_gain, before)
        d_first_sum.append(d)
        before = (sums,)
        da, rows_j = d_att(order, j, lo, swap_pieces(lo), w_out)
        d_attended.append(da)
        mixed.append(rows_j)
        order.hold(d, da, rows_j)
        order.free(d_second[j], normal[j], scale[j])
    mid_sums = sums + swap(sums, "wt", 1)
    d_low, d_high = neighbours(d_attended[0], d_attended[1], "ctx")
    sum_down.fold()
    sum_up.fold()

    order.hold(mid_sums)
    local = attention_back_local(order, bounds, seg, queries, kv, d_attended, att, lse)
    (out_grad,) = call(
        order, "grad_w_out", out_grad_kernel, [(w_out.shape, BF16)], (*att, *mixed),
        scratch=[pltpu.VMEM((width, rows), BF16)],
    )
    order.free(*mixed, *att)

    d_queries, d_keys, d_values = attention_back_edge(
        order, bounds, seg, queries, kv, d_attended, lse,
        (kv_low, kv_high), (qa_low, qa_high), (d_low, d_high), local,
    )
    order.free(queries, kv, *d_attended)
    grads = (d_queries, d_keys, d_values)
    order.hold(*grads)
    keep_a, give_a, keep_b, give_b, small = qkv_grad(
        order, tokens, out_grad, (end_sums, mid_sums, *up_sums), *grads, (bits[0], bits[0]), ctx_count
    )
    order.free(tokens, end_sums, mid_sums, *up_sums)
    order.hold(keep_a, keep_b)
    sum_a = ScatterSum(order, "grad_w_a", keep_a, give_a, bits, ctx_count, small).send()
    sum_b = ScatterSum(order, "grad_w_b", keep_b, give_b, bits, ctx_count).send()
    input_weights = (w_query, w_key, w_value)
    half_shape = (TILE, width)
    input_other = call(
        order, "input_other", input_other_kernel, [(half_shape, BF16)] * 2, (*input_weights, *grads)
    )
    sum_down.fold()
    sum_up.fold()
    here, away = call(
        order, "input_mine", input_mine_kernel, [((TILE, width), F32), ((TILE, width), BF16)],
        (*input_weights, *grads, *d_first_sum, *(swap(v, "wt", 1) for v in input_other)),
    )
    order.held = []
    order.hold(keep_a, keep_b, here)
    arriving = swap(away, "wt", 2)
    for _ in bits[1:]:
        sum_a.fold()
        sum_b.fold()
    for _ in bits[3:]:
        sum_up.fold()
        sum_down.fold()
    (input_grad,) = call(order, "input_grad", input_sum_kernel, [((TILE, width), F32)], (here, arriving))
    summed_down, summed_up = sum_down.last(), sum_up.last()
    piece = (sum_a.keep.shape[0], d_queries.shape[1])
    *summed, small = call(
        order, "grad_w_qkv_sum", last_small_kernel, [(piece, F32)] * 4 + [(small.shape, F32)],
        (sum_a.keep, sum_b.keep, sum_a.small, sum_a.got, sum_b.got),
    )
    head_width = d_queries.shape[1]
    return (
        layer_out, input_grad, *summed, summed_up, summed_down,
        small[7, :head_width], small[7, head_width : 2 * head_width],
        small[5], small[3], small[4], small[6], small[2], small[0], small[1],
    )


def solution(mesh):
    wt = P(None, "wt")
    in_specs = (
        P("ctx", None), P("ctx"), wt, wt, wt, wt, wt, wt, P("wt"), P("wt"),
        P(), P(), P(), P("wt"), P(), P(), P(), P("ctx", None),
    )
    rows = P(("ctx", "wt"), None)
    both = P("ctx", "wt")
    out_specs = (
        rows, rows, both, both, both, both, both, both, P("wt"), P("wt"),
        P(), P(), P(), P("wt"), P(), P(), P(),
    )
    return jax.shard_map(body, mesh=mesh, in_specs=in_specs, out_specs=out_specs, check_vma=False)
```

```python
import functools

import jax
import jax.numpy as jnp
from jax import lax
from jax.experimental import pallas as pl
from jax.experimental.pallas import tpu as pltpu
from jax.sharding import PartitionSpec as P

HEAD_DIM = 64
MAXDOC = 512
TILE = 256
HALO = MAXDOC // TILE
SCALE = HEAD_DIM ** -0.5
SCORE = SCALE * 1.4426950408889634
NEG = -1e30
F32 = jnp.float32
BF16 = jnp.bfloat16
MIB = 1024 * 1024
EXTRA = 16


def dot_nt(left, right):
    return lax.dot_general(left, right, (((1,), (1,)), ((), ())), preferred_element_type=F32)


def dot_nn(left, right):
    return lax.dot_general(left, right, (((1,), (0,)), ((), ())), preferred_element_type=F32)


VMEM = pl.BlockSpec(memory_space=pltpu.VMEM)
SMEM = pl.BlockSpec(memory_space=pltpu.SMEM)
HBM = pl.BlockSpec(memory_space=pltpu.HBM)
HBM_OR_VMEM = pl.BlockSpec(memory_space=pl.ANY)


class Order:
    def __init__(self):
        self.last = ()
        self.held = []

    def hold(self, *arrays):
        self.held += arrays

    def free(self, *arrays):
        self.held = [h for h in self.held if not any(h is a for a in arrays)]


def call(order, name, fn, outs, args, scratch=(), specs=None, limit=16, waits=()):
    held = [h for h in order.held if not any(h is a for a in args)]
    tokens = (*order.last, *waits, *held)
    count = len(tokens) + len(args) + len(outs)

    def kernel(*refs):
        refs[count][...] = jnp.zeros((8, 128), F32)
        fn(*refs[len(tokens) : count], *refs[count + 1 :])

    results = pl.pallas_call(
        kernel,
        in_specs=[HBM_OR_VMEM] * len(tokens) + ([VMEM] * len(args) if specs is None else specs),
        out_specs=[o[2] if len(o) > 2 else VMEM for o in outs] + [VMEM],
        out_shape=[jax.ShapeDtypeStruct(o[0], o[1]) for o in outs] + [jax.ShapeDtypeStruct((8, 128), F32)],
        scratch_shapes=list(scratch),
        compiler_params=pltpu.CompilerParams(vmem_limit_bytes=limit * MIB),
        cost_estimate=pl.CostEstimate(flops=1, bytes_accessed=1, transcendentals=0),
        name=name,
    )(*tokens, *args)
    order.last = (results[-1],)
    return results[:-1]


def position():
    slot, ctx = lax.axis_index("wt"), lax.axis_index("ctx")
    return slot & 1, slot >> 1, ctx, ctx == lax.axis_size("ctx") - 1


def running_count(marks):
    lane = lax.broadcasted_iota(jnp.int32, marks.shape, 1)
    reach = 1
    while reach < marks.shape[1]:
        marks = marks + jnp.where(lane >= reach, pltpu.roll(marks, reach, 1), 0)
        reach *= 2
    return marks


def project_kernel(tok_hbm, wk_hbm, wv_hbm, wq_hbm, bv_hbm, bq_hbm, fl_hbm,
                   tok, kv_ref, q_ref, low_ref, high_ref, seg_ref, bound_sm, wk, wv, wq, bv, bq, fl, sems):
    blocks, width = tok.shape[0] // TILE, wk.shape[1]
    pairs = [(fl_hbm, fl), (bv_hbm, bv), (bq_hbm, bq), (wk_hbm, wk), (wv_hbm, wv), (wq_hbm, wq)]
    first = len(pairs)
    pairs += [(tok_hbm.at[b * TILE : (b + 1) * TILE], tok.at[b * TILE : (b + 1) * TILE]) for b in range(blocks)]
    copies = [pltpu.make_async_copy(a, b, sems.at[n]) for n, (a, b) in enumerate(pairs)]
    for copy in copies:
        copy.start()
    copies[0].wait()
    seg = running_count(jnp.broadcast_to(fl[...], (8, fl.shape[1])))[0:1, :]
    seg_ref[...] = seg
    for b in range(blocks):
        bound_sm[2 * b] = jnp.min(seg[:, b * TILE : (b + 1) * TILE])
        bound_sm[2 * b + 1] = jnp.max(seg[:, b * TILE : (b + 1) * TILE])
    for ref, number in (
        (low_ref, seg[:, :MAXDOC]),
        (high_ref, jnp.max(seg) - seg[:, seg.shape[1] - MAXDOC :]),
    ):
        upper = lax.shift_right_logical(number, 8)
        row = lax.broadcasted_iota(jnp.int32, (EXTRA, MAXDOC), 0)
        digits = jnp.where(row == 0, upper, number - upper * 256)
        ref[MAXDOC:, :MAXDOC] = digits.astype(F32).astype(BF16)
        ref[MAXDOC:, MAXDOC:] = jnp.zeros((EXTRA, ref.shape[1] - MAXDOC), BF16)
    for copy in copies[1:first]:
        copy.wait()
    for b in range(blocks):
        copies[first + b].wait()
        rows = slice(b * TILE, (b + 1) * TILE)
        keys = dot_nn(tok[rows, :], wk[...]).astype(BF16)
        values = (dot_nn(tok[rows, :], wv[...]) + bv[...]).astype(BF16)
        queries = (dot_nn(tok[rows, :], wq[...]) + bq[...]).astype(BF16)
        kv_ref[rows, :width] = keys
        kv_ref[rows, width:] = values
        q_ref[rows, :] = queries
        for ref, at in ((low_ref, b), (high_ref, b - blocks + HALO)):
            if 0 <= at < HALO:
                here = slice(at * TILE, (at + 1) * TILE)
                ref[here, :width] = keys
                ref[here, width : 2 * width] = values
                ref[here, 2 * width :] = queries


def in_hbm(arrays):
    return [pltpu.with_memory_space_constraint(a, pltpu.HBM) for a in arrays]


def project(order, tokens, w_key, w_value, w_query, bias_value, bias_query, flags):
    rows, width = tokens.shape
    cols = w_key.shape[1]
    edge = ((MAXDOC + EXTRA, 3 * cols), BF16)
    blocks = rows // TILE
    params = (tokens, w_key, w_value, w_query, bias_value, bias_query, flags)
    return call(
        order, "project", project_kernel,
        [(tokens.shape, BF16), ((rows, 2 * cols), BF16), ((rows, cols), BF16), edge, edge, ((1, rows), jnp.int32),
         ((2 * blocks,), jnp.int32, SMEM)],
        in_hbm(params),
        scratch=[pltpu.VMEM(p.shape, p.dtype) for p in params[1:]] + [pltpu.SemaphoreType.DMA((6 + blocks,))],
        specs=[HBM] * len(params),
    )


def rows_of(index):
    if isinstance(index, int):
        return pl.ds(index * TILE, TILE)
    return pl.ds(pl.multiple_of(index * TILE, TILE), TILE)


def meet(first_a, last_a, first_b, last_b):
    return jnp.logical_and(first_a <= last_b, last_a >= first_b)


def blocks_meet(bound_sm, a, b):
    return meet(bound_sm[2 * a], bound_sm[2 * a + 1], bound_sm[2 * b], bound_sm[2 * b + 1])


def seg_column(seg_row, index):
    return jnp.broadcast_to(seg_row[:, rows_of(index)], (128, TILE)).T


def edge_segments(seg_row, ref, left):
    digits = ref[MAXDOC : MAXDOC + EXTRA, :MAXDOC].astype(F32)
    segs = (digits[0:1, :] * 256.0 + digits[1:2, :]).astype(jnp.int32)
    if left:
        segs = -segs
    else:
        segs = segs + jnp.max(seg_row[...]) + jnp.where(position()[3], 1, 0)
    pieces = [segs[:, b * TILE : (b + 1) * TILE] for b in range(HALO)]
    return [(piece, jnp.min(piece), jnp.max(piece)) for piece in pieces]


def allowed_of(column, row):
    return jnp.concatenate([column, column], axis=1) == row


def head_mask(value, head):
    lane = lax.broadcasted_iota(jnp.int32, value.shape, 1)
    mine = (lane < HEAD_DIM) if head % 2 == 0 else (lane >= HEAD_DIM)
    return jnp.where(mine, value, jnp.zeros_like(value))


def pair_cols(head, base=0):
    return slice(base + (head // 2) * 128, base + (head // 2) * 128 + 128)


def head_rows(head):
    return slice(head * HEAD_DIM, (head + 1) * HEAD_DIM)


def forward_tile(heads, first, allowed, keys, values_t, q_ref, m_ref, l_ref, acc_ref):
    scores = [dot_nt(keys(head), head_mask(q_ref[:, pair_cols(head)], head)) for head in range(heads)]
    scores = [jnp.where(allowed, s * SCORE, NEG) for s in scores]
    top = jnp.concatenate([jnp.max(s, axis=0, keepdims=True) for s in scores], axis=0)
    if not first:
        before = m_ref[...]
        top = jnp.maximum(before, top)
        keep = jnp.exp2(before - top)
    weights = [jnp.exp2(s - top[head : head + 1, :]) for head, s in enumerate(scores)]
    total = jnp.concatenate([jnp.sum(p, axis=0, keepdims=True) for p in weights], axis=0)
    parts = [dot_nn(values_t(head_rows(head)), p.astype(BF16)) for head, p in enumerate(weights)]
    if first:
        l_ref[...] = total
    else:
        l_ref[...] = l_ref[...] * keep + total
        parts = [acc_ref[head_rows(h), :] * keep[h : h + 1, :] + part for h, part in enumerate(parts)]
    m_ref[...] = top
    for head, part in enumerate(parts):
        acc_ref[head_rows(head), :] = part


def attn_local_kernel(heads, blocks, chunk, bound_sm, seg_row, q_ref, kv_ref, *refs):
    width = heads * HEAD_DIM
    if chunk:
        vt, seg_col, m_ref, l_ref, acc_ref = refs
    else:
        m_ref, l_ref, acc_ref, vt, seg_col = refs
        vt[...] = kv_ref[:, width:].T
        for b in range(blocks):
            seg_col[b * TILE : (b + 1) * TILE, :] = seg_column(seg_row, b)

    def block(step, carry):
        qb = step + chunk * HALO
        qs, here = rows_of(qb), rows_of(step)
        seg_q = seg_row[:, qs]

        def tile(kb, first):
            ks = rows_of(kb)
            forward_tile(
                heads, first, allowed_of(seg_col[ks, :], seg_q),
                lambda head: kv_ref[ks, pair_cols(head)], lambda hd: vt[hd, ks],
                q_ref.at[qs, :], m_ref.at[:, here], l_ref.at[:, here], acc_ref.at[:, here],
            )

        tile(qb, True)

        def other(i, inner):
            kb = qb + i - HALO
            safe = jnp.clip(kb, 0, blocks - 1)

            @pl.when(jnp.logical_and(jnp.logical_and(kb == safe, i != HALO), blocks_meet(bound_sm, safe, qb)))
            def _():
                tile(safe, False)

            return inner

        lax.fori_loop(0, 2 * HALO + 1, other, 0)
        return carry

    lax.fori_loop(0, HALO, block, 0)


def attention_local(order, chunk, bounds, seg, q, kv, shared=()):
    rows, width = q.shape
    heads, blocks = width // HEAD_DIM, rows // TILE
    stat = ((heads, MAXDOC), F32)
    outs = [stat, stat, ((width, MAXDOC), F32)]
    m, l, acc, *rest = call(
        order, f"attention_local_{chunk}",
        functools.partial(attn_local_kernel, heads, blocks, chunk),
        outs if chunk else outs + [((width, rows), BF16), ((rows, 128), jnp.int32)],
        (bounds, seg, q, kv, *shared),
        specs=[SMEM] + [VMEM] * (3 + len(shared)),
    )
    return (m, l, acc), rest


def attn_edge_kernel(
    heads, blocks, base, count,
    bound_sm, seg_row, q_ref, m_in, l_in, acc_in, far_ref, *refs,
):
    sources, (att_ref, lse_ref, mine_ref, other_ref), refs = refs[:count], refs[count : count + 4], refs[count + 4 :]
    held, (m_ref, l_ref, acc_ref, sems) = refs[:count], refs[count:]
    copies = [pltpu.make_async_copy(a, b, sems.at[n]) for n, (a, b) in enumerate(zip(sources, held))]
    for copy in copies:
        copy.start()
    width = heads * HEAD_DIM
    left = base == 0
    edge_segs = edge_segments(seg_row, far_ref, left)
    for step in range(HALO):
        block = step + base
        own = block + HALO
        from_q = slice(block * TILE, (block + 1) * TILE)
        here = slice(step * TILE, (step + 1) * TILE)
        m_ref[...] = m_in[:, here]
        l_ref[...] = l_in[:, here]
        acc_ref[...] = acc_in[:, here]
        seg_q = seg_row[:, from_q]
        for h in range(HALO):
            segs, first, last = edge_segs[h]
            if abs((h if left else h + blocks + HALO) - own) > HALO:
                continue

            @pl.when(meet(first, last, bound_sm[2 * block], bound_sm[2 * block + 1]))
            def _():
                ks = rows_of(h)
                values_t = far_ref[ks, width : 2 * width].T
                forward_tile(
                    heads, False, allowed_of(seg_column(segs, 0), seg_q),
                    lambda head: far_ref[ks, pair_cols(head)], lambda hd: values_t[hd, :],
                    q_ref.at[from_q, :], m_ref, l_ref, acc_ref,
                )

        for head in range(heads):
            row, hd = slice(head, head + 1), head_rows(head)
            total = l_ref[row, :]
            acc_ref[hd, :] = acc_ref[hd, :] * (1.0 / total)
            lse_ref[row, here] = m_ref[row, :] + jnp.log2(total)
        att = acc_ref[...].T.astype(BF16)
        att_ref[here, :] = att

        @pl.when(position()[0] == step)
        def _():
            mine_ref[...] = att

        @pl.when(position()[0] != step)
        def _():
            other_ref[...] = att

    for copy in copies:
        copy.wait()


def attention_edge(order, chunk, bounds, seg, q, local, far, others=()):
    rows, width = q.shape
    heads, blocks = width // HEAD_DIM, rows // TILE
    square = ((TILE, width), BF16)
    att, lse, mine, other, *held = call(
        order, f"attention_edge_{chunk}",
        functools.partial(attn_edge_kernel, heads, blocks, chunk * HALO, len(others)),
        [((MAXDOC, width), BF16), ((heads, MAXDOC), F32), square, square]
        + [(p.shape, p.dtype) for p in others],
        (bounds, seg, q, *local, far, *in_hbm(others)),
        scratch=[
            pltpu.VMEM((heads, TILE), F32), pltpu.VMEM((heads, TILE), F32), pltpu.VMEM((width, TILE), F32),
            pltpu.SemaphoreType.DMA((max(1, len(others)),)),
        ],
        specs=[SMEM] + [VMEM] * 6 + [HBM] * len(others),
    )
    return att, lse, (mine, other), held


def per_head_sums(heads, d, a):
    width = heads * HEAD_DIM
    col = lax.broadcasted_iota(jnp.int32, (8, width), 1) // HEAD_DIM
    row = lax.broadcasted_iota(jnp.int32, (8, width), 0)
    return lax.dot_general(
        (col == row).astype(F32), d.astype(F32) * a.astype(F32), (((1,), (1,)), ((), ())),
        preferred_element_type=F32, precision=lax.Precision.HIGHEST,
    )


def backward_tile(heads, allowed, k_of, v_of, kt, q_of, d_of, lse, delta, dq_add, dkv_add):
    each = range(heads)
    scores = [dot_nt(head_mask(k_of(h), h), q_of(h)) for h in each]
    grads = [dot_nt(head_mask(v_of(h), h), d_of(h)) for h in each]
    probs = [jnp.where(allowed, jnp.exp2(s * SCORE - lse[h : h + 1, :]), 0.0) for h, s in enumerate(scores)]
    ds = [(p * (g - delta[h : h + 1, :])).astype(BF16) for h, (p, g) in enumerate(zip(probs, grads))]
    if dkv_add is not None:
        dk = [dot_nn(ds[h], q_of(h)) for h in each]
        dv = [dot_nn(probs[h].astype(BF16), d_of(h)) for h in each]
    if dq_add is not None:
        dq = [dot_nn(kt[head_rows(h), :], ds[h]) for h in each]
    for h in each:
        if dkv_add is not None:
            dkv_add(h, dk[h], dv[h])
        if dq_add is not None:
            dq_add(h, dq[h])


def merge_pairs(heads, acc):
    lane = lax.broadcasted_iota(jnp.int32, (TILE, 128), 1)
    pieces = [jnp.where(lane < HEAD_DIM, acc[h], acc[h + 1]) for h in range(0, heads, 2)]
    return jnp.concatenate(pieces, axis=1)


def back_local_kernel(
    heads, blocks,
    bound_sm, seg_row, q_ref, kv_ref, lse0, lse1, delta0, delta1, d0, d1,
    dqt_ref, dk_ref, dv_ref,
    dx, lx, delta, dk_acc, dv_acc,
):
    width = heads * HEAD_DIM
    for i, (d, lse, own_delta) in enumerate(((d0, lse0, delta0), (d1, lse1, delta1))):
        part = slice(i * MAXDOC, (i + 1) * MAXDOC)
        dx[part, :] = d[:MAXDOC, :]
        lx[:, part] = lse[...]
        delta[:, part] = own_delta[...]
    dqt_ref[...] = jnp.zeros_like(dqt_ref)

    def block(kb, carry):
        dk_acc[...] = jnp.zeros_like(dk_acc)
        dv_acc[...] = jnp.zeros_like(dv_acc)
        ks = rows_of(kb)
        seg_k = seg_column(seg_row, kb)
        kt = kv_ref[ks, :width].T

        def tile(qb):
            qs = rows_of(qb)

            def dq_add(head, value):
                dqt_ref[head_rows(head), qs] += value

            def dkv_add(head, dk, dv):
                dk_acc[head] += dk
                dv_acc[head] += dv

            backward_tile(
                heads, allowed_of(seg_k, seg_row[:, qs]),
                lambda h: kv_ref[ks, pair_cols(h)], lambda h: kv_ref[ks, pair_cols(h, width)], kt,
                lambda h: q_ref[qs, pair_cols(h)], lambda h: dx[qs, pair_cols(h)],
                lx[:, qs], delta[:, qs], dq_add, dkv_add,
            )

        def other(i, inner):
            qb = kb + i - HALO
            safe = jnp.clip(qb, 0, blocks - 1)

            @pl.when(jnp.logical_and(qb == safe, blocks_meet(bound_sm, safe, kb)))
            def _():
                tile(safe)

            return inner

        lax.fori_loop(0, 2 * HALO + 1, other, 0)
        dk_ref[ks, :] = merge_pairs(heads, dk_acc)
        dv_ref[ks, :] = merge_pairs(heads, dv_acc)
        return carry

    lax.fori_loop(0, blocks, block, 0)


def attention_back_local(order, bounds, seg, q, kv, d_parts, lse_parts, delta_parts):
    rows, width = q.shape
    heads, blocks = width // HEAD_DIM, rows // TILE
    out = ((rows, width), F32)
    return call(
        order, "attention_back_local",
        functools.partial(back_local_kernel, heads, blocks),
        [((width, rows), F32), out, out],
        (bounds, seg, q, kv, *lse_parts, *delta_parts, *d_parts),
        scratch=[
            pltpu.VMEM((rows, width), BF16),
            pltpu.VMEM((heads, rows), F32),
            pltpu.VMEM((heads, rows), F32),
            pltpu.VMEM((heads, TILE, 128), F32),
            pltpu.VMEM((heads, TILE, 128), F32),
        ],
        specs=[SMEM] + [VMEM] * 9,
    )


def digits_of(value):
    rows = []
    for _ in range(3):
        part = value.astype(BF16)
        rows += [part.astype(F32)[:, b * TILE : (b + 1) * TILE] for b in range(HALO)]
        value = value - part.astype(F32)
    return jnp.concatenate(rows, axis=0)


def of_digits(heads, rows):
    digits = [rows[n * HALO * heads : (n + 1) * HALO * heads] for n in range(3)]
    total = digits[0] + digits[1] + digits[2]
    return jnp.concatenate([total[b * heads : (b + 1) * heads] for b in range(HALO)], axis=1)


STATS = 48


def back_edge_kernel(
    heads, blocks,
    bound_sm, seg_row, q_ref, kv_ref, lse0, lse1, delta0, delta1, d0, d1,
    kvq_low, kvq_high, dqt_in, dk_in, dv_in, d_low, d_high,
    dq_ref, dk_ref, dv_ref,
    dqt, dk_acc, dv_acc, stats,
):
    width = heads * HEAD_DIM
    edge_segs = edge_segments(seg_row, kvq_low, True) + edge_segments(seg_row, kvq_high, False)
    low_meets = edge_segs[HALO - 1][2] >= bound_sm[0]
    high_meets = edge_segs[HALO][1] <= bound_sm[2 * blocks - 1]
    for n, (meets, d) in enumerate(((low_meets, d_low), (high_meets, d_high))):

        @pl.when(meets)
        def _():
            rows = d[MAXDOC : MAXDOC + STATS, :].astype(F32)
            stats[n, :heads, :] = of_digits(heads, rows[: STATS // 2])
            stats[n, 8 : 8 + heads, :] = of_digits(heads, rows[STATS // 2 :])

    for step in range(blocks):
        here = slice(step * TILE, (step + 1) * TILE)
        inner = slice((step % HALO) * TILE, (step % HALO + 1) * TILE)
        lse_own, delta_own, d_own = (lse0, delta0, d0) if step < HALO else (lse1, delta1, d1)
        dqt[...] = dqt_in[:, here]
        dk_acc[...] = jnp.zeros_like(dk_acc)
        dv_acc[...] = jnp.zeros_like(dv_acc)

        def dq_add(head, value):
            dqt[head_rows(head), :] += value

        def dkv_add(head, dk, dv):
            dk_acc[head] += dk
            dv_acc[head] += dv

        for h in range(2 * HALO):
            far = h if h < HALO else blocks + h
            if abs(far - step - HALO) > HALO:
                continue
            kvq_far, d_far = (kvq_low, d_low) if h < HALO else (kvq_high, d_high)
            at = slice((h % HALO) * TILE, (h % HALO + 1) * TILE)
            segs, first, last = edge_segs[h]

            @pl.when(meet(first, last, bound_sm[2 * step], bound_sm[2 * step + 1]))
            def _():
                backward_tile(
                    heads, allowed_of(seg_column(segs, 0), seg_row[:, here]),
                    lambda hd: kvq_far[at, pair_cols(hd)], lambda hd: kvq_far[at, pair_cols(hd, width)],
                    kvq_far[at, :width].T,
                    lambda hd: q_ref[here, pair_cols(hd)], lambda hd: d_own[inner, pair_cols(hd)],
                    lse_own[:, inner], delta_own[:, inner], dq_add, None,
                )
                side = h // HALO
                backward_tile(
                    heads, allowed_of(seg_column(seg_row, step), segs),
                    lambda hd: kv_ref[here, pair_cols(hd)], lambda hd: kv_ref[here, pair_cols(hd, width)], None,
                    lambda hd: kvq_far[at, pair_cols(hd, 2 * width)], lambda hd: d_far[at, pair_cols(hd)],
                    stats[side, :heads, at], stats[side, 8:, at], None, dkv_add,
                )

        dq_ref[here, :] = (dqt[...] * SCALE).T.astype(BF16)
        dk_ref[here, :] = ((dk_in[here, :] + merge_pairs(heads, dk_acc)) * SCALE).astype(BF16)
        dv_ref[here, :] = (dv_in[here, :] + merge_pairs(heads, dv_acc)).astype(BF16)


def attention_back_edge(order, bounds, seg, q, kv, d_parts, lse_parts, delta_parts, kvq_far, d_far, local):
    rows, width = q.shape
    heads, blocks = width // HEAD_DIM, rows // TILE
    return call(
        order, "attention_back_edge",
        functools.partial(back_edge_kernel, heads, blocks),
        [((rows, width), BF16)] * 3,
        (bounds, seg, q, kv, *lse_parts, *delta_parts, *d_parts, *kvq_far, *local, *d_far),
        scratch=[
            pltpu.VMEM((width, TILE), F32),
            pltpu.VMEM((heads, TILE, 128), F32),
            pltpu.VMEM((heads, TILE, 128), F32),
            pltpu.VMEM((2, 16, MAXDOC), F32),
        ],
        specs=[SMEM] + [VMEM] * 16,
    )


def moments(value):
    average = jnp.mean(value, axis=-1, keepdims=True)
    centred = value - average
    variance = jnp.mean(centred * centred, axis=-1, keepdims=True)
    scale = lax.rsqrt(variance + 1e-12)
    return centred * scale, scale


def norm_back(grad, normal, scale):
    return scale * (
        grad
        - jnp.mean(grad, axis=-1, keepdims=True)
        - normal * jnp.mean(grad * normal, axis=-1, keepdims=True)
    )


def gelu_both(value):
    half = 0.5 * (1.0 + lax.erf(value * 0.7071067811865476))
    slope = half + value * jnp.exp(-0.5 * value * value) * 0.3989422804014327
    return value * half, slope


PIECE = 64
PIECES = TILE // PIECE


def swap_pieces(pieces):
    return tuple(swap(piece, "wt", 1) for piece in pieces)


def gather(rows, refs):
    for i, ref in enumerate(refs):
        rows[i * PIECE : (i + 1) * PIECE, :] = ref[...]


def scatter(refs, value):
    for i, ref in enumerate(refs):
        ref[...] = value[i * PIECE : (i + 1) * PIECE, :].astype(ref.dtype)


def by_pieces(one):
    for i in range(PIECES):
        one(i, slice(i * PIECE, (i + 1) * PIECE))


def add_sums(ref, rows):
    for i, value in enumerate(rows):
        ref[i : i + 1, :] += jnp.sum(value, axis=0, keepdims=True)


SPLIT = 128


def pick_kernel(value, *outs):
    for i, out in enumerate(outs):
        out[...] = value[i * SPLIT : (i + 1) * SPLIT, :]


def mix_kernel(chunk, tok, w_own, w_core, w_far, w_diag, bias, gain, shift, a_own, a_core, a_far, *refs):
    core, side = position()[:2]
    if chunk:
        pieces, (normal_ref, scale_ref, rows_ref, total, a_diag) = refs[:-5], refs[-5:]
        for i, ref in enumerate(pieces):
            a_diag[i * SPLIT : (i + 1) * SPLIT, :] = ref[...]
    else:
        a_diag, normal_ref, scale_ref, *low_refs, total = refs

    for group in range(1 + chunk):
        at = rows_of(core if group == 0 else 1 - core)
        here = slice(group * TILE, (group + 1) * TILE)
        core_part, far_part, diag_part = (ref[at, :] if chunk else ref[...] for ref in (a_core, a_far, a_diag))
        chip = ((a_own[at, :], w_own), (core_part, w_core))
        far = ((far_part, w_far), (diag_part, w_diag))

        def add_up(pairs):
            total[here, :] = dot_nt(pairs[0][0], pairs[0][1][...])
            for left, right in pairs[1:]:
                total[here, :] += dot_nt(left, right[...])

        @pl.when(side == 0)
        def _():
            add_up(chip + far)

        @pl.when(side != 0)
        def _():
            add_up(far + chip)

        first = (2 * chunk + (core if group == 0 else 1 - core)) * TILE
        for i in range(PIECES):
            piece = slice(group * TILE + i * PIECE, group * TILE + (i + 1) * PIECE)
            there = pl.ds(pl.multiple_of(first + i * PIECE, PIECE), PIECE)
            normal, scale = moments(tok[there, :].astype(F32) + total[piece, :] + bias[...])
            low = (normal * gain[...] + shift[...]).astype(BF16)
            if group == 0:
                normal_ref[piece, :] = normal
                scale_ref[piece, :] = jnp.broadcast_to(scale, (PIECE, 128))
            if chunk:
                rows_ref[piece, :] = low
            else:
                low_refs[i][...] = low


def mix(order, chunk, tokens, att, weights, bias, gain, shift):
    rows, width = tokens.shape
    cols = weights[0].shape[1]
    tall = (1 + chunk) * TILE
    normal, scale, *low = call(
        order, f"mix_{chunk}",
        functools.partial(mix_kernel, chunk),
        [((TILE, width), F32), ((TILE, 128), F32)]
        + ([((2 * TILE, width), BF16)] if chunk else [((PIECE, width), BF16)] * PIECES),
        (tokens, *weights, bias, gain, shift, *att),
        scratch=[pltpu.VMEM((tall, width), F32)] + ([pltpu.VMEM((2 * TILE, cols), BF16)] if chunk else []),
    )
    return normal, scale, low


STRIP = 256


def strips(width, one):
    def step(i, carry):
        one(i, pl.ds(pl.multiple_of(i * STRIP, STRIP), STRIP))
        return carry

    lax.fori_loop(0, width // STRIP, step, 0)


def up_down_kernel(count, w_up, w_down, bias, *refs):
    given, refs = refs[:count], refs[count:]
    hidden_ref, slope_ref, part_mine = refs[:3]
    if count == 1:
        (rows,), part_refs = given, refs[3:]
    else:
        rows, part_refs = refs[3], refs[4:]
        gather(rows, given)

    def one(i, cols):
        active, slope = gelu_both(dot_nn(rows[...], w_up[:, cols]) + bias[:, cols])
        hidden_ref[:, cols] = active.astype(BF16)
        slope_ref[:, cols] = slope.astype(BF16)

    strips(w_up.shape[1], one)
    scatter(part_refs, dot_nt(hidden_ref[TILE:, :], w_down[...]))
    part_mine[...] = dot_nt(hidden_ref[:TILE, :], w_down[...])


def up_down(order, chunk, given, w_up, w_down, bias, waits=()):
    width, hidden = w_up.shape
    both = ((2 * TILE, hidden), BF16)
    collected = [] if len(given) == 1 else [((2 * TILE, width), BF16)]
    hidden, slope, part, *parts = call(
        order, f"up_down_{chunk}", functools.partial(up_down_kernel, len(given)),
        [both, both, ((TILE, width), F32)] + collected + [((PIECE, width), BF16)] * PIECES,
        (w_up, w_down, bias, *given),
        waits=waits,
    )
    rows = parts.pop(0) if collected else given[0]
    return hidden, slope, rows, part, parts


def down_up_kernel(count, w_down, w_up, slope_ref, *refs):
    given, refs = refs[:count], refs[count:]
    inner_ref, sums, part_mine = refs[:3]
    if count == 1:
        (rows,), part_refs = given, refs[3:]
    else:
        rows, part_refs = refs[3], refs[4:]
        gather(rows, given)

    def one(i, cols):
        d_inner = (dot_nn(rows[...], w_down[:, cols]) * slope_ref[:, cols].astype(F32)).astype(BF16)
        inner_ref[:, cols] = d_inner
        sums[:, cols] = jnp.sum(d_inner.astype(F32), axis=0, keepdims=True)

    strips(w_down.shape[1], one)
    scatter(part_refs, dot_nt(inner_ref[TILE:, :], w_up[...]))
    part_mine[...] = dot_nt(inner_ref[:TILE, :], w_up[...])


def down_up_rows(order, chunk, rows, w_down, w_up, slope):
    width, hidden = w_up.shape
    inner, sums, part, *parts = call(
        order, f"down_up_{chunk}", functools.partial(down_up_kernel, 1),
        [((2 * TILE, hidden), BF16), ((1, hidden), F32), ((TILE, width), F32)] + [((PIECE, width), BF16)] * PIECES,
        (w_down, w_up, slope, rows),
    )
    return inner, sums, part, parts


def down_up(order, chunk, mine, other, w_down, w_up, slope):
    width, hidden = w_up.shape
    inner, sums, part, rows, *parts = call(
        order, f"down_up_{chunk}", functools.partial(down_up_kernel, 2 * PIECES),
        [((2 * TILE, hidden), BF16), ((1, hidden), F32), ((TILE, width), F32), ((2 * TILE, width), BF16)]
        + [((PIECE, width), BF16)] * PIECES,
        (w_down, w_up, slope, *mine, *other),
    )
    return inner, sums, rows, part, parts


def chip_sum_kernel(mine, *refs):
    out = refs[-1]
    for i, ref in enumerate(refs[:-1]):
        here = slice(i * PIECE, (i + 1) * PIECE)
        out[here, :] = (mine[here, :] + ref[...].astype(F32)).astype(BF16)


def chip_sum(order, name, mine, parts, waits=()):
    return call(order, name, chip_sum_kernel, [(mine.shape, BF16)], (mine, *swap_pieces(parts)), waits=waits)[0]


def end_kernel(chunk, normal, chip, cot, mid_gain, mid_bias, bias, gain, shift, *refs):
    before, refs = (refs[:2], refs[2:]) if chunk else ((), refs)
    far, out_ref, d_ref, sums = refs[:4]
    low_refs = refs[4:]
    core, side = position()[:2]
    sums[...] = before[1][...] if before else jnp.zeros_like(sums)
    first = (2 * chunk + core) * TILE

    def one(i, here):
        there = pl.ds(pl.multiple_of(first + i * PIECE, PIECE), PIECE)
        both = chip[here, :].astype(F32) + far[here, :].astype(F32)
        second = (normal[here, :] * mid_gain[...] + mid_bias[...]) + both + bias[...]
        unit, scale = moments(second)
        value = (unit * gain[...] + shift[...]).astype(BF16)
        if before:
            value = jnp.where(side == chunk, value, before[0][here, :])
        out_ref[here, :] = value
        upstream = cot[there, :].astype(F32)
        d_second = norm_back(upstream * gain[...], unit, scale)
        low = d_second.astype(BF16)
        d_ref[here, :] = d_second
        low_refs[i][...] = low
        add_sums(sums, (upstream * unit, upstream, low.astype(F32)))

    by_pieces(one)


def end(order, chunk, normal, chip, far, cotangent, vectors, before, waits=()):
    rows, width = normal.shape
    out, d, sums, *low = call(
        order, f"end_{chunk}",
        functools.partial(end_kernel, chunk),
        [((rows, width), BF16), ((rows, width), F32), ((8, width), F32)] + [((PIECE, width), BF16)] * PIECES,
        (normal, chip, cotangent, *vectors, *before, far),
        waits=waits,
    )
    return out, d, sums, low


def mid_kernel(count, d_second, chip, normal, scale, gain, far, *refs):
    before, (d_ref, sums), low_refs = refs[:count], refs[count : count + 2], refs[count + 2 :]
    sums[...] = before[0][...] if before else jnp.zeros_like(sums)

    def one(i, here):
        d_first = d_second[here, :] + (chip[here, :].astype(F32) + far[here, :].astype(F32))
        unit = normal[here, :]
        d_sum = norm_back(d_first * gain[...], unit, scale[here, 0:1])
        low = d_sum.astype(BF16)
        d_ref[here, :] = d_sum
        low_refs[i][...] = low
        add_sums(sums, (d_first * unit, d_first, low.astype(F32)))

    by_pieces(one)


def mid(order, chunk, d_second, chip, far, normal, scale, gain, before, waits=()):
    rows, width = normal.shape
    d, sums, *low = call(
        order, f"mid_{chunk}", functools.partial(mid_kernel, len(before)),
        [((rows, width), F32), ((8, width), F32)] + [((PIECE, width), BF16)] * PIECES,
        (d_second, chip, normal, scale, gain, far, *before),
        waits=waits,
    )
    return d, sums, low


def d_att_kernel(heads, w_out, att, lse, *refs):
    mine, other, (out, rows, delta_ref) = refs[:PIECES], refs[PIECES : 2 * PIECES], refs[2 * PIECES :]
    core = position()[0]
    here = pl.ds(pl.multiple_of(core * TILE, TILE), TILE)
    there = pl.ds(pl.multiple_of((1 - core) * TILE, TILE), TILE)
    gather(rows.at[here, :], mine)
    gather(rows.at[there, :], other)
    d = dot_nn(rows[...], w_out[...]).astype(BF16)
    out[:MAXDOC, :] = d
    delta = per_head_sums(heads, d, att[...])[:heads]
    delta_ref[...] = delta
    out[MAXDOC:, :] = jnp.concatenate([digits_of(lse[...]), digits_of(delta)], axis=0).astype(BF16)


def d_att(order, chunk, mine, other, w_out, att, lse):
    width, cols = w_out.shape
    heads = cols // HEAD_DIM
    return call(
        order, f"d_attended_{chunk}", functools.partial(d_att_kernel, heads),
        [((MAXDOC + STATS, cols), BF16), ((2 * TILE, width), BF16), ((heads, MAXDOC), F32)],
        (w_out, att, lse, *mine, *other),
    )


def part_of(refs, weights, block):
    rows = pl.ds(pl.multiple_of(block * TILE, TILE), TILE)
    total = None
    for ref, weight in zip(refs, weights):
        part = dot_nt(ref[rows, :], weight[...])
        total = part if total is None else total + part
    return total


def input_other_kernel(wq, wk, wv, dq, dk, dv, *others):
    for j in range(2):
        block = 2 * j + 1 - position()[0]
        scatter(others[j * PIECES : (j + 1) * PIECES], part_of((dq, dk, dv), (wq, wk, wv), block))


def input_mine_kernel(wq, wk, wv, dq, dk, dv, d0, d1, *refs):
    got, (here, away) = refs[: 2 * PIECES], refs[2 * PIECES :]
    core, side = position()[:2]
    weights = (wq, wk, wv)

    def chip(j):
        parts = [ref[...].astype(F32) for ref in got[j * PIECES : (j + 1) * PIECES]]
        return part_of((dq, dk, dv), weights, 2 * j + core) + jnp.concatenate(parts, axis=0)

    for mine, d in ((0, d0), (1, d1)):

        @pl.when(side == mine)
        def _():
            here[...] = chip(mine) + d[...]

        @pl.when(side != mine)
        def _():
            away[...] = chip(mine).astype(BF16)


def input_sum_kernel(here, got, out):
    out[...] = here[...] + got[...].astype(F32)


def halves(tall, bit, rows):
    size = (1 << bit[0]) * rows
    mine = (position()[2] >> bit[1]) & 1
    for n in range(tall // (2 * size)):
        for own, side in ((True, mine), (False, 1 - mine)):
            yield own, pl.ds(pl.multiple_of((2 * n + side) * size, size), size), slice(n * size, (n + 1) * size)


def transpose_halves(ref, out, at, bit, rows):
    here = slice(at, at + ref.shape[0])
    half = ref.shape[1] // 2
    size = (1 << bit[0]) * rows
    if size % 128:
        split = ref[...].T.reshape(half // size, 2, size, ref.shape[0])
        zero, one = split[:, 0].reshape(half, ref.shape[0]), split[:, 1].reshape(half, ref.shape[0])
        own = ((position()[2] >> bit[1]) & 1) == 0
        out[:half, here] = jnp.where(own, zero, one)
        out[half:, here] = jnp.where(own, one, zero)
        return
    for own, source, target in halves(ref.shape[1], bit, rows):
        first = target.start + (0 if own else half)
        size = target.stop - target.start
        out[first : first + size, here] = ref[:, source].T


def weight_grad_kernel(bit, rows, count, *refs):
    lefts, rights = refs[:count], refs[count : 2 * count]
    keep_ref, give_ref, left_t = refs[2 * count :]
    at = 0
    for ref in lefts:
        transpose_halves(ref, left_t, at, bit, rows)
        at += ref.shape[0]
    half = left_t.shape[0] // 2
    for first in range(0, keep_ref.shape[1], 256):
        cols = slice(first, first + 256)
        for out, side in ((keep_ref, slice(0, half)), (give_ref, slice(half, 2 * half))):
            total, at = None, 0
            for ref in rights:
                part = dot_nn(left_t[side, at : at + ref.shape[0]], ref[:, cols])
                total = part if total is None else total + part
                at += ref.shape[0]
            out[:, cols] = total.astype(BF16)


def weight_grad(order, name, lefts, rights, bit, ctx_count, waits=()):
    width, cols = lefts[0].shape[1], rights[0].shape[1]
    tall = sum(left.shape[0] for left in lefts)
    return call(
        order, name,
        functools.partial(weight_grad_kernel, (bit, bit), width // ctx_count, len(lefts)),
        [((width // 2, cols), BF16)] * 2, (*lefts, *rights),
        scratch=[pltpu.VMEM((width, tall), BF16)],
        waits=waits,
    )


SMALL = 8


def two_digits(small, width):
    flat = [small[:, at : at + width] for at in range(0, small.shape[1], width)]
    value = jnp.concatenate(flat, axis=0)
    upper = value.astype(BF16)
    return jnp.concatenate([upper, (value - upper.astype(F32)).astype(BF16)], axis=0)


def from_digits(rows, width):
    half = rows.shape[0] // 2
    value = rows[:half].astype(F32) + rows[half:].astype(F32)
    return jnp.concatenate([value[at : at + SMALL] for at in range(0, half, SMALL)], axis=1)


def qkv_grad_kernel(
    bits, rows, tokens, end_own, end_far, mid_own, mid_far, up_0, up_1, dq, dk, dv,
    keep_q, give_q, keep_k, give_k, keep_v, give_v, small_ref, tok_t, tok_v,
):
    for out, bit in ((tok_t, bits[0]), (tok_v, bits[1])):
        transpose_halves(tokens, out, 0, (bit, bit), rows)
    width, half = dq.shape[1], tok_t.shape[0] // 2
    small_ref[0:3, :] = end_own[0:3, :] + end_far[0:3, :]
    small_ref[3:6, :] = mid_own[0:3, :] + mid_far[0:3, :]
    small_ref[6:7, :] = up_0[...] + up_1[...]
    small_ref[7:8, :] = jnp.zeros_like(small_ref[7:8, :])
    small_ref[7:8, :width] = jnp.sum(dq[...].astype(F32), axis=0, keepdims=True)
    small_ref[7:8, width : 2 * width] = jnp.sum(dv[...].astype(F32), axis=0, keepdims=True)
    give_q[half:, :] = two_digits(small_ref[...], width)
    for left, ref, keep, give in ((tok_t, dq, keep_q, give_q), (tok_t, dk, keep_k, give_k), (tok_v, dv, keep_v, give_v)):
        give[:half, :] = dot_nn(left[half:, :], ref[...]).astype(BF16)
        keep[...] = dot_nn(left[:half, :], ref[...]).astype(BF16)


def small_rows(width, cols):
    return 2 * SMALL * (width // cols)


def qkv_grad(order, tokens, sums, dq, dk, dv, bits, ctx_count):
    width, cols = tokens.shape[1], dq.shape[1]
    half = ((width // 2, cols), BF16)
    return call(
        order, "grad_w_qkv",
        functools.partial(qkv_grad_kernel, bits, width // ctx_count),
        [half, ((width // 2 + small_rows(width, cols), cols), BF16), half, half, half, half, ((SMALL, width), F32)],
        (tokens, *sums, dq, dk, dv),
        scratch=[pltpu.VMEM(tokens.shape[::-1], BF16)] * 2,
    )


def fold_rows(keep, got, bit, rows, keep_ref, give_ref):
    for own, source, target in halves(keep.shape[0], bit, rows):
        total = keep[source, :].astype(F32) + got[source, :].astype(F32)
        (keep_ref if own else give_ref)[target, :] = total.astype(BF16)


def fold_small_kernel(bit, rows, keep, small, got, keep_ref, give_ref, small_ref):
    tall, cols = keep.shape
    fold_rows(keep, got, bit, rows, keep_ref, give_ref)
    own = from_digits(two_digits(small[...], cols), cols)
    value = own + from_digits(got[tall:, :], cols)
    small_ref[...] = value
    give_ref[tall // 2 :, :] = two_digits(value, cols)


def last_small_kernel(keep_q, keep_k, keep_v, small, got_q, got_k, got_v, q, k, v, *rows):
    tall, width = keep_q.shape
    for keep, got, out in ((keep_q, got_q, q), (keep_k, got_k, k), (keep_v, got_v, v)):
        out[...] = keep[...].astype(F32) + got[:tall, :].astype(F32)
    value = from_digits(two_digits(small[...], width), width) + from_digits(got_q[tall:, :], width)
    for n, row in enumerate(rows[:7]):
        row[...] = value[n : n + 1, :]
    for n, row in enumerate(rows[7:]):
        row[...] = value[7:8, n * width : (n + 1) * width]


def fold_kernel(bit, rows, keep, got, keep_ref, give_ref):
    fold_rows(keep, got, bit, rows, keep_ref, give_ref)


def last_kernel(keep, got, out):
    out[...] = keep[...].astype(F32) + got[...].astype(F32)


class ScatterSum:
    def __init__(self, order, name, keep, give, bits, ctx_count, small=None):
        self.order, self.name, self.bits, self.small = order, name, bits, small
        self.left = list(range(ctx_count.bit_length() - 1))
        self.keep, self.give, self.done = keep, give, 0
        self.rows = keep.shape[0] * 2 // ctx_count

    def send(self):
        self.got = swap(self.give, "ctx", 1 << self.bits[self.done])
        return self

    def fold(self, waits=(), after=None):
        self.left.remove(self.bits[self.done])
        self.done += 1
        tall, width = self.keep.shape
        bit = self.bits[self.done]
        half = ((tall // 2, width), BF16)
        if self.small is not None:
            extra = small_rows(self.small.shape[1], width)
            self.keep, self.give, self.small = call(
                self.order, f"{self.name}_fold_{self.done}",
                functools.partial(fold_small_kernel, (self.left.index(bit), bit), self.rows),
                [half, ((tall // 2 + extra, width), BF16), (self.small.shape, F32)],
                (self.keep, self.small, self.got), waits=waits,
            )
            return self.send()
        self.keep, self.give = call(
            self.order, f"{self.name}_fold_{self.done}",
            functools.partial(fold_kernel, (self.left.index(bit), bit), self.rows),
            [half, half], (self.keep, self.got), waits=waits,
        )
        if after is not None:
            self.keep, self.give, self.beside = after(self.keep, self.give)
        return self.send()

    def last(self):
        return call(
            self.order, f"{self.name}_sum", last_kernel, [(self.keep.shape, F32)], (self.keep, self.got)
        )[0]


def swap(value, axis, mask):
    return lax.ppermute(value, axis, [(i, i ^ mask) for i in range(lax.axis_size(axis))])


def from_left(value, axis):
    return lax.ppermute(value, axis, [(i, i + 1) for i in range(lax.axis_size(axis) - 1)])


def from_right(value, axis):
    return lax.ppermute(value, axis, [(i + 1, i) for i in range(lax.axis_size(axis) - 1)])


def body(
    tokens, flags, w_query, w_key, w_value, w_out, w_up, w_down, bias_query, bias_value, bias_out,
    mid_gain, mid_bias, bias_up, bias_down, end_gain, end_bias, cotangent,
):
    rows, width = tokens.shape
    assert rows == 4 * TILE == 2 * MAXDOC
    ctx_count = lax.axis_size("ctx")
    bits = list(range(ctx_count.bit_length() - 1))
    turned = bits[1:] + bits[:1]
    order = Order()
    biases = [v[None] for v in (bias_out, mid_gain, mid_bias, bias_up, bias_down, end_gain, end_bias)]

    w_far = swap(w_out, "wt", 2)
    tokens, kv, queries, to_left, to_right, seg, bounds = project(
        order, tokens, w_key, w_value, w_query, bias_value[None], bias_query[None], flags[None]
    )
    kvq_low = from_left(to_right, "ctx")
    order.hold(tokens, kv, queries)
    local_0, shared = attention_local(order, 0, bounds, seg, queries, kv)
    order.hold(*local_0)
    local_1, _ = attention_local(order, 1, bounds, seg, queries, kv, shared)
    kvq_low, to_left, *local_1 = lax.optimization_barrier((kvq_low, to_left, *local_1))
    kvq_high = from_right(to_left, "ctx")
    order.hold(*local_1)
    w_diag = swap(w_far, "wt", 1)

    att_0, lse_0, (mine, other), held = attention_edge(
        order, 0, bounds, seg, queries, local_0, kvq_low, (w_out, w_up, w_down, cotangent, *biases)
    )
    order.free(*local_0)
    w_out, w_up, w_down, cotangent, bias_out, mid_gain, mid_bias, bias_up, bias_down, end_gain, end_bias = held
    w_core = swap(w_out, "wt", 1)
    weights = (w_out, w_core, w_far, w_diag)
    order.hold(w_out, w_up, w_down, cotangent, att_0)
    pieces = (att_0, swap(other, "wt", 1), swap(mine, "wt", 2), swap(other, "wt", 3))
    n_0, s_0, lo = mix(order, 0, tokens, pieces, weights, bias_out, mid_gain, mid_bias)
    order.hold(n_0, s_0)
    att_1, lse_1, _, _ = attention_edge(order, 1, bounds, seg, queries, local_1, kvq_high)
    order.free(*local_1)
    order.hold(att_1)
    att_far = swap(att_1, "wt", 2)
    h_0, sl_0, low_0, part, parts = up_down(order, 0, (*lo, *swap_pieces(lo)), w_up, w_down, bias_up)
    order.hold(h_0, sl_0, low_0)
    picked = call(order, "far_rows", pick_kernel, [((SPLIT, att_1.shape[1]), BF16)] * 4, (att_far,))
    chip_0 = chip_sum(order, "second_0", part, parts)
    far_0 = swap(chip_0, "wt", 2)
    pieces = (att_1, swap(att_1, "wt", 1), att_far, *swap_pieces(picked))
    n_1, s_1, lo = mix(order, 1, tokens, pieces, weights, bias_out, mid_gain, mid_bias)
    h_1, sl_1, low_1, part, parts = up_down(order, 1, lo, w_up, w_down, bias_up)
    order.hold(n_1, s_1, h_1, sl_1, low_1)
    chip_1 = chip_sum(order, "second_1", part, parts)
    far_1 = swap(chip_1, "wt", 2)
    att, lse, normal, scale = (att_0, att_1), (lse_0, lse_1), (n_0, n_1), (s_0, s_1)
    hidden, slope, low, chip, far = (h_0, h_1), (sl_0, sl_1), (low_0, low_1), (chip_0, chip_1), (far_0, far_1)

    vectors = (mid_gain, mid_bias, bias_down, end_gain, end_bias)
    out, d_second_0, sums, lo = end(order, 0, normal[0], chip[0], far[0], cotangent, vectors, ())
    d_inner_0, up_sums_0, down_0, *part = down_up(order, 0, lo, swap_pieces(lo), w_down, w_up, slope[0])
    order.hold(d_second_0, d_inner_0, down_0)
    d_chip_0 = chip_sum(order, "first_0", *part, (far[1],))
    d_far_0 = swap(d_chip_0, "wt", 2)
    layer_out, d_second_1, end_sums, lo = end(
        order, 1, normal[1], chip[1], far[1], cotangent, vectors, (out, sums)
    )
    d_inner_1, up_sums_1, down_1, part, parts = down_up(
        order, 1, lo, swap_pieces(lo), w_down, w_up, slope[1]
    )
    order.hold(d_second_1, d_inner_1)
    order.free(w_up, w_down, *slope, cotangent)
    keep, give = weight_grad(order, "grad_w_down", (down_0, down_1), hidden, bits[0], ctx_count)
    order.free(*hidden, down_0)
    sum_down = ScatterSum(order, "grad_w_down", keep, give, bits, ctx_count).send()
    d_chip_1 = chip_sum(order, "first_1", part, parts)
    d_far_1 = swap(d_chip_1, "wt", 2)
    keep, give = weight_grad(order, "grad_w_up", low, (d_inner_0, d_inner_1), turned[0], ctx_count)
    order.free(*low, d_inner_0, d_inner_1)
    sum_up = ScatterSum(order, "grad_w_up", keep, give, turned, ctx_count).send()
    d_first_sum_0, sums, lo = mid(order, 0, d_second_0, d_chip_0, d_far_0, normal[0], scale[0], mid_gain, ())
    order.hold(d_first_sum_0)
    order.free(d_second_0, normal[0], scale[0])
    d_attended_0, mixed_0, delta_0 = d_att(order, 0, lo, swap_pieces(lo), w_out, att[0], lse[0])
    order.hold(d_attended_0, mixed_0)
    d_first_sum_1, mid_sums, lo = mid(
        order, 1, d_second_1, d_chip_1, d_far_1, normal[1], scale[1], mid_gain, (sums,)
    )
    order.hold(d_first_sum_1)
    order.free(d_second_1, normal[1], scale[1])
    d_attended_1, mixed_1, delta_1 = d_att(order, 1, lo, swap_pieces(lo), w_out, att[1], lse[1])
    order.hold(d_attended_1, mixed_1)
    order.free(w_out)
    d_low, d_high = from_left(d_attended_1, "ctx"), from_right(d_attended_0, "ctx")
    d_attended, delta, mixed = (d_attended_0, d_attended_1), (delta_0, delta_1), (mixed_0, mixed_1)
    d_first_sum, up_sums = (d_first_sum_0, d_first_sum_1), (up_sums_0, up_sums_1)

    local = attention_back_local(order, bounds, seg, queries, kv, d_attended, lse, delta)
    sum_up.fold((d_low, d_high))
    sum_down.fold()
    keep, give = weight_grad(order, "grad_w_out", mixed, att, bits[0], ctx_count)
    order.free(*mixed, *att)
    sum_out = ScatterSum(order, "grad_w_out", keep, give, bits, ctx_count).send()

    d_queries, d_keys, d_values = attention_back_edge(
        order, bounds, seg, queries, kv, d_attended, lse, delta, (kvq_low, kvq_high), (d_low, d_high), local,
    )
    order.free(queries, kv, *d_attended)
    grads = (d_queries, d_keys, d_values)
    order.hold(*grads)
    sums = (end_sums, swap(end_sums, "wt", 1), mid_sums, swap(mid_sums, "wt", 1), *up_sums)
    *parts, small = qkv_grad(order, tokens, sums, *grads, (bits[0], bits[0]), ctx_count)
    order.free(tokens)
    order.hold(*parts[::2])
    sums_qkv = [
        ScatterSum(order, f"grad_w_{name}", parts[2 * n], parts[2 * n + 1], way, ctx_count, None if n else small).send()
        for n, (name, way) in enumerate((("q", bits), ("k", bits), ("v", bits)))
    ]
    sum_q, sum_k, sum_v = sums_qkv
    input_weights = (w_query, w_key, w_value)
    input_other = call(
        order, "input_other", input_other_kernel, [((PIECE, width), BF16)] * (2 * PIECES), (*input_weights, *grads)
    )
    input_far = swap_pieces(input_other)
    sum_out.fold()
    sum_down.fold()
    here, away = call(
        order, "input_mine", input_mine_kernel, [((TILE, width), F32), ((TILE, width), BF16)],
        (*input_weights, *grads, *d_first_sum, *input_far),
    )
    order.held = []
    order.hold(here)
    arriving = swap(away, "wt", 2)
    for part in (sum_q, sum_up, sum_k, sum_q, sum_out, sum_v, sum_k, sum_v):
        part.fold()
    for _ in bits[3:]:
        for part in (sum_up, sum_down, sum_out, *sums_qkv):
            part.fold()
    (input_grad,) = call(order, "input_grad", input_sum_kernel, [((TILE, width), F32)], (here, arriving))
    summed_down = sum_down.last()
    summed_out = sum_out.last()
    summed_up = sum_up.last()
    piece = (sums_qkv[0].keep.shape[0], d_queries.shape[1])
    wide, narrow = ((1, width), F32), ((1, d_queries.shape[1]), F32)
    *summed, g_end_gain, g_end_bias, g_down, g_mid_gain, g_mid_bias, g_out, g_up, g_query, g_value = call(
        order, "grad_w_qkv_sum", last_small_kernel, [(piece, F32)] * 3 + [wide] * 7 + [narrow] * 2,
        (*(part.keep for part in sums_qkv), sums_qkv[0].small, *(part.got for part in sums_qkv)),
    )
    vectors = (g_query, g_value, g_out, g_mid_gain, g_mid_bias, g_up, g_down, g_end_gain, g_end_bias)
    return (
        layer_out, input_grad, *summed, summed_out, summed_up, summed_down, *(v.reshape(-1) for v in vectors)
    )


def solution(mesh):
    wt = P(None, "wt")
    in_specs = (
        P("ctx", None), P("ctx"), wt, wt, wt, wt, wt, wt, P("wt"), P("wt"),
        P(), P(), P(), P("wt"), P(), P(), P(), P("ctx", None),
    )
    rows = P(("ctx", "wt"), None)
    both = P("ctx", "wt")
    out_specs = (
        rows, rows, both, both, both, both, both, both, P("wt"), P("wt"),
        P(), P(), P(), P("wt"), P(), P(), P(),
    )
    return jax.shard_map(body, mesh=mesh, in_specs=in_specs, out_specs=out_specs, check_vma=False)
```

```python
import functools
import types

import jax
import jax.numpy as jnp
from jax import lax
from jax.experimental import pallas as pl
from jax.experimental.pallas import tpu as pltpu
from jax.sharding import PartitionSpec as P

HEAD_DIM = 64
MAXDOC = 512
TILE = 256
HALO = MAXDOC // TILE
SCALE = HEAD_DIM ** -0.5
SCORE = SCALE * 1.4426950408889634
NEG = -1e30
F32 = jnp.float32
BF16 = jnp.bfloat16
MIB = 1024 * 1024
EXTRA = 16
CTX, WT = "ctx", "wt"
SPLITS = (96, 80, 80)
LAST_SPLITS = (256,)
INPUT_SPLITS = (128, 128, 128, 128)
CUTS = (512,)


def dot_nt(left, right):
    return lax.dot_general(left, right, (((1,), (1,)), ((), ())), preferred_element_type=F32)


def dot_nn(left, right):
    return lax.dot_general(left, right, (((1,), (0,)), ((), ())), preferred_element_type=F32)


VMEM = pl.BlockSpec(memory_space=pltpu.VMEM)
SMEM = pl.BlockSpec(memory_space=pltpu.SMEM)
HBM = pl.BlockSpec(memory_space=pltpu.HBM)
HBM_OR_VMEM = pl.BlockSpec(memory_space=pl.ANY)


class Order:
    def __init__(self):
        self.last = ()
        self.held = []

    def hold(self, *arrays):
        self.held += arrays

    def free(self, *arrays):
        self.held = [h for h in self.held if not any(h is a for a in arrays)]


def call(order, name, fn, outs, args, scratch=(), specs=None, limit=16, waits=()):
    held = [h for h in order.held if not any(h is a for a in args)]
    tokens = (*order.last, *waits, *held)
    count = len(tokens) + len(args) + len(outs)

    def kernel(*refs):
        refs[count][...] = jnp.zeros((8, 128), F32)
        fn(*refs[len(tokens) : count], *refs[count + 1 :])

    results = pl.pallas_call(
        kernel,
        in_specs=[HBM_OR_VMEM] * len(tokens) + ([VMEM] * len(args) if specs is None else specs),
        out_specs=[o[2] if len(o) > 2 else VMEM for o in outs] + [VMEM],
        out_shape=[jax.ShapeDtypeStruct(o[0], o[1]) for o in outs] + [jax.ShapeDtypeStruct((8, 128), F32)],
        scratch_shapes=list(scratch),
        compiler_params=pltpu.CompilerParams(vmem_limit_bytes=limit * MIB),
        cost_estimate=pl.CostEstimate(flops=1, bytes_accessed=1, transcendentals=0),
        name=name,
    )(*tokens, *args)
    order.last = (results[-1],)
    return results[:-1]


def position():
    slot, ctx = lax.axis_index(WT), lax.axis_index(CTX)
    return slot & 1, slot >> 1, ctx, ctx == lax.axis_size(CTX) - 1


def running_count(marks):
    lane = lax.broadcasted_iota(jnp.int32, marks.shape, 1)
    reach = 1
    while reach < marks.shape[1]:
        marks = marks + jnp.where(lane >= reach, pltpu.roll(marks, reach, 1), 0)
        reach *= 2
    return marks


def keys_kernel(tok_hbm, wk_hbm, wv_hbm, bv_hbm, fl_hbm,
                tok, kv_ref, low_ref, high_ref, seg_ref, bound_sm, wk, wv, bv, fl, sems):
    blocks, width = tok.shape[0] // TILE, wk.shape[1]
    pairs = [(fl_hbm, fl), (bv_hbm, bv), (wk_hbm, wk), (wv_hbm, wv)]
    first = len(pairs)
    pairs += [(tok_hbm.at[b * TILE : (b + 1) * TILE], tok.at[b * TILE : (b + 1) * TILE]) for b in range(blocks)]
    copies = [pltpu.make_async_copy(a, b, sems.at[n]) for n, (a, b) in enumerate(pairs)]
    for copy in copies:
        copy.start()
    copies[0].wait()
    seg = running_count(jnp.broadcast_to(fl[...], (8, fl.shape[1])))[0:1, :]
    seg_ref[...] = seg
    for b in range(blocks):
        bound_sm[2 * b] = jnp.min(seg[:, b * TILE : (b + 1) * TILE])
        bound_sm[2 * b + 1] = jnp.max(seg[:, b * TILE : (b + 1) * TILE])
    for ref, number in (
        (low_ref, seg[:, :MAXDOC]),
        (high_ref, jnp.max(seg) - seg[:, seg.shape[1] - MAXDOC :]),
    ):
        upper = lax.shift_right_logical(number, 8)
        row = lax.broadcasted_iota(jnp.int32, (EXTRA, MAXDOC), 0)
        digits = jnp.where(row == 0, upper, number - upper * 256)
        ref[MAXDOC:, :MAXDOC] = digits.astype(F32).astype(BF16)
    for copy in copies[1:first]:
        copy.wait()
    for b in range(blocks):
        copies[first + b].wait()
        rows = slice(b * TILE, (b + 1) * TILE)
        keys = dot_nn(tok[rows, :], wk[...]).astype(BF16)
        values = (dot_nn(tok[rows, :], wv[...]) + bv[...]).astype(BF16)
        kv_ref[rows, :width] = keys
        kv_ref[rows, width:] = values
        for ref, at in ((low_ref, b), (high_ref, b - blocks + HALO)):
            if 0 <= at < HALO:
                here = slice(at * TILE, (at + 1) * TILE)
                ref[here, :width] = keys
                ref[here, width:] = values


def queries_kernel(tok, wq_hbm, bq_hbm, q_ref, low_ref, high_ref, wq, bq, sems):
    copies = [pltpu.make_async_copy(wq_hbm, wq, sems.at[0]), pltpu.make_async_copy(bq_hbm, bq, sems.at[1])]
    for copy in copies:
        copy.start()
    for copy in copies:
        copy.wait()
    blocks = tok.shape[0] // TILE
    for b in range(blocks):
        rows = slice(b * TILE, (b + 1) * TILE)
        queries = (dot_nn(tok[rows, :], wq[...]) + bq[...]).astype(BF16)
        q_ref[rows, :] = queries
        for ref, at in ((low_ref, b), (high_ref, b - blocks + HALO)):
            if 0 <= at < HALO:
                ref[at * TILE : (at + 1) * TILE, :] = queries


def in_hbm(arrays):
    return [pltpu.with_memory_space_constraint(a, pltpu.HBM) for a in arrays]


def project_keys(order, tokens, w_key, w_value, bias_value, flags):
    rows, width = tokens.shape
    cols = w_key.shape[1]
    edge = ((MAXDOC + EXTRA, 2 * cols), BF16)
    blocks = rows // TILE
    params = (tokens, w_key, w_value, bias_value, flags)
    return call(
        order, "keys", keys_kernel,
        [(tokens.shape, BF16), ((rows, 2 * cols), BF16), edge, edge, ((1, rows), jnp.int32),
         ((2 * blocks,), jnp.int32, SMEM)],
        in_hbm(params),
        scratch=[pltpu.VMEM(p.shape, p.dtype) for p in params[1:]] + [pltpu.SemaphoreType.DMA((4 + blocks,))],
        specs=[HBM] * len(params),
    )


def project_queries(order, tokens, w_query, bias_query):
    rows, cols = tokens.shape[0], w_query.shape[1]
    edge = ((MAXDOC, cols), BF16)
    return call(
        order, "queries", queries_kernel, [((rows, cols), BF16), edge, edge],
        (tokens, *in_hbm((w_query, bias_query))),
        scratch=[pltpu.VMEM(w_query.shape, BF16), pltpu.VMEM(bias_query.shape, F32), pltpu.SemaphoreType.DMA((2,))],
        specs=[VMEM, HBM, HBM],
    )


def rows_of(index):
    if isinstance(index, int):
        return pl.ds(index * TILE, TILE)
    return pl.ds(pl.multiple_of(index * TILE, TILE), TILE)


def meet(first_a, last_a, first_b, last_b):
    return jnp.logical_and(first_a <= last_b, last_a >= first_b)


def blocks_meet(bound_sm, a, b):
    return meet(bound_sm[2 * a], bound_sm[2 * a + 1], bound_sm[2 * b], bound_sm[2 * b + 1])


def seg_column(seg_row, index):
    return jnp.broadcast_to(seg_row[:, rows_of(index)], (128, TILE)).T


def edge_segments(seg_row, ref, left):
    digits = ref[MAXDOC : MAXDOC + EXTRA, :MAXDOC].astype(F32)
    segs = (digits[0:1, :] * 256.0 + digits[1:2, :]).astype(jnp.int32)
    if left:
        segs = -segs
    else:
        segs = segs + jnp.max(seg_row[...]) + jnp.where(position()[3], 1, 0)
    pieces = [segs[:, b * TILE : (b + 1) * TILE] for b in range(HALO)]
    return [(piece, jnp.min(piece), jnp.max(piece)) for piece in pieces]


def allowed_of(column, row):
    return jnp.concatenate([column, column], axis=1) == row


def head_mask(value, head):
    lane = lax.broadcasted_iota(jnp.int32, value.shape, 1)
    mine = (lane < HEAD_DIM) if head % 2 == 0 else (lane >= HEAD_DIM)
    return jnp.where(mine, value, jnp.zeros_like(value))


def pair_cols(head, base=0):
    return slice(base + (head // 2) * 128, base + (head // 2) * 128 + 128)


def head_rows(head):
    return slice(head * HEAD_DIM, (head + 1) * HEAD_DIM)


def forward_tile(heads, first, allowed, keys, values_t, q_ref, m_ref, l_ref, acc_ref):
    scores = [dot_nt(keys(head), head_mask(q_ref[:, pair_cols(head)], head)) for head in range(heads)]
    scores = [jnp.where(allowed, s * SCORE, NEG) for s in scores]
    top = jnp.concatenate([jnp.max(s, axis=0, keepdims=True) for s in scores], axis=0)
    if not first:
        before = m_ref[...]
        top = jnp.maximum(before, top)
        keep = jnp.exp2(before - top)
    weights = [jnp.exp2(s - top[head : head + 1, :]) for head, s in enumerate(scores)]
    total = jnp.concatenate([jnp.sum(p, axis=0, keepdims=True) for p in weights], axis=0)
    parts = [dot_nn(values_t(head_rows(head)), p.astype(BF16)) for head, p in enumerate(weights)]
    if first:
        l_ref[...] = total
    else:
        l_ref[...] = l_ref[...] * keep + total
        parts = [acc_ref[head_rows(h), :] * keep[h : h + 1, :] + part for h, part in enumerate(parts)]
    m_ref[...] = top
    for head, part in enumerate(parts):
        acc_ref[head_rows(head), :] = part


def attn_local_kernel(heads, blocks, chunk, bound_sm, seg_row, q_ref, kv_ref, *refs):
    width = heads * HEAD_DIM
    if chunk:
        vt, seg_col, m_ref, l_ref, acc_ref = refs
    else:
        m_ref, l_ref, acc_ref, vt, seg_col = refs
        vt[...] = kv_ref[:, width:].T
        for b in range(blocks):
            seg_col[b * TILE : (b + 1) * TILE, :] = seg_column(seg_row, b)

    def block(step, carry):
        qb = step + chunk * HALO
        qs, here = rows_of(qb), rows_of(step)
        seg_q = seg_row[:, qs]

        def tile(kb, first):
            ks = rows_of(kb)
            forward_tile(
                heads, first, allowed_of(seg_col[ks, :], seg_q),
                lambda head: kv_ref[ks, pair_cols(head)], lambda hd: vt[hd, ks],
                q_ref.at[qs, :], m_ref.at[:, here], l_ref.at[:, here], acc_ref.at[:, here],
            )

        tile(qb, True)

        def other(i, inner):
            kb = qb + i - HALO
            safe = jnp.clip(kb, 0, blocks - 1)

            @pl.when(jnp.logical_and(jnp.logical_and(kb == safe, i != HALO), blocks_meet(bound_sm, safe, qb)))
            def _():
                tile(safe, False)

            return inner

        lax.fori_loop(0, 2 * HALO + 1, other, 0)
        return carry

    lax.fori_loop(0, HALO, block, 0)


def attention_local(order, chunk, bounds, seg, q, kv, shared=()):
    rows, width = q.shape
    heads, blocks = width // HEAD_DIM, rows // TILE
    stat = ((heads, MAXDOC), F32)
    outs = [stat, stat, ((width, MAXDOC), F32)]
    m, l, acc, *rest = call(
        order, "local",
        functools.partial(attn_local_kernel, heads, blocks, chunk),
        outs if chunk else outs + [((width, rows), BF16), ((rows, 128), jnp.int32)],
        (bounds, seg, q, kv, *shared),
        specs=[SMEM] + [VMEM] * (3 + len(shared)),
    )
    return (m, l, acc), rest


def attn_edge_kernel(
    heads, blocks, base, count,
    bound_sm, seg_row, q_ref, m_in, l_in, acc_in, far_ref, *refs,
):
    sources, (att_ref, lse_ref, mine_ref, other_ref), refs = refs[:count], refs[count : count + 4], refs[count + 4 :]
    held, (m_ref, l_ref, acc_ref, sems) = refs[:count], refs[count:]
    copies = [pltpu.make_async_copy(a, b, sems.at[n]) for n, (a, b) in enumerate(zip(sources, held))]
    for copy in copies:
        copy.start()
    width = heads * HEAD_DIM
    left = base == 0
    edge_segs = edge_segments(seg_row, far_ref, left)
    for step in range(HALO):
        block = step + base
        own = block + HALO
        from_q = slice(block * TILE, (block + 1) * TILE)
        here = slice(step * TILE, (step + 1) * TILE)
        m_ref[...] = m_in[:, here]
        l_ref[...] = l_in[:, here]
        acc_ref[...] = acc_in[:, here]
        seg_q = seg_row[:, from_q]
        for h in range(HALO):
            segs, first, last = edge_segs[h]
            if abs((h if left else h + blocks + HALO) - own) > HALO:
                continue

            @pl.when(meet(first, last, bound_sm[2 * block], bound_sm[2 * block + 1]))
            def _():
                ks = rows_of(h)
                values_t = far_ref[ks, width : 2 * width].T
                forward_tile(
                    heads, False, allowed_of(seg_column(segs, 0), seg_q),
                    lambda head: far_ref[ks, pair_cols(head)], lambda hd: values_t[hd, :],
                    q_ref.at[from_q, :], m_ref, l_ref, acc_ref,
                )

        for head in range(heads):
            row, hd = slice(head, head + 1), head_rows(head)
            total = l_ref[row, :]
            acc_ref[hd, :] = acc_ref[hd, :] * (1.0 / total)
            lse_ref[row, here] = m_ref[row, :] + jnp.log2(total)
        att = acc_ref[...].T.astype(BF16)
        att_ref[here, :] = att

        @pl.when(position()[0] == step)
        def _():
            mine_ref[...] = att

        @pl.when(position()[0] != step)
        def _():
            other_ref[...] = att

    for copy in copies:
        copy.wait()


def attention_edge(order, chunk, bounds, seg, q, local, far, others=()):
    rows, width = q.shape
    heads, blocks = width // HEAD_DIM, rows // TILE
    square = ((TILE, width), BF16)
    att, lse, mine, other, *held = call(
        order, "edge",
        functools.partial(attn_edge_kernel, heads, blocks, chunk * HALO, len(others)),
        [((MAXDOC, width), BF16), ((heads, MAXDOC), F32), square, square]
        + [(p.shape, p.dtype) for p in others],
        (bounds, seg, q, *local, far, *in_hbm(others)),
        scratch=[
            pltpu.VMEM((heads, TILE), F32), pltpu.VMEM((heads, TILE), F32), pltpu.VMEM((width, TILE), F32),
            pltpu.SemaphoreType.DMA((max(1, len(others)),)),
        ],
        specs=[SMEM] + [VMEM] * 6 + [HBM] * len(others),
    )
    return att, lse, (mine, other), held


def per_head_sums(heads, d, a):
    width = heads * HEAD_DIM
    col = lax.broadcasted_iota(jnp.int32, (8, width), 1) // HEAD_DIM
    row = lax.broadcasted_iota(jnp.int32, (8, width), 0)
    return lax.dot_general(
        (col == row).astype(F32), d.astype(F32) * a.astype(F32), (((1,), (1,)), ((), ())),
        preferred_element_type=F32, precision=lax.Precision.HIGHEST,
    )


def backward_tile(heads, allowed, k_of, v_of, kt, q_of, d_of, lse, delta, dq_add, dkv_add):
    each = range(heads)
    scores = [dot_nt(head_mask(k_of(h), h), q_of(h)) for h in each]
    grads = [dot_nt(head_mask(v_of(h), h), d_of(h)) for h in each]
    probs = [jnp.where(allowed, jnp.exp2(s * SCORE - lse[h : h + 1, :]), 0.0) for h, s in enumerate(scores)]
    ds = [(p * (g - delta[h : h + 1, :])).astype(BF16) for h, (p, g) in enumerate(zip(probs, grads))]
    if dkv_add is not None:
        dk = [dot_nn(ds[h], q_of(h)) for h in each]
        dv = [dot_nn(probs[h].astype(BF16), d_of(h)) for h in each]
    if dq_add is not None:
        dq = [dot_nn(kt[head_rows(h), :], ds[h]) for h in each]
    for h in each:
        if dkv_add is not None:
            dkv_add(h, dk[h], dv[h])
        if dq_add is not None:
            dq_add(h, dq[h])


def merge_pairs(heads, acc):
    lane = lax.broadcasted_iota(jnp.int32, (TILE, 128), 1)
    pieces = [jnp.where(lane < HEAD_DIM, acc[h], acc[h + 1]) for h in range(0, heads, 2)]
    return jnp.concatenate(pieces, axis=1)


def back_local_kernel(
    heads, blocks,
    bound_sm, seg_row, q_ref, kv_ref, lse0, lse1, delta0, delta1, d0, d1,
    dqt_ref, dk_ref, dv_ref,
    dx, lx, delta, dk_acc, dv_acc,
):
    width = heads * HEAD_DIM
    for i, (d, lse, own_delta) in enumerate(((d0, lse0, delta0), (d1, lse1, delta1))):
        part = slice(i * MAXDOC, (i + 1) * MAXDOC)
        dx[part, :] = d[:MAXDOC, :]
        lx[:, part] = lse[...]
        delta[:, part] = own_delta[...]
    dqt_ref[...] = jnp.zeros_like(dqt_ref)

    def block(kb, carry):
        dk_acc[...] = jnp.zeros_like(dk_acc)
        dv_acc[...] = jnp.zeros_like(dv_acc)
        ks = rows_of(kb)
        seg_k = seg_column(seg_row, kb)
        kt = kv_ref[ks, :width].T

        def tile(qb):
            qs = rows_of(qb)

            def dq_add(head, value):
                dqt_ref[head_rows(head), qs] += value

            def dkv_add(head, dk, dv):
                dk_acc[head] += dk
                dv_acc[head] += dv

            backward_tile(
                heads, allowed_of(seg_k, seg_row[:, qs]),
                lambda h: kv_ref[ks, pair_cols(h)], lambda h: kv_ref[ks, pair_cols(h, width)], kt,
                lambda h: q_ref[qs, pair_cols(h)], lambda h: dx[qs, pair_cols(h)],
                lx[:, qs], delta[:, qs], dq_add, dkv_add,
            )

        def other(i, inner):
            qb = kb + i - HALO
            safe = jnp.clip(qb, 0, blocks - 1)

            @pl.when(jnp.logical_and(qb == safe, blocks_meet(bound_sm, safe, kb)))
            def _():
                tile(safe)

            return inner

        lax.fori_loop(0, 2 * HALO + 1, other, 0)
        dk_ref[ks, :] = merge_pairs(heads, dk_acc)
        dv_ref[ks, :] = merge_pairs(heads, dv_acc)
        return carry

    lax.fori_loop(0, blocks, block, 0)


def attention_back_local(order, bounds, seg, q, kv, d_parts, lse_parts, delta_parts):
    rows, width = q.shape
    heads, blocks = width // HEAD_DIM, rows // TILE
    out = ((rows, width), F32)
    return call(
        order, "back_local",
        functools.partial(back_local_kernel, heads, blocks),
        [((width, rows), F32), out, out],
        (bounds, seg, q, kv, *lse_parts, *delta_parts, *d_parts),
        scratch=[
            pltpu.VMEM((rows, width), BF16),
            pltpu.VMEM((heads, rows), F32),
            pltpu.VMEM((heads, rows), F32),
            pltpu.VMEM((heads, TILE, 128), F32),
            pltpu.VMEM((heads, TILE, 128), F32),
        ],
        specs=[SMEM] + [VMEM] * 9,
    )


def digits_of(value):
    rows = []
    for _ in range(3):
        part = value.astype(BF16)
        rows += [part.astype(F32)[:, b * TILE : (b + 1) * TILE] for b in range(HALO)]
        value = value - part.astype(F32)
    return jnp.concatenate(rows, axis=0)


def of_digits(heads, rows):
    digits = [rows[n * HALO * heads : (n + 1) * HALO * heads] for n in range(3)]
    total = digits[0] + digits[1] + digits[2]
    return jnp.concatenate([total[b * heads : (b + 1) * heads] for b in range(HALO)], axis=1)


STATS = 48


def back_edge_kernel(
    heads, blocks,
    bound_sm, seg_row, q_ref, kv_ref, lse0, lse1, delta0, delta1, d0, d1,
    kv_low, kv_high, q_low, q_high, dqt_in, dk_in, dv_in, d_low, d_high,
    dq_ref, dk_ref, dv_ref,
    dqt, dk_acc, dv_acc, stats,
):
    width = heads * HEAD_DIM
    edge_segs = edge_segments(seg_row, kv_low, True) + edge_segments(seg_row, kv_high, False)
    low_meets = edge_segs[HALO - 1][2] >= bound_sm[0]
    high_meets = edge_segs[HALO][1] <= bound_sm[2 * blocks - 1]
    for n, (meets, d) in enumerate(((low_meets, d_low), (high_meets, d_high))):

        @pl.when(meets)
        def _():
            rows = d[MAXDOC : MAXDOC + STATS, :].astype(F32)
            stats[n, :heads, :] = of_digits(heads, rows[: STATS // 2])
            stats[n, 8 : 8 + heads, :] = of_digits(heads, rows[STATS // 2 :])

    for step in range(blocks):
        here = slice(step * TILE, (step + 1) * TILE)
        inner = slice((step % HALO) * TILE, (step % HALO + 1) * TILE)
        lse_own, delta_own, d_own = (lse0, delta0, d0) if step < HALO else (lse1, delta1, d1)
        dqt[...] = dqt_in[:, here]
        dk_acc[...] = jnp.zeros_like(dk_acc)
        dv_acc[...] = jnp.zeros_like(dv_acc)

        def dq_add(head, value):
            dqt[head_rows(head), :] += value

        def dkv_add(head, dk, dv):
            dk_acc[head] += dk
            dv_acc[head] += dv

        for h in range(2 * HALO):
            far = h if h < HALO else blocks + h
            if abs(far - step - HALO) > HALO:
                continue
            kv_far, q_far, d_far = (kv_low, q_low, d_low) if h < HALO else (kv_high, q_high, d_high)
            at = slice((h % HALO) * TILE, (h % HALO + 1) * TILE)
            segs, first, last = edge_segs[h]

            @pl.when(meet(first, last, bound_sm[2 * step], bound_sm[2 * step + 1]))
            def _():
                backward_tile(
                    heads, allowed_of(seg_column(segs, 0), seg_row[:, here]),
                    lambda hd: kv_far[at, pair_cols(hd)], lambda hd: kv_far[at, pair_cols(hd, width)],
                    kv_far[at, :width].T,
                    lambda hd: q_ref[here, pair_cols(hd)], lambda hd: d_own[inner, pair_cols(hd)],
                    lse_own[:, inner], delta_own[:, inner], dq_add, None,
                )
                side = h // HALO
                backward_tile(
                    heads, allowed_of(seg_column(seg_row, step), segs),
                    lambda hd: kv_ref[here, pair_cols(hd)], lambda hd: kv_ref[here, pair_cols(hd, width)], None,
                    lambda hd: q_far[at, pair_cols(hd)], lambda hd: d_far[at, pair_cols(hd)],
                    stats[side, :heads, at], stats[side, 8:, at], None, dkv_add,
                )

        dq_ref[here, :] = (dqt[...] * SCALE).T.astype(BF16)
        dk_ref[here, :] = ((dk_in[here, :] + merge_pairs(heads, dk_acc)) * SCALE).astype(BF16)
        dv_ref[here, :] = (dv_in[here, :] + merge_pairs(heads, dv_acc)).astype(BF16)


def attention_back_edge(order, bounds, seg, q, kv, d_parts, lse_parts, delta_parts, kv_far, q_far, d_far, local):
    rows, width = q.shape
    heads, blocks = width // HEAD_DIM, rows // TILE
    return call(
        order, "back_edge",
        functools.partial(back_edge_kernel, heads, blocks),
        [((rows, width), BF16)] * 3,
        (bounds, seg, q, kv, *lse_parts, *delta_parts, *d_parts, *kv_far, *q_far, *local, *d_far),
        scratch=[
            pltpu.VMEM((width, TILE), F32),
            pltpu.VMEM((heads, TILE, 128), F32),
            pltpu.VMEM((heads, TILE, 128), F32),
            pltpu.VMEM((2, 16, MAXDOC), F32),
        ],
        specs=[SMEM] + [VMEM] * 18,
    )


def moments(value):
    average = jnp.mean(value, axis=-1, keepdims=True)
    centred = value - average
    variance = jnp.mean(centred * centred, axis=-1, keepdims=True)
    scale = lax.rsqrt(variance + 1e-12)
    return centred * scale, scale


def norm_back(grad, normal, scale):
    return scale * (
        grad
        - jnp.mean(grad, axis=-1, keepdims=True)
        - normal * jnp.mean(grad * normal, axis=-1, keepdims=True)
    )


def gelu_both(value):
    half = 0.5 * (1.0 + lax.erf(value * 0.7071067811865476))
    slope = half + value * jnp.exp(-0.5 * value * value) * 0.3989422804014327
    return value * half, slope


PARTS = tuple((sum(SPLITS[:n]), rows) for n, rows in enumerate(SPLITS))
PIECES = len(PARTS)


def pieces_of(width):
    return [((count, width), BF16) for _, count in PARTS]


def swap_pieces(pieces):
    return tuple(swap(piece, WT, 1) for piece in pieces)


def gather(rows, refs):
    if len(refs) == 1:
        rows[...] = refs[0][...]
        return
    start = 0
    for ref in refs:
        rows[start : start + ref.shape[0], :] = ref[...]
        start += ref.shape[0]


def scatter(refs, value):
    for (start, count), ref in zip(PARTS, refs):
        ref[...] = value[start : start + count, :].astype(ref.dtype)


def by_pieces(one):
    for i, (start, count) in enumerate(PARTS):
        one(i, slice(start, start + count))


def add_sums(ref, first, rows):
    for i, value in enumerate(rows, first):
        ref[i : i + 1, :] += jnp.sum(value, axis=0, keepdims=True)


SPLIT = 128


def pick_kernel(value, *outs):
    for i, out in enumerate(outs):
        out[...] = value[i * SPLIT : (i + 1) * SPLIT, :]


def mix_kernel(chunk, tok, w_own, w_core, w_far, w_diag, bias, gain, shift, a_own, a_core, a_far, *refs):
    core, side = position()[:2]
    if chunk:
        pieces, (normal_ref, scale_ref, rows_ref, total, a_diag) = refs[:-5], refs[-5:]
        for i, ref in enumerate(pieces):
            a_diag[i * SPLIT : (i + 1) * SPLIT, :] = ref[...]
    else:
        a_diag, normal_ref, scale_ref, *low_refs, total = refs

    for group in range(1 + chunk):
        at = rows_of(core if group == 0 else 1 - core)
        here = slice(group * TILE, (group + 1) * TILE)
        core_part, far_part, diag_part = (ref[at, :] if chunk else ref[...] for ref in (a_core, a_far, a_diag))
        chip = ((a_own[at, :], w_own), (core_part, w_core))
        far = ((far_part, w_far), (diag_part, w_diag))

        def add_up(pairs):
            total[here, :] = dot_nt(pairs[0][0], pairs[0][1][...])
            for left, right in pairs[1:]:
                total[here, :] += dot_nt(left, right[...])

        @pl.when(side == 0)
        def _():
            add_up(chip + far)

        @pl.when(side != 0)
        def _():
            add_up(far + chip)

        first = (2 * chunk + (core if group == 0 else 1 - core)) * TILE
        for i, (start, rows) in enumerate(PARTS):
            piece = slice(group * TILE + start, group * TILE + start + rows)
            there = pl.ds(pl.multiple_of(first + start, 16), rows)
            normal, scale = moments(tok[there, :].astype(F32) + total[piece, :] + bias[...])
            low = (normal * gain[...] + shift[...]).astype(BF16)
            if group == 0:
                normal_ref[piece, :] = normal
                scale_ref[piece, :] = jnp.broadcast_to(scale, (rows, 128))
            if chunk:
                rows_ref[piece, :] = low
            else:
                low_refs[i][...] = low


def mix(order, chunk, tokens, att, weights, bias, gain, shift):
    rows, width = tokens.shape
    cols = weights[0].shape[1]
    tall = (1 + chunk) * TILE
    normal, scale, *low = call(
        order, "mix",
        functools.partial(mix_kernel, chunk),
        [((TILE, width), F32), ((TILE, 128), F32)]
        + ([((2 * TILE, width), BF16)] if chunk else pieces_of(width)),
        (tokens, *weights, bias, gain, shift, *att),
        scratch=[pltpu.VMEM((tall, width), F32)] + ([pltpu.VMEM((2 * TILE, cols), BF16)] if chunk else []),
    )
    return normal, scale, low


STRIP = 256


def strips(width, one):
    def step(i, carry):
        one(i, pl.ds(pl.multiple_of(i * STRIP, STRIP), STRIP))
        return carry

    lax.fori_loop(0, width // STRIP, step, 0)


def up_down_kernel(count, w_up, w_down, bias, *refs):
    given, refs = refs[:count], refs[count:]
    hidden_ref, slope_ref, part_mine = refs[:3]
    if count == 1:
        (rows,), part_refs = given, refs[3:]
    else:
        rows, part_refs = refs[3], refs[4:]
        gather(rows.at[:TILE, :], given[:PIECES])
        gather(rows.at[TILE:, :], given[PIECES:])

    def one(i, cols):
        active, slope = gelu_both(dot_nn(rows[...], w_up[:, cols]) + bias[:, cols])
        hidden_ref[:, cols] = active.astype(BF16)
        slope_ref[:, cols] = slope.astype(BF16)

    strips(w_up.shape[1], one)
    scatter(part_refs, dot_nt(hidden_ref[TILE:, :], w_down[...]))
    part_mine[...] = dot_nt(hidden_ref[:TILE, :], w_down[...])


def up_down(order, chunk, given, w_up, w_down, bias, waits=()):
    width, hidden = w_up.shape
    both = ((2 * TILE, hidden), BF16)
    collected = [] if len(given) == 1 else [((2 * TILE, width), BF16)]
    hidden, slope, part, *parts = call(
        order, "up_down", functools.partial(up_down_kernel, len(given)),
        [both, both, ((TILE, width), F32)] + collected + pieces_of(width),
        (w_up, w_down, bias, *given),
        waits=waits,
    )
    rows = parts.pop(0) if collected else given[0]
    return hidden, slope, rows, part, parts


def down_up_kernel(count, w_down, w_up, slope_ref, *refs):
    given, refs = refs[:count], refs[count:]
    inner_ref, sums, part_mine = refs[:3]
    if count == 1:
        (rows,), part_refs = given, refs[3:]
    else:
        rows, part_refs = refs[3], refs[4:]
        gather(rows.at[:TILE, :], given[:PIECES])
        gather(rows.at[TILE:, :], given[PIECES:])

    def one(i, cols):
        d_inner = (dot_nn(rows[...], w_down[:, cols]) * slope_ref[:, cols].astype(F32)).astype(BF16)
        inner_ref[:, cols] = d_inner
        sums[:, cols] = jnp.sum(d_inner.astype(F32), axis=0, keepdims=True)

    strips(w_down.shape[1], one)
    scatter(part_refs, dot_nt(inner_ref[TILE:, :], w_up[...]))
    part_mine[...] = dot_nt(inner_ref[:TILE, :], w_up[...])


def down_up_rows(order, chunk, rows, w_down, w_up, slope):
    width, hidden = w_up.shape
    inner, sums, part, *parts = call(
        order, "down_up", functools.partial(down_up_kernel, 1),
        [((2 * TILE, hidden), BF16), ((1, hidden), F32), ((TILE, width), F32)] + pieces_of(width),
        (w_down, w_up, slope, rows),
    )
    return inner, sums, part, parts


def down_up(order, chunk, mine, other, w_down, w_up, slope):
    width, hidden = w_up.shape
    inner, sums, part, rows, *parts = call(
        order, "down_up", functools.partial(down_up_kernel, 2 * PIECES),
        [((2 * TILE, hidden), BF16), ((1, hidden), F32), ((TILE, width), F32), ((2 * TILE, width), BF16)]
        + pieces_of(width),
        (w_down, w_up, slope, *mine, *other),
    )
    return inner, sums, rows, part, parts


def chip_sum_kernel(mine, *refs):
    out = refs[-1]
    for i, ref in enumerate(refs[:-1]):
        here = slice(PARTS[i][0], sum(PARTS[i]))
        out[here, :] = (mine[here, :] + ref[...].astype(F32)).astype(BF16)


def chip_sum(order, name, mine, parts, waits=()):
    return call(order, name, chip_sum_kernel, [(mine.shape, BF16)], (mine, *swap_pieces(parts)), waits=waits)[0]


def end_kernel(chunk, normal, chip, cot, mid_gain, mid_bias, bias, gain, shift, *refs):
    before, refs = (refs[:2], refs[2:]) if chunk else ((), refs)
    far, out_ref, d_ref, sums = refs[:4]
    low_refs = refs[4:]
    core, side = position()[:2]
    sums[...] = before[1][...] if before else jnp.zeros_like(sums)
    first = (2 * chunk + core) * TILE

    def one(i, here):
        there = pl.ds(pl.multiple_of(first + PARTS[i][0], 16), PARTS[i][1])
        both = chip[here, :].astype(F32) + far[here, :].astype(F32)
        second = (normal[here, :] * mid_gain[...] + mid_bias[...]) + both + bias[...]
        unit, scale = moments(second)
        value = (unit * gain[...] + shift[...]).astype(BF16)
        if before:
            value = jnp.where(side == chunk, value, before[0][here, :])
        out_ref[here, :] = value
        upstream = cot[there, :].astype(F32)
        d_second = norm_back(upstream * gain[...], unit, scale)
        low = d_second.astype(BF16)
        d_ref[here, :] = d_second
        low_refs[i][...] = low
        add_sums(sums, 0, (upstream * unit, upstream, low.astype(F32)))

    by_pieces(one)


def end(order, chunk, normal, chip, far, cotangent, vectors, before, waits=()):
    rows, width = normal.shape
    out, d, sums, *low = call(
        order, "end",
        functools.partial(end_kernel, chunk),
        [((rows, width), BF16), ((rows, width), F32), ((8, width), F32)] + pieces_of(width),
        (normal, chip, cotangent, *vectors, *before, far),
        waits=waits,
    )
    return out, d, sums, low


def mid_kernel(d_second, chip, normal, scale, gain, before, far, d_ref, sums, *low_refs):
    sums[...] = before[...]

    def one(i, here):
        d_first = d_second[here, :] + (chip[here, :].astype(F32) + far[here, :].astype(F32))
        unit = normal[here, :]
        d_sum = norm_back(d_first * gain[...], unit, scale[here, 0:1])
        low = d_sum.astype(BF16)
        d_ref[here, :] = d_sum
        if len(low_refs) == len(PARTS):
            low_refs[i][...] = low
        else:
            low_refs[0][here, :] = low
        add_sums(sums, 3, (d_first * unit, d_first, low.astype(F32)))

    by_pieces(one)


def mid(order, chunk, d_second, chip, far, normal, scale, gain, before, waits=()):
    rows, width = normal.shape
    d, sums, *low = call(
        order, "mid", mid_kernel,
        [((rows, width), F32), ((8, width), F32)] + ([((rows, width), BF16)] if chunk and LAST_SPLITS == (256,) else pieces_of(width)),
        (d_second, chip, normal, scale, gain, before, far),
        waits=waits,
    )
    return d, sums, low


def d_att_kernel(heads, w_out, att, lse, *refs):
    count = (len(refs) - 3) // 2
    mine, other, (out, rows, delta_ref) = refs[:count], refs[count : 2 * count], refs[2 * count :]
    core = position()[0]
    here = pl.ds(pl.multiple_of(core * TILE, TILE), TILE)
    there = pl.ds(pl.multiple_of((1 - core) * TILE, TILE), TILE)
    gather(rows.at[here, :], mine)
    gather(rows.at[there, :], other)
    d = dot_nn(rows[...], w_out[...]).astype(BF16)
    out[:MAXDOC, :] = d
    delta = per_head_sums(heads, d, att[...])[:heads]
    delta_ref[...] = delta
    out[MAXDOC:, :] = jnp.concatenate([digits_of(lse[...]), digits_of(delta)], axis=0).astype(BF16)


def d_att(order, chunk, mine, other, w_out, att, lse):
    width, cols = w_out.shape
    heads = cols // HEAD_DIM
    return call(
        order, "d_att", functools.partial(d_att_kernel, heads),
        [((MAXDOC + STATS, cols), BF16), ((2 * TILE, width), BF16), ((heads, MAXDOC), F32)],
        (w_out, att, lse, *mine, *other),
    )


def part_of(refs, weights, block):
    rows = pl.ds(pl.multiple_of(block * TILE, TILE), TILE)
    total = None
    for ref, weight in zip(refs, weights):
        part = dot_nt(ref[rows, :], weight[...])
        total = part if total is None else total + part
    return total


def input_other_kernel(wq, wk, wv, dq, dk, dv, *others):
    for j in range(2):
        block = 2 * j + 1 - position()[0]
        part = part_of((dq, dk, dv), (wq, wk, wv), block).astype(BF16)
        each = len(others) // 2
        for n, ref in enumerate(others[j * each : (j + 1) * each] if each else others):
            rows = slice(n * ref.shape[0], (n + 1) * ref.shape[0]) if each else slice(0, TILE)
            (ref if each else ref.at[j * TILE : (j + 1) * TILE, :])[...] = part[rows]


def input_mine_kernel(wq, wk, wv, dq, dk, dv, d0, d1, *refs):
    got, (here, away) = refs[:-2], refs[-2:]
    core, side = position()[:2]

    def chip(j):
        each = len(got) // 2
        if each:
            far = jnp.concatenate([ref[...].astype(F32) for ref in got[j * each : (j + 1) * each]], axis=0)
        else:
            far = got[0][j * TILE : (j + 1) * TILE, :].astype(F32)
        return part_of((dq, dk, dv), (wq, wk, wv), 2 * j + core) + far

    for mine, d in ((0, d0), (1, d1)):

        @pl.when(side == mine)
        def _():
            here[...] = chip(mine) + d[...]

        @pl.when(side != mine)
        def _():
            away[...] = chip(mine).astype(BF16)


def input_sum_kernel(here, got, out):
    out[...] = here[...] + got[...].astype(F32)


def halves(tall, bit, rows):
    size = (1 << bit[0]) * rows
    mine = (position()[2] >> bit[1]) & 1
    for n in range(tall // (2 * size)):
        for own, side in ((True, mine), (False, 1 - mine)):
            yield own, pl.ds(pl.multiple_of((2 * n + side) * size, size), size), slice(n * size, (n + 1) * size)


def transpose_halves(ref, out, at, bit, rows):
    here = slice(at, at + ref.shape[0])
    half = ref.shape[1] // 2
    size = (1 << bit[0]) * rows
    if size % 128:
        split = ref[...].T.reshape(half // size, 2, size, ref.shape[0])
        zero, one = split[:, 0].reshape(half, ref.shape[0]), split[:, 1].reshape(half, ref.shape[0])
        own = ((position()[2] >> bit[1]) & 1) == 0
        out[:half, here] = jnp.where(own, zero, one)
        out[half:, here] = jnp.where(own, one, zero)
        return
    for own, source, target in halves(ref.shape[1], bit, rows):
        first = target.start + (0 if own else half)
        size = target.stop - target.start
        out[first : first + size, here] = ref[:, source].T


def weight_grad_kernel(bit, rows, count, *refs):
    lefts, rights = refs[:count], refs[count : 2 * count]
    keep_ref, give_ref, left_t = refs[2 * count :]
    at = 0
    for ref in lefts:
        transpose_halves(ref, left_t, at, bit, rows)
        at += ref.shape[0]
    half = left_t.shape[0] // 2
    for first in range(0, keep_ref.shape[1], 256):
        cols = slice(first, first + 256)
        for out, side in ((keep_ref, slice(0, half)), (give_ref, slice(half, 2 * half))):
            total, at = None, 0
            for ref in rights:
                part = dot_nn(left_t[side, at : at + ref.shape[0]], ref[:, cols])
                total = part if total is None else total + part
                at += ref.shape[0]
            out[:, cols] = total.astype(BF16)


def weight_grad(order, name, lefts, rights, bit, ctx_count, waits=()):
    width, cols = lefts[0].shape[1], rights[0].shape[1]
    tall = sum(left.shape[0] for left in lefts)
    return call(
        order, name,
        functools.partial(weight_grad_kernel, (bit, bit), width // ctx_count, len(lefts)),
        [((width // 2, cols), BF16)] * 2, (*lefts, *rights),
        scratch=[pltpu.VMEM((width, tall), BF16)],
        waits=waits,
    )


SMALL = 8


def two_digits(small, width):
    flat = [small[:, at : at + width] for at in range(0, small.shape[1], width)]
    value = jnp.concatenate(flat, axis=0)
    upper = value.astype(BF16)
    return jnp.concatenate([upper, (value - upper.astype(F32)).astype(BF16)], axis=0)


def from_digits(rows, width):
    half = rows.shape[0] // 2
    value = rows[:half].astype(F32) + rows[half:].astype(F32)
    return jnp.concatenate([value[at : at + SMALL] for at in range(0, half, SMALL)], axis=1)


def groups_of(width):
    cuts = (0, *CUTS, 3 * width)
    return list(zip(cuts[:-1], cuts[1:]))


def small_width(group):
    return 512 if group >= 512 else 256


def small_rows(width, group):
    return 2 * SMALL * (width // small_width(group))


def qkv_grad_kernel(bits, rows, tokens, sums_own, sums_far, up_0, up_1, dq, dk, dv, *refs):
    width = dq.shape[1]
    groups = groups_of(width)
    outs, (small_ref, tok_t, *more) = refs[: 2 * len(groups)], refs[2 * len(groups) :]
    lefts = {bits[0]: tok_t}
    for bit in bits:
        if bit not in lefts:
            lefts[bit] = more[0]
    for bit, ref in lefts.items():
        transpose_halves(tokens, ref, 0, (bit, bit), rows)
    half = tok_t.shape[0] // 2
    small_ref[0:6, :] = sums_own[0:6, :] + sums_far[0:6, :]
    small_ref[6:7, :] = up_0[...] + up_1[...]
    small_ref[7:8, :] = jnp.zeros_like(small_ref[7:8, :])
    small_ref[7:8, :width] = jnp.sum(dq[...].astype(F32), axis=0, keepdims=True)
    small_ref[7:8, width : 2 * width] = jnp.sum(dv[...].astype(F32), axis=0, keepdims=True)
    put_small(outs[1], small_ref[...], half)
    for n, (low, high) in enumerate(groups):
        keep, give, left = outs[2 * n], outs[2 * n + 1], lefts[bits[n]]
        for which, ref in enumerate((dq, dk, dv)):
            first, last = max(low, which * width), min(high, (which + 1) * width)
            if first < last:
                right = ref[:, first - which * width : last - which * width]
                here = slice(first - low, last - low)
                give[:half, here] = dot_nn(left[half:, :], right).astype(BF16)
                keep[:, here] = dot_nn(left[:half, :], right).astype(BF16)


def put_small(give, small, tall):
    width = small_width(give.shape[1])
    give[tall:, :width] = two_digits(small, width)
    if give.shape[1] > width:
        give[tall:, width:] = jnp.zeros((give.shape[0] - tall, give.shape[1] - width), BF16)


def qkv_grad(order, tokens, sums, dq, dk, dv, bits, ctx_count):
    width, cols = tokens.shape[1], dq.shape[1]
    half = width // 2
    outs = []
    for n, (low, high) in enumerate(groups_of(cols)):
        extra = 0 if n else small_rows(width, high - low)
        outs += [((half, high - low), BF16), ((half + extra, high - low), BF16)]
    return call(
        order, "grad_qkv",
        functools.partial(qkv_grad_kernel, bits, width // ctx_count),
        outs + [((SMALL, width), F32)], (tokens, *sums, dq, dk, dv),
        scratch=[pltpu.VMEM(tokens.shape[::-1], BF16)] * len(set(bits)),
    )


def fold_rows(keep, got, bit, rows, keep_ref, give_ref):
    for own, source, target in halves(keep.shape[0], bit, rows):
        total = keep[source, :].astype(F32) + got[source, :].astype(F32)
        (keep_ref if own else give_ref)[target, :] = total.astype(BF16)


def small_sum(small, got, tall):
    width = small_width(got.shape[1])
    own = from_digits(two_digits(small[...], width), width)
    return own + from_digits(got[tall:, :width], width)


def fold_small_kernel(bit, rows, keep, small, got, keep_ref, give_ref, small_ref):
    tall = keep.shape[0]
    fold_rows(keep, got, bit, rows, keep_ref, give_ref)
    value = small_sum(small, got, tall)
    small_ref[...] = value
    put_small(give_ref, value, tall // 2)


def last_small_kernel(small, *refs):
    count = len(CUTS) + 1
    keeps, gots, outs, rows = refs[:count], refs[count : 2 * count], refs[2 * count : 2 * count + 3], refs[2 * count + 3 :]
    tall, width = outs[0].shape
    for n, (low, high) in enumerate(groups_of(width)):
        value = keeps[n][...].astype(F32) + gots[n][:tall, :].astype(F32)
        for which, out in enumerate(outs):
            first, last = max(low, which * width), min(high, (which + 1) * width)
            if first < last:
                out[:, first - which * width : last - which * width] = value[:, first - low : last - low]
    value = small_sum(small, gots[0], tall)
    for n, row in enumerate(rows[:7]):
        row[...] = value[n : n + 1, :]
    for n, row in enumerate(rows[7:]):
        row[...] = value[7:8, n * width : (n + 1) * width]


def fold_kernel(bit, rows, keep, got, keep_ref, give_ref):
    fold_rows(keep, got, bit, rows, keep_ref, give_ref)


def last_kernel(keep, got, out):
    out[...] = keep[...].astype(F32) + got[...].astype(F32)


class ScatterSum:
    def __init__(self, order, name, keep, give, bits, ctx_count, small=None):
        self.order, self.name, self.bits, self.small = order, name, bits, small
        self.left = list(range(ctx_count.bit_length() - 1))
        self.keep, self.give, self.done = keep, give, 0
        self.rows = keep.shape[0] * 2 // ctx_count

    def send(self):
        self.got = swap(self.give, CTX, 1 << self.bits[self.done])
        return self

    def fold(self, waits=()):
        self.left.remove(self.bits[self.done])
        self.done += 1
        tall, width = self.keep.shape
        bit = self.bits[self.done]
        half = ((tall // 2, width), BF16)
        if self.small is not None:
            extra = self.got.shape[0] - tall
            self.keep, self.give, self.small = call(
                self.order, self.name,
                functools.partial(fold_small_kernel, (self.left.index(bit), bit), self.rows),
                [half, ((tall // 2 + extra, width), BF16), (self.small.shape, F32)],
                (self.keep, self.small, self.got), waits=waits,
            )
            return self.send()
        self.keep, self.give = call(
            self.order, self.name,
            functools.partial(fold_kernel, (self.left.index(bit), bit), self.rows),
            [half, half], (self.keep, self.got), waits=waits,
        )
        return self.send()

    def last(self):
        return call(
            self.order, self.name, last_kernel, [(self.keep.shape, F32)], (self.keep, self.got)
        )[0]


def swap(value, axis, mask):
    return lax.ppermute(value, axis, [(i, i ^ mask) for i in range(lax.axis_size(axis))])


def from_left(value, axis):
    return lax.ppermute(value, axis, [(i, i + 1) for i in range(lax.axis_size(axis) - 1)])


def from_right(value, axis):
    return lax.ppermute(value, axis, [(i + 1, i) for i in range(lax.axis_size(axis) - 1)])


def body(
    tokens, flags, w_query, w_key, w_value, w_out, w_up, w_down, bias_query, bias_value, bias_out,
    mid_gain, mid_bias, bias_up, bias_down, end_gain, end_bias, cotangent,
):
    rows, width = tokens.shape
    assert rows == 4 * TILE == 2 * MAXDOC
    ctx_count = lax.axis_size(CTX)
    bits = list(range(ctx_count.bit_length() - 1))
    turned = bits[1:] + bits[:1]
    order = Order()
    biases = [v[None] for v in (bias_out, mid_gain, mid_bias, bias_up, bias_down, end_gain, end_bias)]

    tokens, kv, to_left, to_right, seg, bounds = project_keys(
        order, tokens, w_key, w_value, bias_value[None], flags[None]
    )
    kv_low = from_left(to_right, CTX)
    queries, q_to_left, q_to_right = project_queries(order, tokens, w_query, bias_query[None])
    queries, w_out = lax.optimization_barrier((queries, w_out))
    w_far = swap(w_out, WT, 2)
    order.hold(tokens, kv, queries)
    local_0, shared = attention_local(order, 0, bounds, seg, queries, kv)
    order.hold(*local_0)
    local_1, _ = attention_local(order, 1, bounds, seg, queries, kv, shared)
    kv_low, to_left, *local_1 = lax.optimization_barrier((kv_low, to_left, *local_1))
    kv_high = from_right(to_left, CTX)
    order.hold(*local_1)
    w_diag = swap(w_far, WT, 1)

    att_0, lse_0, (mine, other), held = attention_edge(
        order, 0, bounds, seg, queries, local_0, kv_low, (w_out, w_up, w_down, cotangent, *biases)
    )
    order.free(*local_0)
    w_out, w_up, w_down, cotangent, bias_out, mid_gain, mid_bias, bias_up, bias_down, end_gain, end_bias = held
    w_core = swap(w_out, WT, 1)
    weights = (w_out, w_core, w_far, w_diag)
    order.hold(w_out, w_up, w_down, cotangent, att_0)
    pieces = (att_0, swap(other, WT, 1), swap(mine, WT, 2), swap(other, WT, 3))
    n_0, s_0, lo = mix(order, 0, tokens, pieces, weights, bias_out, mid_gain, mid_bias)
    order.hold(n_0, s_0)
    att_1, lse_1, _, _ = attention_edge(order, 1, bounds, seg, queries, local_1, kv_high)
    order.free(*local_1)
    order.hold(att_1)
    att_1, q_to_left, q_to_right = lax.optimization_barrier((att_1, q_to_left, q_to_right))
    q_low, q_high = from_left(q_to_right, CTX), from_right(q_to_left, CTX)
    att_far = swap(att_1, WT, 2)
    h_0, sl_0, low_0, part, parts = up_down(
        order, 0, (*lo, *swap_pieces(lo)), w_up, w_down, bias_up
    )
    order.hold(h_0, sl_0, low_0)
    picked = call(order, "far", pick_kernel, [((SPLIT, att_1.shape[1]), BF16)] * 4, (att_far,))
    chip_0 = chip_sum(order, "chip", part, parts, (q_low,))
    far_0 = swap(chip_0, WT, 2)
    pieces = (att_1, swap(att_1, WT, 1), att_far, *swap_pieces(picked))
    n_1, s_1, lo = mix(order, 1, tokens, pieces, weights, bias_out, mid_gain, mid_bias)
    h_1, sl_1, low_1, part, parts = up_down(order, 1, lo, w_up, w_down, bias_up)
    order.hold(n_1, s_1, h_1, sl_1, low_1)
    chip_1 = chip_sum(order, "chip", part, parts, (q_high,))
    far_1 = swap(chip_1, WT, 2)
    att, lse, normal, scale = (att_0, att_1), (lse_0, lse_1), (n_0, n_1), (s_0, s_1)
    hidden, slope, low, chip, far = (h_0, h_1), (sl_0, sl_1), (low_0, low_1), (chip_0, chip_1), (far_0, far_1)

    vectors = (mid_gain, mid_bias, bias_down, end_gain, end_bias)
    out, d_second_0, sums, lo = end(order, 0, normal[0], chip[0], far[0], cotangent, vectors, ())
    d_inner_0, up_sums_0, down_0, *part = down_up(order, 0, lo, swap_pieces(lo), w_down, w_up, slope[0])
    order.hold(d_second_0, d_inner_0, down_0)
    d_chip_0 = chip_sum(order, "chip", *part, (far[1],))
    d_far_0 = swap(d_chip_0, WT, 2)
    layer_out, d_second_1, end_sums, lo = end(
        order, 1, normal[1], chip[1], far[1], cotangent, vectors, (out, sums)
    )
    d_inner_1, up_sums_1, down_1, part, parts = down_up(
        order, 1, lo, swap_pieces(lo), w_down, w_up, slope[1]
    )
    order.hold(d_second_1, d_inner_1, down_1)
    order.free(w_up, w_down, *slope, cotangent)
    v = types.SimpleNamespace(d_sum=[], d=[], mixed=[], delta=[], lo=[])
    up_sums = (up_sums_0, up_sums_1)

    def first_1():
        v.d_chip = chip_sum(order, "chip", part, parts)
        v.d_far = swap(v.d_chip, WT, 2)

    def grad_down():
        keep, give = weight_grad(order, "grad_down", (down_0, down_1), hidden, bits[0], ctx_count)
        order.free(*hidden, down_0, down_1)
        v.down = ScatterSum(order, "fold_down", keep, give, bits, ctx_count).send()

    def grad_up():
        keep, give = weight_grad(order, "grad_up", low, (d_inner_0, d_inner_1), turned[0], ctx_count)
        order.free(*low, d_inner_0, d_inner_1)
        v.up = ScatterSum(order, "fold_up", keep, give, turned, ctx_count).send()

    def mid_0():
        d_sum, v.sums, lo = mid(
            order, 0, d_second_0, d_chip_0, d_far_0, normal[0], scale[0], mid_gain, end_sums
        )
        v.d_sum.append(d_sum)
        v.lo.append(lo)
        order.hold(d_sum)
        order.free(d_second_0, normal[0], scale[0])

    def mid_1():
        d_sum, v.sums, lo = mid(
            order, 1, d_second_1, v.d_chip, v.d_far, normal[1], scale[1], mid_gain, v.sums
        )
        v.d_sum.append(d_sum)
        v.lo.append(lo)
        order.hold(d_sum)
        order.free(d_second_1, normal[1], scale[1])

    def d_att_of(j):
        d, mixed, delta = d_att(order, j, v.lo[j], swap_pieces(v.lo[j]), w_out, att[j], lse[j])
        v.d.append(d)
        v.mixed.append(mixed)
        v.delta.append(delta)
        order.hold(d, mixed)
        if j == 0:
            v.d_high = from_right(d, CTX)
        else:
            v.d_low = from_left(d, CTX)

    def back_local():
        v.local = attention_back_local(order, bounds, seg, queries, kv, v.d, lse, v.delta)

    def grad_out():
        keep, give = weight_grad(
            order, "grad_out", v.mixed, att, bits[0], ctx_count, (v.d_low, v.d_high)
        )
        order.free(*v.mixed, *att, w_out)
        v.out = ScatterSum(order, "fold_out", keep, give, bits, ctx_count).send()

    def back_edge():
        v.grads = attention_back_edge(
            order, bounds, seg, queries, kv, v.d, lse, v.delta,
            (kv_low, kv_high), (q_low, q_high), (v.d_low, v.d_high), v.local,
        )
        order.free(queries, kv, *v.d)
        order.hold(*v.grads)

    def grad_qkv():
        sums = (v.sums, swap(v.sums, WT, 1), *up_sums)
        *parts, small = qkv_grad(order, tokens, sums, *v.grads, (bits[0],) * (len(CUTS) + 1), ctx_count)
        order.free(tokens)
        order.hold(*parts[::2])
        v.qkv = [
            ScatterSum(order, "fold_qkv", keep, give, bits, ctx_count, None if n else small).send()
            for n, (keep, give) in enumerate(zip(parts[::2], parts[1::2]))
        ]

    input_weights = (w_query, w_key, w_value)

    def input_other():
        parts = call(
            order, "input", input_other_kernel, [((rows, width), BF16) for rows in INPUT_SPLITS],
            (*input_weights, *v.grads),
        )
        v.input_far = [swap(part, WT, 1) for part in parts]

    def input_mine():
        v.here, v.away = call(
            order, "input", input_mine_kernel, [((TILE, width), F32), ((TILE, width), BF16)],
            (*input_weights, *v.grads, *v.d_sum, *v.input_far),
        )
        order.free(*v.grads, *v.d_sum)
        order.hold(v.here)
        v.arriving = swap(v.away, WT, 2)

    grad_down()
    grad_up()
    mid_0()
    first_1()
    d_att_of(0)
    mid_1()
    d_att_of(1)
    back_local()
    v.up.fold()
    v.down.fold()
    grad_out()
    back_edge()
    grad_qkv()
    v.out.fold()
    v.down.fold()
    input_other()
    v.up.fold()
    input_mine()
    v.qkv[0].fold()
    v.qkv[1].fold()
    v.qkv[0].fold()
    v.out.fold()
    v.qkv[1].fold()
    sums = (v.up, v.down, v.out, *v.qkv)
    while any(part.done < len(bits) - 1 for part in sums):
        for part in sums:
            if part.done < len(bits) - 1:
                part.fold()
    (input_grad,) = call(order, "input", input_sum_kernel, [((TILE, width), F32)], (v.here, v.arriving))
    summed_down, summed_out, summed_up = v.down.last(), v.out.last(), v.up.last()
    piece = (v.qkv[0].keep.shape[0], queries.shape[1])
    wide, narrow = ((1, width), F32), ((1, queries.shape[1]), F32)
    *summed, g_end_gain, g_end_bias, g_down, g_mid_gain, g_mid_bias, g_out, g_up, g_query, g_value = call(
        order, "sum", last_small_kernel, [(piece, F32)] * 3 + [wide] * 7 + [narrow] * 2,
        (v.qkv[0].small, *(part.keep for part in v.qkv), *(part.got for part in v.qkv)),
    )
    vectors = (g_query, g_value, g_out, g_mid_gain, g_mid_bias, g_up, g_down, g_end_gain, g_end_bias)
    return (
        layer_out, input_grad, *summed, summed_out, summed_up, summed_down, *(v.reshape(-1) for v in vectors)
    )


def solution(mesh):
    wt = P(None, WT)
    in_specs = (
        P(CTX, None), P(CTX), wt, wt, wt, wt, wt, wt, P(WT), P(WT),
        P(), P(), P(), P(WT), P(), P(), P(), P(CTX, None),
    )
    rows = P((CTX, WT), None)
    both = P(CTX, WT)
    out_specs = (
        rows, rows, both, both, both, both, both, both, P(WT), P(WT),
        P(), P(), P(), P(WT), P(), P(), P(),
    )
    return jax.shard_map(body, mesh=mesh, in_specs=in_specs, out_specs=out_specs, check_vma=False)
```

```python
import functools
import types

import jax
import jax.numpy as jnp
from jax import lax
from jax.experimental import pallas as pl
from jax.experimental.pallas import tpu as pltpu
from jax.sharding import PartitionSpec as P

HEAD_DIM = 64
MAXDOC = 512
TILE = 256
HALO = MAXDOC // TILE
SCALE = HEAD_DIM ** -0.5
SCORE = SCALE * 1.4426950408889634
NEG = -1e30
F32 = jnp.float32
BF16 = jnp.bfloat16
MIB = 1024 * 1024
EXTRA = 16
CTX, WT = "ctx", "wt"
SPLITS = (96, 80, 80)
LAST_SPLITS = (256,)
INPUT_SPLITS = (128, 128, 128, 128)
CUTS = (512,)
DOWN_TURNED, UP_TURNED, OUT_TURNED, QKV_TURNED = False, True, False, (False, False)


def dot_nt(left, right):
    return lax.dot_general(left, right, (((1,), (1,)), ((), ())), preferred_element_type=F32)


def dot_nn(left, right):
    return lax.dot_general(left, right, (((1,), (0,)), ((), ())), preferred_element_type=F32)


VMEM = pl.BlockSpec(memory_space=pltpu.VMEM)
SMEM = pl.BlockSpec(memory_space=pltpu.SMEM)
HBM = pl.BlockSpec(memory_space=pltpu.HBM)
HBM_OR_VMEM = pl.BlockSpec(memory_space=pl.ANY)


class Order:
    def __init__(self):
        self.last = ()
        self.held = []

    def hold(self, *arrays):
        self.held += arrays

    def free(self, *arrays):
        self.held = [h for h in self.held if not any(h is a for a in arrays)]


def call(order, name, fn, outs, args, scratch=(), specs=None, limit=16, waits=()):
    held = [h for h in order.held if not any(h is a for a in args)]
    tokens = (*order.last, *waits, *held)
    count = len(tokens) + len(args) + len(outs)

    def kernel(*refs):
        refs[count][...] = jnp.zeros((8, 128), F32)
        fn(*refs[len(tokens) : count], *refs[count + 1 :])

    results = pl.pallas_call(
        kernel,
        in_specs=[HBM_OR_VMEM] * len(tokens) + ([VMEM] * len(args) if specs is None else specs),
        out_specs=[o[2] if len(o) > 2 else VMEM for o in outs] + [VMEM],
        out_shape=[jax.ShapeDtypeStruct(o[0], o[1]) for o in outs] + [jax.ShapeDtypeStruct((8, 128), F32)],
        scratch_shapes=list(scratch),
        compiler_params=pltpu.CompilerParams(vmem_limit_bytes=limit * MIB),
        cost_estimate=pl.CostEstimate(flops=1, bytes_accessed=1, transcendentals=0),
        name=name,
    )(*tokens, *args)
    order.last = (results[-1],)
    return results[:-1]


def position():
    slot, ctx = lax.axis_index(WT), lax.axis_index(CTX)
    return slot & 1, slot >> 1, ctx, ctx == lax.axis_size(CTX) - 1


def running_count(marks):
    lane = lax.broadcasted_iota(jnp.int32, marks.shape, 1)
    reach = 1
    while reach < marks.shape[1]:
        marks = marks + jnp.where(lane >= reach, pltpu.roll(marks, reach, 1), 0)
        reach *= 2
    return marks


def keys_kernel(tok_hbm, wk_hbm, wv_hbm, bv_hbm, fl_hbm,
                tok, kv_ref, low_ref, high_ref, seg_ref, bound_sm, wk, wv, bv, fl, sems):
    blocks, width = tok.shape[0] // TILE, wk.shape[1]
    pairs = [(fl_hbm, fl), (bv_hbm, bv), (wk_hbm, wk), (wv_hbm, wv)]
    first = len(pairs)
    pairs += [(tok_hbm.at[b * TILE : (b + 1) * TILE], tok.at[b * TILE : (b + 1) * TILE]) for b in range(blocks)]
    copies = [pltpu.make_async_copy(a, b, sems.at[n]) for n, (a, b) in enumerate(pairs)]
    for copy in copies:
        copy.start()
    copies[0].wait()
    seg = running_count(jnp.broadcast_to(fl[...], (8, fl.shape[1])))[0:1, :]
    seg_ref[...] = seg
    for b in range(blocks):
        bound_sm[2 * b] = jnp.min(seg[:, b * TILE : (b + 1) * TILE])
        bound_sm[2 * b + 1] = jnp.max(seg[:, b * TILE : (b + 1) * TILE])
    for ref, number in (
        (low_ref, seg[:, :MAXDOC]),
        (high_ref, jnp.max(seg) - seg[:, seg.shape[1] - MAXDOC :]),
    ):
        upper = lax.shift_right_logical(number, 8)
        row = lax.broadcasted_iota(jnp.int32, (EXTRA, MAXDOC), 0)
        digits = jnp.where(row == 0, upper, number - upper * 256)
        ref[MAXDOC:, :MAXDOC] = digits.astype(F32).astype(BF16)
    for copy in copies[1:first]:
        copy.wait()
    for b in range(blocks):
        copies[first + b].wait()
        rows = slice(b * TILE, (b + 1) * TILE)
        keys = dot_nn(tok[rows, :], wk[...]).astype(BF16)
        values = (dot_nn(tok[rows, :], wv[...]) + bv[...]).astype(BF16)
        kv_ref[rows, :width] = keys
        kv_ref[rows, width:] = values
        for ref, at in ((low_ref, b), (high_ref, b - blocks + HALO)):
            if 0 <= at < HALO:
                here = slice(at * TILE, (at + 1) * TILE)
                ref[here, :width] = keys
                ref[here, width:] = values


def queries_kernel(tok, wq_hbm, bq_hbm, q_ref, low_ref, high_ref, wq, bq, sems):
    copies = [pltpu.make_async_copy(wq_hbm, wq, sems.at[0]), pltpu.make_async_copy(bq_hbm, bq, sems.at[1])]
    for copy in copies:
        copy.start()
    for copy in copies:
        copy.wait()
    blocks = tok.shape[0] // TILE
    for b in range(blocks):
        rows = slice(b * TILE, (b + 1) * TILE)
        queries = (dot_nn(tok[rows, :], wq[...]) + bq[...]).astype(BF16)
        q_ref[rows, :] = queries
        for ref, at in ((low_ref, b), (high_ref, b - blocks + HALO)):
            if 0 <= at < HALO:
                ref[at * TILE : (at + 1) * TILE, :] = queries


def in_hbm(arrays):
    return [pltpu.with_memory_space_constraint(a, pltpu.HBM) for a in arrays]


def project_keys(order, tokens, w_key, w_value, bias_value, flags):
    rows, width = tokens.shape
    cols = w_key.shape[1]
    edge = ((MAXDOC + EXTRA, 2 * cols), BF16)
    blocks = rows // TILE
    params = (tokens, w_key, w_value, bias_value, flags)
    return call(
        order, "keys", keys_kernel,
        [(tokens.shape, BF16), ((rows, 2 * cols), BF16), edge, edge, ((1, rows), jnp.int32),
         ((2 * blocks,), jnp.int32, SMEM)],
        in_hbm(params),
        scratch=[pltpu.VMEM(p.shape, p.dtype) for p in params[1:]] + [pltpu.SemaphoreType.DMA((4 + blocks,))],
        specs=[HBM] * len(params),
    )


def project_queries(order, tokens, w_query, bias_query):
    rows, cols = tokens.shape[0], w_query.shape[1]
    edge = ((MAXDOC, cols), BF16)
    return call(
        order, "queries", queries_kernel, [((rows, cols), BF16), edge, edge],
        (tokens, *in_hbm((w_query, bias_query))),
        scratch=[pltpu.VMEM(w_query.shape, BF16), pltpu.VMEM(bias_query.shape, F32), pltpu.SemaphoreType.DMA((2,))],
        specs=[VMEM, HBM, HBM],
    )


def rows_of(index):
    if isinstance(index, int):
        return pl.ds(index * TILE, TILE)
    return pl.ds(pl.multiple_of(index * TILE, TILE), TILE)


def meet(first_a, last_a, first_b, last_b):
    return jnp.logical_and(first_a <= last_b, last_a >= first_b)


def blocks_meet(bound_sm, a, b):
    return meet(bound_sm[2 * a], bound_sm[2 * a + 1], bound_sm[2 * b], bound_sm[2 * b + 1])


def seg_column(seg_row, index):
    return jnp.broadcast_to(seg_row[:, rows_of(index)], (128, TILE)).T


def edge_segments(seg_row, ref, left):
    digits = ref[MAXDOC : MAXDOC + EXTRA, :MAXDOC].astype(F32)
    segs = (digits[0:1, :] * 256.0 + digits[1:2, :]).astype(jnp.int32)
    if left:
        segs = -segs
    else:
        segs = segs + jnp.max(seg_row[...]) + jnp.where(position()[3], 1, 0)
    pieces = [segs[:, b * TILE : (b + 1) * TILE] for b in range(HALO)]
    return [(piece, jnp.min(piece), jnp.max(piece)) for piece in pieces]


def allowed_of(column, row):
    return jnp.concatenate([column, column], axis=1) == row


def head_mask(value, head):
    lane = lax.broadcasted_iota(jnp.int32, value.shape, 1)
    mine = (lane < HEAD_DIM) if head % 2 == 0 else (lane >= HEAD_DIM)
    return jnp.where(mine, value, jnp.zeros_like(value))


def pair_cols(head, base=0):
    return slice(base + (head // 2) * 128, base + (head // 2) * 128 + 128)


def head_rows(head):
    return slice(head * HEAD_DIM, (head + 1) * HEAD_DIM)


def forward_tile(heads, first, allowed, keys, values_t, q_ref, m_ref, l_ref, acc_ref):
    scores = [dot_nt(keys(head), head_mask(q_ref[:, pair_cols(head)], head)) for head in range(heads)]
    scores = [jnp.where(allowed, s * SCORE, NEG) for s in scores]
    top = jnp.concatenate([jnp.max(s, axis=0, keepdims=True) for s in scores], axis=0)
    if not first:
        before = m_ref[...]
        top = jnp.maximum(before, top)
        keep = jnp.exp2(before - top)
    weights = [jnp.exp2(s - top[head : head + 1, :]) for head, s in enumerate(scores)]
    total = jnp.concatenate([jnp.sum(p, axis=0, keepdims=True) for p in weights], axis=0)
    parts = [dot_nn(values_t(head_rows(head)), p.astype(BF16)) for head, p in enumerate(weights)]
    if first:
        l_ref[...] = total
    else:
        l_ref[...] = l_ref[...] * keep + total
        parts = [acc_ref[head_rows(h), :] * keep[h : h + 1, :] + part for h, part in enumerate(parts)]
    m_ref[...] = top
    for head, part in enumerate(parts):
        acc_ref[head_rows(head), :] = part


def attn_local_kernel(heads, blocks, chunk, bound_sm, seg_row, q_ref, kv_ref, *refs):
    width = heads * HEAD_DIM
    if chunk:
        vt, seg_col, m_ref, l_ref, acc_ref = refs
    else:
        m_ref, l_ref, acc_ref, vt, seg_col = refs
        vt[...] = kv_ref[:, width:].T
        for b in range(blocks):
            seg_col[b * TILE : (b + 1) * TILE, :] = seg_column(seg_row, b)

    def block(step, carry):
        qb = step + chunk * HALO
        qs, here = rows_of(qb), rows_of(step)
        seg_q = seg_row[:, qs]

        def tile(kb, first):
            ks = rows_of(kb)
            forward_tile(
                heads, first, allowed_of(seg_col[ks, :], seg_q),
                lambda head: kv_ref[ks, pair_cols(head)], lambda hd: vt[hd, ks],
                q_ref.at[qs, :], m_ref.at[:, here], l_ref.at[:, here], acc_ref.at[:, here],
            )

        tile(qb, True)

        def other(i, inner):
            kb = qb + i - HALO
            safe = jnp.clip(kb, 0, blocks - 1)

            @pl.when(jnp.logical_and(jnp.logical_and(kb == safe, i != HALO), blocks_meet(bound_sm, safe, qb)))
            def _():
                tile(safe, False)

            return inner

        lax.fori_loop(0, 2 * HALO + 1, other, 0)
        return carry

    lax.fori_loop(0, HALO, block, 0)


def attention_local(order, chunk, bounds, seg, q, kv, shared=()):
    rows, width = q.shape
    heads, blocks = width // HEAD_DIM, rows // TILE
    stat = ((heads, MAXDOC), F32)
    outs = [stat, stat, ((width, MAXDOC), F32)]
    m, l, acc, *rest = call(
        order, "local",
        functools.partial(attn_local_kernel, heads, blocks, chunk),
        outs if chunk else outs + [((width, rows), BF16), ((rows, 128), jnp.int32)],
        (bounds, seg, q, kv, *shared),
        specs=[SMEM] + [VMEM] * (3 + len(shared)),
    )
    return (m, l, acc), rest


def attn_edge_kernel(
    heads, blocks, base, count,
    bound_sm, seg_row, q_ref, m_in, l_in, acc_in, far_ref, *refs,
):
    sources, (att_ref, lse_ref, mine_ref, other_ref), refs = refs[:count], refs[count : count + 4], refs[count + 4 :]
    held, (m_ref, l_ref, acc_ref, sems) = refs[:count], refs[count:]
    copies = [pltpu.make_async_copy(a, b, sems.at[n]) for n, (a, b) in enumerate(zip(sources, held))]
    for copy in copies:
        copy.start()
    width = heads * HEAD_DIM
    left = base == 0
    edge_segs = edge_segments(seg_row, far_ref, left)
    for step in range(HALO):
        block = step + base
        own = block + HALO
        from_q = slice(block * TILE, (block + 1) * TILE)
        here = slice(step * TILE, (step + 1) * TILE)
        m_ref[...] = m_in[:, here]
        l_ref[...] = l_in[:, here]
        acc_ref[...] = acc_in[:, here]
        seg_q = seg_row[:, from_q]
        for h in range(HALO):
            segs, first, last = edge_segs[h]
            if abs((h if left else h + blocks + HALO) - own) > HALO:
                continue

            @pl.when(meet(first, last, bound_sm[2 * block], bound_sm[2 * block + 1]))
            def _():
                ks = rows_of(h)
                values_t = far_ref[ks, width : 2 * width].T
                forward_tile(
                    heads, False, allowed_of(seg_column(segs, 0), seg_q),
                    lambda head: far_ref[ks, pair_cols(head)], lambda hd: values_t[hd, :],
                    q_ref.at[from_q, :], m_ref, l_ref, acc_ref,
                )

        for head in range(heads):
            row, hd = slice(head, head + 1), head_rows(head)
            total = l_ref[row, :]
            acc_ref[hd, :] = acc_ref[hd, :] * (1.0 / total)
            lse_ref[row, here] = m_ref[row, :] + jnp.log2(total)
        att = acc_ref[...].T.astype(BF16)
        att_ref[here, :] = att

        @pl.when(position()[0] == step)
        def _():
            mine_ref[...] = att

        @pl.when(position()[0] != step)
        def _():
            other_ref[...] = att

    for copy in copies:
        copy.wait()


def attention_edge(order, chunk, bounds, seg, q, local, far, others=()):
    rows, width = q.shape
    heads, blocks = width // HEAD_DIM, rows // TILE
    square = ((TILE, width), BF16)
    att, lse, mine, other, *held = call(
        order, "edge",
        functools.partial(attn_edge_kernel, heads, blocks, chunk * HALO, len(others)),
        [((MAXDOC, width), BF16), ((heads, MAXDOC), F32), square, square]
        + [(p.shape, p.dtype) for p in others],
        (bounds, seg, q, *local, far, *in_hbm(others)),
        scratch=[
            pltpu.VMEM((heads, TILE), F32), pltpu.VMEM((heads, TILE), F32), pltpu.VMEM((width, TILE), F32),
            pltpu.SemaphoreType.DMA((max(1, len(others)),)),
        ],
        specs=[SMEM] + [VMEM] * 6 + [HBM] * len(others),
    )
    return att, lse, (mine, other), held


def per_head_sums(heads, d, a):
    width = heads * HEAD_DIM
    col = lax.broadcasted_iota(jnp.int32, (8, width), 1) // HEAD_DIM
    row = lax.broadcasted_iota(jnp.int32, (8, width), 0)
    return lax.dot_general(
        (col == row).astype(F32), d.astype(F32) * a.astype(F32), (((1,), (1,)), ((), ())),
        preferred_element_type=F32, precision=lax.Precision.HIGHEST,
    )


def backward_tile(heads, allowed, k_of, v_of, kt, q_of, d_of, lse, delta, dq_add, dkv_add):
    each = range(heads)
    scores = [dot_nt(head_mask(k_of(h), h), q_of(h)) for h in each]
    grads = [dot_nt(head_mask(v_of(h), h), d_of(h)) for h in each]
    probs = [jnp.where(allowed, jnp.exp2(s * SCORE - lse[h : h + 1, :]), 0.0) for h, s in enumerate(scores)]
    ds = [(p * (g - delta[h : h + 1, :])).astype(BF16) for h, (p, g) in enumerate(zip(probs, grads))]
    if dkv_add is not None:
        dk = [dot_nn(ds[h], q_of(h)) for h in each]
        dv = [dot_nn(probs[h].astype(BF16), d_of(h)) for h in each]
    if dq_add is not None:
        dq = [dot_nn(kt[head_rows(h), :], ds[h]) for h in each]
    for h in each:
        if dkv_add is not None:
            dkv_add(h, dk[h], dv[h])
        if dq_add is not None:
            dq_add(h, dq[h])


def merge_pairs(heads, acc):
    lane = lax.broadcasted_iota(jnp.int32, (TILE, 128), 1)
    pieces = [jnp.where(lane < HEAD_DIM, acc[h], acc[h + 1]) for h in range(0, heads, 2)]
    return jnp.concatenate(pieces, axis=1)


def back_local_kernel(
    heads, blocks,
    bound_sm, seg_row, q_ref, kv_ref, lse0, lse1, delta0, delta1, d0, d1,
    dqt_ref, dk_ref, dv_ref,
    dx, lx, delta, dk_acc, dv_acc,
):
    width = heads * HEAD_DIM
    for i, (d, lse, own_delta) in enumerate(((d0, lse0, delta0), (d1, lse1, delta1))):
        part = slice(i * MAXDOC, (i + 1) * MAXDOC)
        dx[part, :] = d[:MAXDOC, :]
        lx[:, part] = lse[...]
        delta[:, part] = own_delta[...]
    dqt_ref[...] = jnp.zeros_like(dqt_ref)

    def block(kb, carry):
        dk_acc[...] = jnp.zeros_like(dk_acc)
        dv_acc[...] = jnp.zeros_like(dv_acc)
        ks = rows_of(kb)
        seg_k = seg_column(seg_row, kb)
        kt = kv_ref[ks, :width].T

        def tile(qb):
            qs = rows_of(qb)

            def dq_add(head, value):
                dqt_ref[head_rows(head), qs] += value

            def dkv_add(head, dk, dv):
                dk_acc[head] += dk
                dv_acc[head] += dv

            backward_tile(
                heads, allowed_of(seg_k, seg_row[:, qs]),
                lambda h: kv_ref[ks, pair_cols(h)], lambda h: kv_ref[ks, pair_cols(h, width)], kt,
                lambda h: q_ref[qs, pair_cols(h)], lambda h: dx[qs, pair_cols(h)],
                lx[:, qs], delta[:, qs], dq_add, dkv_add,
            )

        def other(i, inner):
            qb = kb + i - HALO
            safe = jnp.clip(qb, 0, blocks - 1)

            @pl.when(jnp.logical_and(qb == safe, blocks_meet(bound_sm, safe, kb)))
            def _():
                tile(safe)

            return inner

        lax.fori_loop(0, 2 * HALO + 1, other, 0)
        dk_ref[ks, :] = merge_pairs(heads, dk_acc)
        dv_ref[ks, :] = merge_pairs(heads, dv_acc)
        return carry

    lax.fori_loop(0, blocks, block, 0)


def attention_back_local(order, bounds, seg, q, kv, d_parts, lse_parts, delta_parts):
    rows, width = q.shape
    heads, blocks = width // HEAD_DIM, rows // TILE
    out = ((rows, width), F32)
    return call(
        order, "back_local",
        functools.partial(back_local_kernel, heads, blocks),
        [((width, rows), F32), out, out],
        (bounds, seg, q, kv, *lse_parts, *delta_parts, *d_parts),
        scratch=[
            pltpu.VMEM((rows, width), BF16),
            pltpu.VMEM((heads, rows), F32),
            pltpu.VMEM((heads, rows), F32),
            pltpu.VMEM((heads, TILE, 128), F32),
            pltpu.VMEM((heads, TILE, 128), F32),
        ],
        specs=[SMEM] + [VMEM] * 9,
    )


def digits_of(value):
    rows = []
    for _ in range(3):
        part = value.astype(BF16)
        rows += [part.astype(F32)[:, b * TILE : (b + 1) * TILE] for b in range(HALO)]
        value = value - part.astype(F32)
    return jnp.concatenate(rows, axis=0)


def of_digits(heads, rows):
    digits = [rows[n * HALO * heads : (n + 1) * HALO * heads] for n in range(3)]
    total = digits[0] + digits[1] + digits[2]
    return jnp.concatenate([total[b * heads : (b + 1) * heads] for b in range(HALO)], axis=1)


STATS = 48


def back_edge_kernel(
    heads, blocks,
    bound_sm, seg_row, q_ref, kv_ref, lse0, lse1, delta0, delta1, d0, d1,
    kv_low, kv_high, q_low, q_high, dqt_in, dk_in, dv_in, d_low, d_high, *refs,
):
    count = (len(refs) - 8) // 2
    sources, (dq_ref, dk_ref, dv_ref), refs = refs[:count], refs[count : count + 3], refs[count + 3 :]
    copies = [pltpu.make_async_copy(a, b, refs[-1].at[n]) for n, (a, b) in enumerate(zip(sources, refs))]
    dqt, dk_acc, dv_acc, stats = refs[count:-1]
    for copy in copies:
        copy.start()
    width = heads * HEAD_DIM
    edge_segs = edge_segments(seg_row, kv_low, True) + edge_segments(seg_row, kv_high, False)
    low_meets = edge_segs[HALO - 1][2] >= bound_sm[0]
    high_meets = edge_segs[HALO][1] <= bound_sm[2 * blocks - 1]
    for n, (meets, d) in enumerate(((low_meets, d_low), (high_meets, d_high))):

        @pl.when(meets)
        def _():
            rows = d[MAXDOC : MAXDOC + STATS, :].astype(F32)
            stats[n, :heads, :] = of_digits(heads, rows[: STATS // 2])
            stats[n, 8 : 8 + heads, :] = of_digits(heads, rows[STATS // 2 :])

    for step in range(blocks):
        here = slice(step * TILE, (step + 1) * TILE)
        inner = slice((step % HALO) * TILE, (step % HALO + 1) * TILE)
        lse_own, delta_own, d_own = (lse0, delta0, d0) if step < HALO else (lse1, delta1, d1)
        dqt[...] = dqt_in[:, here]
        dk_acc[...] = jnp.zeros_like(dk_acc)
        dv_acc[...] = jnp.zeros_like(dv_acc)

        def dq_add(head, value):
            dqt[head_rows(head), :] += value

        def dkv_add(head, dk, dv):
            dk_acc[head] += dk
            dv_acc[head] += dv

        for h in range(2 * HALO):
            far = h if h < HALO else blocks + h
            if abs(far - step - HALO) > HALO:
                continue
            kv_far, q_far, d_far = (kv_low, q_low, d_low) if h < HALO else (kv_high, q_high, d_high)
            at = slice((h % HALO) * TILE, (h % HALO + 1) * TILE)
            segs, first, last = edge_segs[h]

            @pl.when(meet(first, last, bound_sm[2 * step], bound_sm[2 * step + 1]))
            def _():
                backward_tile(
                    heads, allowed_of(seg_column(segs, 0), seg_row[:, here]),
                    lambda hd: kv_far[at, pair_cols(hd)], lambda hd: kv_far[at, pair_cols(hd, width)],
                    kv_far[at, :width].T,
                    lambda hd: q_ref[here, pair_cols(hd)], lambda hd: d_own[inner, pair_cols(hd)],
                    lse_own[:, inner], delta_own[:, inner], dq_add, None,
                )
                side = h // HALO
                backward_tile(
                    heads, allowed_of(seg_column(seg_row, step), segs),
                    lambda hd: kv_ref[here, pair_cols(hd)], lambda hd: kv_ref[here, pair_cols(hd, width)], None,
                    lambda hd: q_far[at, pair_cols(hd)], lambda hd: d_far[at, pair_cols(hd)],
                    stats[side, :heads, at], stats[side, 8:, at], None, dkv_add,
                )

        dq_ref[here, :] = (dqt[...] * SCALE).T.astype(BF16)
        dk_ref[here, :] = ((dk_in[here, :] + merge_pairs(heads, dk_acc)) * SCALE).astype(BF16)
        dv_ref[here, :] = (dv_in[here, :] + merge_pairs(heads, dv_acc)).astype(BF16)
    for copy in copies:
        copy.wait()


def attention_back_edge(order, bounds, seg, q, kv, d_parts, lse_parts, delta_parts, kv_far, q_far, d_far, local, others):
    rows, width = q.shape
    heads, blocks = width // HEAD_DIM, rows // TILE
    return call(
        order, "back_edge",
        functools.partial(back_edge_kernel, heads, blocks),
        [((rows, width), BF16)] * 3 + [(p.shape, p.dtype) for p in others],
        (bounds, seg, q, kv, *lse_parts, *delta_parts, *d_parts, *kv_far, *q_far, *local, *d_far, *in_hbm(others)),
        scratch=[
            pltpu.VMEM((width, TILE), F32),
            pltpu.VMEM((heads, TILE, 128), F32),
            pltpu.VMEM((heads, TILE, 128), F32),
            pltpu.VMEM((2, 16, MAXDOC), F32),
            pltpu.SemaphoreType.DMA((len(others),)),
        ],
        specs=[SMEM] + [VMEM] * 18 + [HBM] * len(others),
    )


def moments(value):
    average = jnp.mean(value, axis=-1, keepdims=True)
    centred = value - average
    variance = jnp.mean(centred * centred, axis=-1, keepdims=True)
    scale = lax.rsqrt(variance + 1e-12)
    return centred * scale, scale


def norm_back(grad, normal, scale):
    return scale * (
        grad
        - jnp.mean(grad, axis=-1, keepdims=True)
        - normal * jnp.mean(grad * normal, axis=-1, keepdims=True)
    )


def gelu_both(value):
    half = 0.5 * (1.0 + lax.erf(value * 0.7071067811865476))
    slope = half + value * jnp.exp(-0.5 * value * value) * 0.3989422804014327
    return value * half, slope


PARTS = tuple((sum(SPLITS[:n]), rows) for n, rows in enumerate(SPLITS))
PIECES = len(PARTS)


def pieces_of(width):
    return [((count, width), BF16) for _, count in PARTS]


def swap_pieces(pieces):
    return tuple(swap(piece, WT, 1) for piece in pieces)


def gather(rows, refs):
    if len(refs) == 1:
        rows[...] = refs[0][...]
        return
    start = 0
    for ref in refs:
        rows[start : start + ref.shape[0], :] = ref[...]
        start += ref.shape[0]


def scatter(refs, value):
    for (start, count), ref in zip(PARTS, refs):
        ref[...] = value[start : start + count, :].astype(ref.dtype)


def by_pieces(one):
    for i, (start, count) in enumerate(PARTS):
        one(i, slice(start, start + count))


def add_sums(ref, first, rows):
    for i, value in enumerate(rows, first):
        ref[i : i + 1, :] += jnp.sum(value, axis=0, keepdims=True)


SPLIT = 128


def pick_kernel(value, *outs):
    for i, out in enumerate(outs):
        out[...] = value[i * SPLIT : (i + 1) * SPLIT, :]


def mix_kernel(chunk, tok, w_own, w_core, w_far, w_diag, bias, gain, shift, a_own, a_core, a_far, *refs):
    core, side = position()[:2]
    if chunk:
        pieces, (normal_ref, scale_ref, rows_ref, total, a_diag) = refs[:-5], refs[-5:]
        for i, ref in enumerate(pieces):
            a_diag[i * SPLIT : (i + 1) * SPLIT, :] = ref[...]
    else:
        a_diag, normal_ref, scale_ref, *low_refs, total = refs

    for group in range(1 + chunk):
        at = rows_of(core if group == 0 else 1 - core)
        here = slice(group * TILE, (group + 1) * TILE)
        core_part, far_part, diag_part = (ref[at, :] if chunk else ref[...] for ref in (a_core, a_far, a_diag))
        chip = ((a_own[at, :], w_own), (core_part, w_core))
        far = ((far_part, w_far), (diag_part, w_diag))

        def add_up(pairs):
            total[here, :] = dot_nt(pairs[0][0], pairs[0][1][...])
            for left, right in pairs[1:]:
                total[here, :] += dot_nt(left, right[...])

        @pl.when(side == 0)
        def _():
            add_up(chip + far)

        @pl.when(side != 0)
        def _():
            add_up(far + chip)

        first = (2 * chunk + (core if group == 0 else 1 - core)) * TILE
        for i, (start, rows) in enumerate(PARTS):
            piece = slice(group * TILE + start, group * TILE + start + rows)
            there = pl.ds(pl.multiple_of(first + start, 16), rows)
            normal, scale = moments(tok[there, :].astype(F32) + total[piece, :] + bias[...])
            low = (normal * gain[...] + shift[...]).astype(BF16)
            if group == 0:
                normal_ref[piece, :] = normal
                scale_ref[piece, :] = jnp.broadcast_to(scale, (rows, 128))
            if chunk:
                rows_ref[piece, :] = low
            else:
                low_refs[i][...] = low


def mix(order, chunk, tokens, att, weights, bias, gain, shift):
    rows, width = tokens.shape
    cols = weights[0].shape[1]
    tall = (1 + chunk) * TILE
    normal, scale, *low = call(
        order, "mix",
        functools.partial(mix_kernel, chunk),
        [((TILE, width), F32), ((TILE, 128), F32)]
        + ([((2 * TILE, width), BF16)] if chunk else pieces_of(width)),
        (tokens, *weights, bias, gain, shift, *att),
        scratch=[pltpu.VMEM((tall, width), F32)] + ([pltpu.VMEM((2 * TILE, cols), BF16)] if chunk else []),
    )
    return normal, scale, low


STRIP = 256


def strips(width, one):
    def step(i, carry):
        one(i, pl.ds(pl.multiple_of(i * STRIP, STRIP), STRIP))
        return carry

    lax.fori_loop(0, width // STRIP, step, 0)


def up_down_kernel(count, w_up, w_down, bias, *refs):
    given, refs = refs[:count], refs[count:]
    hidden_ref, slope_ref, part_mine = refs[:3]
    if count == 1:
        (rows,), part_refs = given, refs[3:]
    else:
        rows, part_refs = refs[3], refs[4:]
        gather(rows.at[:TILE, :], given[:PIECES])
        gather(rows.at[TILE:, :], given[PIECES:])

    def one(i, cols):
        active, slope = gelu_both(dot_nn(rows[...], w_up[:, cols]) + bias[:, cols])
        hidden_ref[:, cols] = active.astype(BF16)
        slope_ref[:, cols] = slope.astype(BF16)

    strips(w_up.shape[1], one)
    scatter(part_refs, dot_nt(hidden_ref[TILE:, :], w_down[...]))
    part_mine[...] = dot_nt(hidden_ref[:TILE, :], w_down[...])


def up_down(order, chunk, given, w_up, w_down, bias, waits=()):
    width, hidden = w_up.shape
    both = ((2 * TILE, hidden), BF16)
    collected = [] if len(given) == 1 else [((2 * TILE, width), BF16)]
    hidden, slope, part, *parts = call(
        order, "up_down", functools.partial(up_down_kernel, len(given)),
        [both, both, ((TILE, width), F32)] + collected + pieces_of(width),
        (w_up, w_down, bias, *given),
        waits=waits,
    )
    rows = parts.pop(0) if collected else given[0]
    return hidden, slope, rows, part, parts


def down_up_kernel(count, w_down, w_up, slope_ref, *refs):
    given, refs = refs[:count], refs[count:]
    inner_ref, sums, part_mine = refs[:3]
    if count == 1:
        (rows,), part_refs = given, refs[3:]
    else:
        rows, part_refs = refs[3], refs[4:]
        gather(rows.at[:TILE, :], given[:PIECES])
        gather(rows.at[TILE:, :], given[PIECES:])

    def one(i, cols):
        d_inner = (dot_nn(rows[...], w_down[:, cols]) * slope_ref[:, cols].astype(F32)).astype(BF16)
        inner_ref[:, cols] = d_inner
        sums[:, cols] = jnp.sum(d_inner.astype(F32), axis=0, keepdims=True)

    strips(w_down.shape[1], one)
    scatter(part_refs, dot_nt(inner_ref[TILE:, :], w_up[...]))
    part_mine[...] = dot_nt(inner_ref[:TILE, :], w_up[...])


def down_up_rows(order, chunk, rows, w_down, w_up, slope):
    width, hidden = w_up.shape
    inner, sums, part, *parts = call(
        order, "down_up", functools.partial(down_up_kernel, 1),
        [((2 * TILE, hidden), BF16), ((1, hidden), F32), ((TILE, width), F32)] + pieces_of(width),
        (w_down, w_up, slope, rows),
    )
    return inner, sums, part, parts


def down_up(order, chunk, mine, other, w_down, w_up, slope):
    width, hidden = w_up.shape
    inner, sums, part, rows, *parts = call(
        order, "down_up", functools.partial(down_up_kernel, 2 * PIECES),
        [((2 * TILE, hidden), BF16), ((1, hidden), F32), ((TILE, width), F32), ((2 * TILE, width), BF16)]
        + pieces_of(width),
        (w_down, w_up, slope, *mine, *other),
    )
    return inner, sums, rows, part, parts


def chip_sum_kernel(mine, *refs):
    out = refs[-1]
    for i, ref in enumerate(refs[:-1]):
        here = slice(PARTS[i][0], sum(PARTS[i]))
        out[here, :] = (mine[here, :] + ref[...].astype(F32)).astype(BF16)


def chip_sum(order, name, mine, parts, waits=()):
    return call(order, name, chip_sum_kernel, [(mine.shape, BF16)], (mine, *swap_pieces(parts)), waits=waits)[0]


def end_kernel(chunk, normal, chip, cot, mid_gain, mid_bias, bias, gain, shift, *refs):
    before, refs = (refs[:2], refs[2:]) if chunk else ((), refs)
    far, out_ref, d_ref, sums = refs[:4]
    low_refs = refs[4:]
    core, side = position()[:2]
    sums[...] = before[1][...] if before else jnp.zeros_like(sums)
    first = (2 * chunk + core) * TILE

    def one(i, here):
        there = pl.ds(pl.multiple_of(first + PARTS[i][0], 16), PARTS[i][1])
        both = chip[here, :].astype(F32) + far[here, :].astype(F32)
        second = (normal[here, :] * mid_gain[...] + mid_bias[...]) + both + bias[...]
        unit, scale = moments(second)
        value = (unit * gain[...] + shift[...]).astype(BF16)
        if before:
            value = jnp.where(side == chunk, value, before[0][here, :])
        out_ref[here, :] = value
        upstream = cot[there, :].astype(F32)
        d_second = norm_back(upstream * gain[...], unit, scale)
        low = d_second.astype(BF16)
        d_ref[here, :] = d_second
        low_refs[i][...] = low
        add_sums(sums, 0, (upstream * unit, upstream, low.astype(F32)))

    by_pieces(one)


def end(order, chunk, normal, chip, far, cotangent, vectors, before, waits=()):
    rows, width = normal.shape
    out, d, sums, *low = call(
        order, "end",
        functools.partial(end_kernel, chunk),
        [((rows, width), BF16), ((rows, width), F32), ((8, width), F32)] + pieces_of(width),
        (normal, chip, cotangent, *vectors, *before, far),
        waits=waits,
    )
    return out, d, sums, low


def mid_kernel(d_second, chip, normal, scale, gain, before, far, d_ref, sums, *low_refs):
    sums[...] = before[...]

    def one(i, here):
        d_first = d_second[here, :] + (chip[here, :].astype(F32) + far[here, :].astype(F32))
        unit = normal[here, :]
        d_sum = norm_back(d_first * gain[...], unit, scale[here, 0:1])
        low = d_sum.astype(BF16)
        d_ref[here, :] = d_sum
        if len(low_refs) == len(PARTS):
            low_refs[i][...] = low
        else:
            low_refs[0][here, :] = low
        add_sums(sums, 3, (d_first * unit, d_first, low.astype(F32)))

    by_pieces(one)


def mid(order, chunk, d_second, chip, far, normal, scale, gain, before, waits=()):
    rows, width = normal.shape
    d, sums, *low = call(
        order, "mid", mid_kernel,
        [((rows, width), F32), ((8, width), F32)] + ([((rows, width), BF16)] if chunk and LAST_SPLITS == (256,) else pieces_of(width)),
        (d_second, chip, normal, scale, gain, before, far),
        waits=waits,
    )
    return d, sums, low


def d_att_kernel(heads, w_out, att, lse, *refs):
    count = (len(refs) - 3) // 2
    mine, other, (out, rows, delta_ref) = refs[:count], refs[count : 2 * count], refs[2 * count :]
    core = position()[0]
    here = pl.ds(pl.multiple_of(core * TILE, TILE), TILE)
    there = pl.ds(pl.multiple_of((1 - core) * TILE, TILE), TILE)
    gather(rows.at[here, :], mine)
    gather(rows.at[there, :], other)
    d = dot_nn(rows[...], w_out[...]).astype(BF16)
    out[:MAXDOC, :] = d
    delta = per_head_sums(heads, d, att[...])[:heads]
    delta_ref[...] = delta
    out[MAXDOC:, :] = jnp.concatenate([digits_of(lse[...]), digits_of(delta)], axis=0).astype(BF16)


def d_att(order, chunk, mine, other, w_out, att, lse):
    width, cols = w_out.shape
    heads = cols // HEAD_DIM
    return call(
        order, "d_att", functools.partial(d_att_kernel, heads),
        [((MAXDOC + STATS, cols), BF16), ((2 * TILE, width), BF16), ((heads, MAXDOC), F32)],
        (w_out, att, lse, *mine, *other),
    )


def part_of(refs, weights, block):
    rows = pl.ds(pl.multiple_of(block * TILE, TILE), TILE)
    total = None
    for ref, weight in zip(refs, weights):
        part = dot_nt(ref[rows, :], weight[...])
        total = part if total is None else total + part
    return total


def input_other_kernel(wq, wk, wv, dq, dk, dv, *others):
    for j in range(2):
        block = 2 * j + 1 - position()[0]
        part = part_of((dq, dk, dv), (wq, wk, wv), block).astype(BF16)
        each = len(others) // 2
        for n, ref in enumerate(others[j * each : (j + 1) * each] if each else others):
            rows = slice(n * ref.shape[0], (n + 1) * ref.shape[0]) if each else slice(0, TILE)
            (ref if each else ref.at[j * TILE : (j + 1) * TILE, :])[...] = part[rows]


def input_mine_kernel(wq, wk, wv, dq, dk, dv, d0, d1, *refs):
    got, (here, away) = refs[:-2], refs[-2:]
    core, side = position()[:2]

    def chip(j):
        each = len(got) // 2
        if each:
            far = jnp.concatenate([ref[...].astype(F32) for ref in got[j * each : (j + 1) * each]], axis=0)
        else:
            far = got[0][j * TILE : (j + 1) * TILE, :].astype(F32)
        return part_of((dq, dk, dv), (wq, wk, wv), 2 * j + core) + far

    for mine, d in ((0, d0), (1, d1)):

        @pl.when(side == mine)
        def _():
            here[...] = chip(mine) + d[...]

        @pl.when(side != mine)
        def _():
            away[...] = chip(mine).astype(BF16)


def input_sum_kernel(here, got, out):
    out[...] = here[...] + got[...].astype(F32)


def halves(tall, bit, rows):
    size = (1 << bit[0]) * rows
    mine = (position()[2] >> bit[1]) & 1
    for n in range(tall // (2 * size)):
        for own, side in ((True, mine), (False, 1 - mine)):
            yield own, pl.ds(pl.multiple_of((2 * n + side) * size, size), size), slice(n * size, (n + 1) * size)


def transpose_halves(ref, out, at, bit, rows):
    here = slice(at, at + ref.shape[0])
    half = ref.shape[1] // 2
    size = (1 << bit[0]) * rows
    if size % 128:
        split = ref[...].T.reshape(half // size, 2, size, ref.shape[0])
        zero, one = split[:, 0].reshape(half, ref.shape[0]), split[:, 1].reshape(half, ref.shape[0])
        own = ((position()[2] >> bit[1]) & 1) == 0
        out[:half, here] = jnp.where(own, zero, one)
        out[half:, here] = jnp.where(own, one, zero)
        return
    for own, source, target in halves(ref.shape[1], bit, rows):
        first = target.start + (0 if own else half)
        size = target.stop - target.start
        out[first : first + size, here] = ref[:, source].T


def weight_grad_kernel(bit, rows, count, *refs):
    lefts, rights = refs[:count], refs[count : 2 * count]
    keep_ref, give_ref, left_t = refs[2 * count :]
    at = 0
    for ref in lefts:
        transpose_halves(ref, left_t, at, bit, rows)
        at += ref.shape[0]
    half = left_t.shape[0] // 2
    for first in range(0, keep_ref.shape[1], 256):
        cols = slice(first, first + 256)
        for out, side in ((keep_ref, slice(0, half)), (give_ref, slice(half, 2 * half))):
            total, at = None, 0
            for ref in rights:
                part = dot_nn(left_t[side, at : at + ref.shape[0]], ref[:, cols])
                total = part if total is None else total + part
                at += ref.shape[0]
            out[:, cols] = total.astype(BF16)


def weight_grad(order, name, lefts, rights, bit, ctx_count, waits=()):
    width, cols = lefts[0].shape[1], rights[0].shape[1]
    tall = sum(left.shape[0] for left in lefts)
    return call(
        order, name,
        functools.partial(weight_grad_kernel, (bit, bit), width // ctx_count, len(lefts)),
        [((width // 2, cols), BF16)] * 2, (*lefts, *rights),
        scratch=[pltpu.VMEM((width, tall), BF16)],
        waits=waits,
    )


SMALL = 8


def two_digits(small, width):
    flat = [small[:, at : at + width] for at in range(0, small.shape[1], width)]
    value = jnp.concatenate(flat, axis=0)
    upper = value.astype(BF16)
    return jnp.concatenate([upper, (value - upper.astype(F32)).astype(BF16)], axis=0)


def from_digits(rows, width):
    half = rows.shape[0] // 2
    value = rows[:half].astype(F32) + rows[half:].astype(F32)
    return jnp.concatenate([value[at : at + SMALL] for at in range(0, half, SMALL)], axis=1)


def groups_of(width):
    cuts = (0, *CUTS, 3 * width)
    return list(zip(cuts[:-1], cuts[1:]))


def small_width(group):
    return 512 if group >= 512 else 256


def small_rows(width, group):
    return 2 * SMALL * (width // small_width(group))


def qkv_grad_kernel(bits, rows, tokens, sums_own, sums_far, up_0, up_1, dq, dk, dv, *refs):
    width = dq.shape[1]
    groups = groups_of(width)
    outs, (small_ref, tok_t, *more) = refs[: 2 * len(groups)], refs[2 * len(groups) :]
    lefts = {bits[0]: tok_t}
    for bit in bits:
        if bit not in lefts:
            lefts[bit] = more[0]
    for bit, ref in lefts.items():
        transpose_halves(tokens, ref, 0, (bit, bit), rows)
    half = tok_t.shape[0] // 2
    small_ref[0:6, :] = sums_own[0:6, :] + sums_far[0:6, :]
    small_ref[6:7, :] = up_0[...] + up_1[...]
    small_ref[7:8, :] = jnp.zeros_like(small_ref[7:8, :])
    small_ref[7:8, :width] = jnp.sum(dq[...].astype(F32), axis=0, keepdims=True)
    small_ref[7:8, width : 2 * width] = jnp.sum(dv[...].astype(F32), axis=0, keepdims=True)
    put_small(outs[1], small_ref[...], half)
    for n, (low, high) in enumerate(groups):
        keep, give, left = outs[2 * n], outs[2 * n + 1], lefts[bits[n]]
        for which, ref in enumerate((dq, dk, dv)):
            first, last = max(low, which * width), min(high, (which + 1) * width)
            if first < last:
                right = ref[:, first - which * width : last - which * width]
                here = slice(first - low, last - low)
                give[:half, here] = dot_nn(left[half:, :], right).astype(BF16)
                keep[:, here] = dot_nn(left[:half, :], right).astype(BF16)


def put_small(give, small, tall):
    width = small_width(give.shape[1])
    give[tall:, :width] = two_digits(small, width)
    if give.shape[1] > width:
        give[tall:, width:] = jnp.zeros((give.shape[0] - tall, give.shape[1] - width), BF16)


def qkv_grad(order, tokens, sums, dq, dk, dv, bits, ctx_count):
    width, cols = tokens.shape[1], dq.shape[1]
    half = width // 2
    outs = []
    for n, (low, high) in enumerate(groups_of(cols)):
        extra = 0 if n else small_rows(width, high - low)
        outs += [((half, high - low), BF16), ((half + extra, high - low), BF16)]
    return call(
        order, "grad_qkv",
        functools.partial(qkv_grad_kernel, bits, width // ctx_count),
        outs + [((SMALL, width), F32)], (tokens, *sums, dq, dk, dv),
        scratch=[pltpu.VMEM(tokens.shape[::-1], BF16)] * len(set(bits)),
    )


def fold_rows(keep, got, bit, rows, keep_ref, give_ref):
    for own, source, target in halves(keep.shape[0], bit, rows):
        total = keep[source, :].astype(F32) + got[source, :].astype(F32)
        (keep_ref if own else give_ref)[target, :] = total.astype(BF16)


def small_sum(small, got, tall):
    width = small_width(got.shape[1])
    own = from_digits(two_digits(small[...], width), width)
    return own + from_digits(got[tall:, :width], width)


def fold_small_kernel(bit, rows, keep, small, got, keep_ref, give_ref, small_ref):
    tall = keep.shape[0]
    fold_rows(keep, got, bit, rows, keep_ref, give_ref)
    value = small_sum(small, got, tall)
    small_ref[...] = value
    put_small(give_ref, value, tall // 2)


def last_small_kernel(small, *refs):
    count = len(CUTS) + 1
    keeps, gots, outs, rows = refs[:count], refs[count : 2 * count], refs[2 * count : 2 * count + 3], refs[2 * count + 3 :]
    tall, width = outs[0].shape
    for n, (low, high) in enumerate(groups_of(width)):
        value = keeps[n][...].astype(F32) + gots[n][:tall, :].astype(F32)
        for which, out in enumerate(outs):
            first, last = max(low, which * width), min(high, (which + 1) * width)
            if first < last:
                out[:, first - which * width : last - which * width] = value[:, first - low : last - low]
    value = small_sum(small, gots[0], tall)
    for n, row in enumerate(rows[:7]):
        row[...] = value[n : n + 1, :]
    for n, row in enumerate(rows[7:]):
        row[...] = value[7:8, n * width : (n + 1) * width]


def fold_kernel(bit, rows, keep, got, keep_ref, give_ref):
    fold_rows(keep, got, bit, rows, keep_ref, give_ref)


def last_kernel(keep, got, out):
    out[...] = keep[...].astype(F32) + got[...].astype(F32)


class ScatterSum:
    def __init__(self, order, name, keep, give, bits, ctx_count, small=None):
        self.order, self.name, self.bits, self.small = order, name, bits, small
        self.left = list(range(ctx_count.bit_length() - 1))
        self.keep, self.give, self.done = keep, give, 0
        self.rows = keep.shape[0] * 2 // ctx_count

    def send(self):
        self.got = swap(self.give, CTX, 1 << self.bits[self.done])
        return self

    def rest(self):
        while self.done < len(self.bits) - 1:
            self.fold()
        return self

    def fold(self, waits=()):
        self.left.remove(self.bits[self.done])
        self.done += 1
        tall, width = self.keep.shape
        bit = self.bits[self.done]
        half = ((tall // 2, width), BF16)
        if self.small is not None:
            extra = self.got.shape[0] - tall
            self.keep, self.give, self.small = call(
                self.order, self.name,
                functools.partial(fold_small_kernel, (self.left.index(bit), bit), self.rows),
                [half, ((tall // 2 + extra, width), BF16), (self.small.shape, F32)],
                (self.keep, self.small, self.got), waits=waits,
            )
            return self.send()
        self.keep, self.give = call(
            self.order, self.name,
            functools.partial(fold_kernel, (self.left.index(bit), bit), self.rows),
            [half, half], (self.keep, self.got), waits=waits,
        )
        return self.send()

    def last(self):
        return call(
            self.order, self.name, last_kernel, [(self.keep.shape, F32)], (self.keep, self.got)
        )[0]


def swap(value, axis, mask):
    return lax.ppermute(value, axis, [(i, i ^ mask) for i in range(lax.axis_size(axis))])


def from_left(value, axis):
    return lax.ppermute(value, axis, [(i, i + 1) for i in range(lax.axis_size(axis) - 1)])


def from_right(value, axis):
    return lax.ppermute(value, axis, [(i + 1, i) for i in range(lax.axis_size(axis) - 1)])


def body(
    tokens, flags, w_query, w_key, w_value, w_out, w_up, w_down, bias_query, bias_value, bias_out,
    mid_gain, mid_bias, bias_up, bias_down, end_gain, end_bias, cotangent,
):
    rows, width = tokens.shape
    assert rows == 4 * TILE == 2 * MAXDOC
    ctx_count = lax.axis_size(CTX)
    bits = list(range(ctx_count.bit_length() - 1))
    turned = bits[1:] + bits[:1]
    order = Order()
    biases = [v[None] for v in (bias_out, mid_gain, mid_bias, bias_up, bias_down, end_gain, end_bias)]

    tokens, kv, to_left, to_right, seg, bounds = project_keys(
        order, tokens, w_key, w_value, bias_value[None], flags[None]
    )
    kv_low = from_left(to_right, CTX)
    queries, q_to_left, q_to_right = project_queries(order, tokens, w_query, bias_query[None])
    queries, w_out = lax.optimization_barrier((queries, w_out))
    w_far = swap(w_out, WT, 2)
    order.hold(tokens, kv, queries)
    local_0, shared = attention_local(order, 0, bounds, seg, queries, kv)
    order.hold(*local_0)
    local_1, _ = attention_local(order, 1, bounds, seg, queries, kv, shared)
    kv_low, to_left, *local_1 = lax.optimization_barrier((kv_low, to_left, *local_1))
    kv_high = from_right(to_left, CTX)
    order.hold(*local_1)
    w_diag = swap(w_far, WT, 1)

    att_0, lse_0, (mine, other), held = attention_edge(
        order, 0, bounds, seg, queries, local_0, kv_low, (w_out, w_up, w_down, cotangent, *biases)
    )
    order.free(*local_0)
    w_out, w_up, w_down, cotangent, bias_out, mid_gain, mid_bias, bias_up, bias_down, end_gain, end_bias = held
    w_core = swap(w_out, WT, 1)
    weights = (w_out, w_core, w_far, w_diag)
    order.hold(w_out, w_up, w_down, cotangent, att_0)
    pieces = (att_0, swap(other, WT, 1), swap(mine, WT, 2), swap(other, WT, 3))
    n_0, s_0, lo = mix(order, 0, tokens, pieces, weights, bias_out, mid_gain, mid_bias)
    order.hold(n_0, s_0)
    att_1, lse_1, _, _ = attention_edge(order, 1, bounds, seg, queries, local_1, kv_high)
    order.free(*local_1)
    order.hold(att_1)
    att_1, q_to_left, q_to_right = lax.optimization_barrier((att_1, q_to_left, q_to_right))
    q_low, q_high = from_left(q_to_right, CTX), from_right(q_to_left, CTX)
    att_far = swap(att_1, WT, 2)
    h_0, sl_0, low_0, part, parts = up_down(
        order, 0, (*lo, *swap_pieces(lo)), w_up, w_down, bias_up
    )
    order.hold(h_0, sl_0, low_0)
    picked = call(order, "far", pick_kernel, [((SPLIT, att_1.shape[1]), BF16)] * 4, (att_far,))
    chip_0 = chip_sum(order, "chip", part, parts, (q_low,))
    far_0 = swap(chip_0, WT, 2)
    pieces = (att_1, swap(att_1, WT, 1), att_far, *swap_pieces(picked))
    n_1, s_1, lo = mix(order, 1, tokens, pieces, weights, bias_out, mid_gain, mid_bias)
    h_1, sl_1, low_1, part, parts = up_down(order, 1, lo, w_up, w_down, bias_up)
    order.hold(n_1, s_1, h_1, sl_1, low_1)
    chip_1 = chip_sum(order, "chip", part, parts, (q_high,))
    far_1 = swap(chip_1, WT, 2)
    att, lse, normal, scale = (att_0, att_1), (lse_0, lse_1), (n_0, n_1), (s_0, s_1)
    hidden, slope, low, chip, far = (h_0, h_1), (sl_0, sl_1), (low_0, low_1), (chip_0, chip_1), (far_0, far_1)

    vectors = (mid_gain, mid_bias, bias_down, end_gain, end_bias)
    out, d_second_0, sums, lo = end(order, 0, normal[0], chip[0], far[0], cotangent, vectors, ())
    d_inner_0, up_sums_0, down_0, *part = down_up(order, 0, lo, swap_pieces(lo), w_down, w_up, slope[0])
    order.hold(d_second_0, d_inner_0, down_0)
    d_chip_0 = chip_sum(order, "chip", *part, (far[1],))
    d_far_0 = swap(d_chip_0, WT, 2)
    layer_out, d_second_1, end_sums, lo = end(
        order, 1, normal[1], chip[1], far[1], cotangent, vectors, (out, sums)
    )
    d_inner_1, up_sums_1, down_1, part, parts = down_up(
        order, 1, lo, swap_pieces(lo), w_down, w_up, slope[1]
    )
    order.hold(d_second_1, d_inner_1, down_1)
    order.free(w_up, w_down, *slope, cotangent)
    v = types.SimpleNamespace(d_sum=[], d=[], mixed=[], delta=[], lo=[])
    up_sums = (up_sums_0, up_sums_1)

    def first_1():
        v.d_chip = chip_sum(order, "chip", part, parts)
        v.d_far = swap(v.d_chip, WT, 2)

    def grad_down():
        way = turned if DOWN_TURNED else bits
        keep, give = weight_grad(order, "grad_down", (down_0, down_1), hidden, way[0], ctx_count)
        order.free(*hidden, down_0, down_1)
        v.down = ScatterSum(order, "fold_down", keep, give, way, ctx_count).send()

    def grad_up():
        way = turned if UP_TURNED else bits
        keep, give = weight_grad(order, "grad_up", low, (d_inner_0, d_inner_1), way[0], ctx_count)
        order.free(*low, d_inner_0, d_inner_1)
        v.up = ScatterSum(order, "fold_up", keep, give, way, ctx_count).send()

    def mid_0():
        d_sum, v.sums, lo = mid(
            order, 0, d_second_0, d_chip_0, d_far_0, normal[0], scale[0], mid_gain, end_sums
        )
        v.d_sum.append(d_sum)
        v.lo.append(lo)
        order.hold(d_sum)
        order.free(d_second_0, normal[0], scale[0])

    def mid_1():
        d_sum, v.sums, lo = mid(
            order, 1, d_second_1, v.d_chip, v.d_far, normal[1], scale[1], mid_gain, v.sums
        )
        v.d_sum.append(d_sum)
        v.lo.append(lo)
        order.hold(d_sum)
        order.free(d_second_1, normal[1], scale[1])

    def d_att_of(j):
        d, mixed, delta = d_att(order, j, v.lo[j], swap_pieces(v.lo[j]), w_out, att[j], lse[j])
        v.d.append(d)
        v.mixed.append(mixed)
        v.delta.append(delta)
        order.hold(d, mixed)
        if j == 0:
            v.d_high = from_right(d, CTX)
        else:
            v.d_low = from_left(d, CTX)

    def back_local():
        v.local = attention_back_local(order, bounds, seg, queries, kv, v.d, lse, v.delta)

    def grad_out(waits=()):
        way = turned if OUT_TURNED else bits
        keep, give = weight_grad(order, "grad_out", v.mixed, att, way[0], ctx_count, waits)
        order.free(*v.mixed, *att, w_out)
        v.out = ScatterSum(order, "fold_out", keep, give, way, ctx_count).send()

    def back_edge():
        *v.grads, v.wq, v.wk, v.wv = attention_back_edge(
            order, bounds, seg, queries, kv, v.d, lse, v.delta,
            (kv_low, kv_high), (q_low, q_high), (v.d_low, v.d_high), v.local, (w_query, w_key, w_value),
        )
        order.free(queries, kv, *v.d)
        order.hold(*v.grads, v.wq, v.wk, v.wv)

    def grad_qkv():
        sums = (v.sums, swap(v.sums, WT, 1), *up_sums)
        ways = [turned if t else bits for t in QKV_TURNED]
        *parts, small = qkv_grad(order, tokens, sums, *v.grads, tuple(way[0] for way in ways), ctx_count)
        order.free(tokens)
        order.hold(*parts[::2])
        v.qkv = [
            ScatterSum(order, "fold_qkv", keep, give, way, ctx_count, None if n else small).send()
            for n, (keep, give, way) in enumerate(zip(parts[::2], parts[1::2], ways))
        ]

    def input_other():
        parts = call(
            order, "input", input_other_kernel, [((rows, width), BF16) for rows in INPUT_SPLITS],
            (v.wq, v.wk, v.wv, *v.grads),
        )
        v.input_far = [swap(part, WT, 1) for part in parts]

    def input_mine():
        v.here, v.away = call(
            order, "input", input_mine_kernel, [((TILE, width), F32), ((TILE, width), BF16)],
            (v.wq, v.wk, v.wv, *v.grads, *v.d_sum, *v.input_far),
        )
        order.free(*v.grads, v.wq, v.wk, v.wv, *v.d_sum)
        order.hold(v.here)
        v.arriving = swap(v.away, WT, 2)

    def last_down():
        v.summed_down = v.down.rest().last()

    def last_out():
        v.summed_out = v.out.rest().last()

    def last_up():
        v.summed_up = v.up.rest().last()

    def input_last():
        (v.input_grad,) = call(order, "input", input_sum_kernel, [((TILE, width), F32)], (v.here, v.arriving))

    grad_down()
    grad_up()
    mid_0()
    first_1()
    d_att_of(0)
    mid_1()
    d_att_of(1)
    back_local()
    v.up.fold()
    v.down.fold()
    grad_out((v.d_low, v.d_high))
    back_edge()
    grad_qkv()
    v.out.fold()
    v.down.fold()
    input_other()
    v.up.fold()
    input_mine()
    v.out.fold()
    v.qkv[0].fold()
    v.qkv[1].fold()
    last_down()
    v.qkv[0].fold()
    v.qkv[1].fold()
    input_last()
    last_out()
    last_up()
    for part in v.qkv:
        part.rest()
    piece = (v.qkv[0].keep.shape[0], queries.shape[1])
    wide, narrow = ((1, width), F32), ((1, queries.shape[1]), F32)
    *summed, g_end_gain, g_end_bias, g_down, g_mid_gain, g_mid_bias, g_out, g_up, g_query, g_value = call(
        order, "sum", last_small_kernel, [(piece, F32)] * 3 + [wide] * 7 + [narrow] * 2,
        (v.qkv[0].small, *(part.keep for part in v.qkv), *(part.got for part in v.qkv)),
    )
    vectors = (g_query, g_value, g_out, g_mid_gain, g_mid_bias, g_up, g_down, g_end_gain, g_end_bias)
    return (
        layer_out, v.input_grad, *summed, v.summed_out, v.summed_up, v.summed_down, *(v.reshape(-1) for v in vectors)
    )


def solution(mesh):
    wt = P(None, WT)
    in_specs = (
        P(CTX, None), P(CTX), wt, wt, wt, wt, wt, wt, P(WT), P(WT),
        P(), P(), P(), P(WT), P(), P(), P(), P(CTX, None),
    )
    rows = P((CTX, WT), None)
    both = P(CTX, WT)
    out_specs = (
        rows, rows, both, both, both, both, both, both, P(WT), P(WT),
        P(), P(), P(), P(WT), P(), P(), P(),
    )
    return jax.shard_map(body, mesh=mesh, in_specs=in_specs, out_specs=out_specs, check_vma=False)
```

```python
import functools
import types

import jax
import jax.numpy as jnp
from jax import lax
from jax.experimental import pallas as pl
from jax.experimental.pallas import tpu as pltpu
from jax.sharding import PartitionSpec as P

HEAD_DIM = 64
MAXDOC = 512
TILE = 256
HALO = MAXDOC // TILE
SCALE = HEAD_DIM ** -0.5
SCORE = SCALE * 1.4426950408889634
NEG = -1e30
F32 = jnp.float32
BF16 = jnp.bfloat16
MIB = 1024 * 1024
EXTRA = 16
CTX, WT = "ctx", "wt"
SPLITS = (96, 80, 80)
LAST_SPLITS = (256,)
INPUT_SPLITS = (128, 128, 128, 128)
CUTS = (512,)
DOWN_TURNED, UP_TURNED, OUT_TURNED, QKV_TURNED = False, True, False, (False, False)


def dot_nt(left, right):
    return lax.dot_general(left, right, (((1,), (1,)), ((), ())), preferred_element_type=F32)


def dot_nn(left, right):
    return lax.dot_general(left, right, (((1,), (0,)), ((), ())), preferred_element_type=F32)


VMEM = pl.BlockSpec(memory_space=pltpu.VMEM)
SMEM = pl.BlockSpec(memory_space=pltpu.SMEM)
HBM = pl.BlockSpec(memory_space=pltpu.HBM)
HBM_OR_VMEM = pl.BlockSpec(memory_space=pl.ANY)


class Order:
    def __init__(self):
        self.last = ()
        self.held = []

    def hold(self, *arrays):
        self.held += arrays

    def free(self, *arrays):
        self.held = [h for h in self.held if not any(h is a for a in arrays)]


def call(order, name, fn, outs, args, scratch=(), specs=None, limit=16, waits=()):
    held = [h for h in order.held if not any(h is a for a in args)]
    tokens = (*order.last, *waits, *held)
    count = len(tokens) + len(args) + len(outs)

    def kernel(*refs):
        refs[count][...] = jnp.zeros((8, 128), F32)
        fn(*refs[len(tokens) : count], *refs[count + 1 :])

    results = pl.pallas_call(
        kernel,
        in_specs=[HBM_OR_VMEM] * len(tokens) + ([VMEM] * len(args) if specs is None else specs),
        out_specs=[o[2] if len(o) > 2 else VMEM for o in outs] + [VMEM],
        out_shape=[jax.ShapeDtypeStruct(o[0], o[1]) for o in outs] + [jax.ShapeDtypeStruct((8, 128), F32)],
        scratch_shapes=list(scratch),
        compiler_params=pltpu.CompilerParams(vmem_limit_bytes=limit * MIB),
        cost_estimate=pl.CostEstimate(flops=1, bytes_accessed=1, transcendentals=0),
        name=name,
    )(*tokens, *args)
    order.last = (results[-1],)
    return results[:-1]


def position():
    slot, ctx = lax.axis_index(WT), lax.axis_index(CTX)
    return slot & 1, slot >> 1, ctx, ctx == lax.axis_size(CTX) - 1


def running_count(marks):
    lane = lax.broadcasted_iota(jnp.int32, marks.shape, 1)
    reach = 1
    while reach < marks.shape[1]:
        marks = marks + jnp.where(lane >= reach, pltpu.roll(marks, reach, 1), 0)
        reach *= 2
    return marks


def keys_kernel(tok_hbm, wk_hbm, wv_hbm, bv_hbm, fl_hbm,
                tok, kv_ref, low_ref, high_ref, seg_ref, bound_sm, wk, wv, bv, fl, sems):
    blocks, width = tok.shape[0] // TILE, wk.shape[1]
    pairs = [(fl_hbm, fl), (bv_hbm, bv), (wk_hbm, wk), (wv_hbm, wv)]
    first = len(pairs)
    pairs += [(tok_hbm.at[b * TILE : (b + 1) * TILE], tok.at[b * TILE : (b + 1) * TILE]) for b in range(blocks)]
    copies = [pltpu.make_async_copy(a, b, sems.at[n]) for n, (a, b) in enumerate(pairs)]
    for copy in copies:
        copy.start()
    copies[0].wait()
    seg = running_count(jnp.broadcast_to(fl[...], (8, fl.shape[1])))[0:1, :]
    seg_ref[...] = seg
    for b in range(blocks):
        bound_sm[2 * b] = jnp.min(seg[:, b * TILE : (b + 1) * TILE])
        bound_sm[2 * b + 1] = jnp.max(seg[:, b * TILE : (b + 1) * TILE])
    for ref, number in (
        (low_ref, seg[:, :MAXDOC]),
        (high_ref, jnp.max(seg) - seg[:, seg.shape[1] - MAXDOC :]),
    ):
        upper = lax.shift_right_logical(number, 8)
        row = lax.broadcasted_iota(jnp.int32, (EXTRA, MAXDOC), 0)
        digits = jnp.where(row == 0, upper, number - upper * 256)
        ref[MAXDOC:, :MAXDOC] = digits.astype(F32).astype(BF16)
    for copy in copies[1:first]:
        copy.wait()
    for b in range(blocks):
        copies[first + b].wait()
        rows = slice(b * TILE, (b + 1) * TILE)
        keys = dot_nn(tok[rows, :], wk[...]).astype(BF16)
        values = (dot_nn(tok[rows, :], wv[...]) + bv[...]).astype(BF16)
        kv_ref[rows, :width] = keys
        kv_ref[rows, width:] = values
        for ref, at in ((low_ref, b), (high_ref, b - blocks + HALO)):
            if 0 <= at < HALO:
                here = slice(at * TILE, (at + 1) * TILE)
                ref[here, :width] = keys
                ref[here, width:] = values


def queries_kernel(tok, wq_hbm, bq_hbm, q_ref, low_ref, high_ref, wq, bq, sems):
    copies = [pltpu.make_async_copy(wq_hbm, wq, sems.at[0]), pltpu.make_async_copy(bq_hbm, bq, sems.at[1])]
    for copy in copies:
        copy.start()
    for copy in copies:
        copy.wait()
    blocks = tok.shape[0] // TILE
    for b in range(blocks):
        rows = slice(b * TILE, (b + 1) * TILE)
        queries = (dot_nn(tok[rows, :], wq[...]) + bq[...]).astype(BF16)
        q_ref[rows, :] = queries
        for ref, at in ((low_ref, b), (high_ref, b - blocks + HALO)):
            if 0 <= at < HALO:
                ref[at * TILE : (at + 1) * TILE, :] = queries


def in_hbm(arrays):
    return [pltpu.with_memory_space_constraint(a, pltpu.HBM) for a in arrays]


def project_keys(order, tokens, w_key, w_value, bias_value, flags):
    rows, width = tokens.shape
    cols = w_key.shape[1]
    edge = ((MAXDOC + EXTRA, 2 * cols), BF16)
    blocks = rows // TILE
    params = (tokens, w_key, w_value, bias_value, flags)
    return call(
        order, "keys", keys_kernel,
        [(tokens.shape, BF16), ((rows, 2 * cols), BF16), edge, edge, ((1, rows), jnp.int32),
         ((2 * blocks,), jnp.int32, SMEM)],
        in_hbm(params),
        scratch=[pltpu.VMEM(p.shape, p.dtype) for p in params[1:]] + [pltpu.SemaphoreType.DMA((4 + blocks,))],
        specs=[HBM] * len(params),
    )


def project_queries(order, tokens, w_query, bias_query):
    rows, cols = tokens.shape[0], w_query.shape[1]
    edge = ((MAXDOC, cols), BF16)
    return call(
        order, "queries", queries_kernel, [((rows, cols), BF16), edge, edge],
        (tokens, *in_hbm((w_query, bias_query))),
        scratch=[pltpu.VMEM(w_query.shape, BF16), pltpu.VMEM(bias_query.shape, F32), pltpu.SemaphoreType.DMA((2,))],
        specs=[VMEM, HBM, HBM],
    )


def rows_of(index):
    if isinstance(index, int):
        return pl.ds(index * TILE, TILE)
    return pl.ds(pl.multiple_of(index * TILE, TILE), TILE)


def meet(first_a, last_a, first_b, last_b):
    return jnp.logical_and(first_a <= last_b, last_a >= first_b)


def blocks_meet(bound_sm, a, b):
    return meet(bound_sm[2 * a], bound_sm[2 * a + 1], bound_sm[2 * b], bound_sm[2 * b + 1])


def seg_column(seg_row, index):
    return jnp.broadcast_to(seg_row[:, rows_of(index)], (128, TILE)).T


def edge_segments(seg_row, ref, left):
    digits = ref[MAXDOC : MAXDOC + EXTRA, :MAXDOC].astype(F32)
    segs = (digits[0:1, :] * 256.0 + digits[1:2, :]).astype(jnp.int32)
    if left:
        segs = -segs
    else:
        segs = segs + jnp.max(seg_row[...]) + jnp.where(position()[3], 1, 0)
    pieces = [segs[:, b * TILE : (b + 1) * TILE] for b in range(HALO)]
    return [(piece, jnp.min(piece), jnp.max(piece)) for piece in pieces]


def allowed_of(column, row):
    return jnp.concatenate([column, column], axis=1) == row


def head_mask(value, head):
    lane = lax.broadcasted_iota(jnp.int32, value.shape, 1)
    mine = (lane < HEAD_DIM) if head % 2 == 0 else (lane >= HEAD_DIM)
    return jnp.where(mine, value, jnp.zeros_like(value))


def pair_cols(head, base=0):
    return slice(base + (head // 2) * 128, base + (head // 2) * 128 + 128)


def head_rows(head):
    return slice(head * HEAD_DIM, (head + 1) * HEAD_DIM)


def forward_tile(heads, first, allowed, keys, values_t, q_ref, m_ref, l_ref, acc_ref):
    scores = [dot_nt(keys(head), head_mask(q_ref[:, pair_cols(head)], head)) for head in range(heads)]
    scores = [jnp.where(allowed, s * SCORE, NEG) for s in scores]
    top = jnp.concatenate([jnp.max(s, axis=0, keepdims=True) for s in scores], axis=0)
    if not first:
        before = m_ref[...]
        top = jnp.maximum(before, top)
        keep = jnp.exp2(before - top)
    weights = [jnp.exp2(s - top[head : head + 1, :]) for head, s in enumerate(scores)]
    total = jnp.concatenate([jnp.sum(p, axis=0, keepdims=True) for p in weights], axis=0)
    parts = [dot_nn(values_t(head_rows(head)), p.astype(BF16)) for head, p in enumerate(weights)]
    if first:
        l_ref[...] = total
    else:
        l_ref[...] = l_ref[...] * keep + total
        parts = [acc_ref[head_rows(h), :] * keep[h : h + 1, :] + part for h, part in enumerate(parts)]
    m_ref[...] = top
    for head, part in enumerate(parts):
        acc_ref[head_rows(head), :] = part


def attn_local_kernel(heads, blocks, chunk, bound_sm, seg_row, q_ref, kv_ref, *refs):
    width = heads * HEAD_DIM
    if chunk:
        vt, seg_col, m_ref, l_ref, acc_ref = refs
    else:
        m_ref, l_ref, acc_ref, vt, seg_col = refs
        vt[...] = kv_ref[:, width:].T
        for b in range(blocks):
            seg_col[b * TILE : (b + 1) * TILE, :] = seg_column(seg_row, b)

    def block(step, carry):
        qb = step + chunk * HALO
        qs, here = rows_of(qb), rows_of(step)
        seg_q = seg_row[:, qs]

        def tile(kb, first):
            ks = rows_of(kb)
            forward_tile(
                heads, first, allowed_of(seg_col[ks, :], seg_q),
                lambda head: kv_ref[ks, pair_cols(head)], lambda hd: vt[hd, ks],
                q_ref.at[qs, :], m_ref.at[:, here], l_ref.at[:, here], acc_ref.at[:, here],
            )

        tile(qb, True)

        def other(i, inner):
            kb = qb + i - HALO
            safe = jnp.clip(kb, 0, blocks - 1)

            @pl.when(jnp.logical_and(jnp.logical_and(kb == safe, i != HALO), blocks_meet(bound_sm, safe, qb)))
            def _():
                tile(safe, False)

            return inner

        lax.fori_loop(0, 2 * HALO + 1, other, 0)
        return carry

    lax.fori_loop(0, HALO, block, 0)


def attention_local(order, chunk, bounds, seg, q, kv, shared=()):
    rows, width = q.shape
    heads, blocks = width // HEAD_DIM, rows // TILE
    stat = ((heads, MAXDOC), F32)
    outs = [stat, stat, ((width, MAXDOC), F32)]
    m, l, acc, *rest = call(
        order, "local",
        functools.partial(attn_local_kernel, heads, blocks, chunk),
        outs if chunk else outs + [((width, rows), BF16), ((rows, 128), jnp.int32)],
        (bounds, seg, q, kv, *shared),
        specs=[SMEM] + [VMEM] * (3 + len(shared)),
    )
    return (m, l, acc), rest


def attn_edge_kernel(
    heads, blocks, base, count,
    bound_sm, seg_row, q_ref, m_in, l_in, acc_in, far_ref, *refs,
):
    sources, (att_ref, lse_ref, mine_ref, other_ref), refs = refs[:count], refs[count : count + 4], refs[count + 4 :]
    held, (m_ref, l_ref, acc_ref, sems) = refs[:count], refs[count:]
    copies = [pltpu.make_async_copy(a, b, sems.at[n]) for n, (a, b) in enumerate(zip(sources, held))]
    for copy in copies:
        copy.start()
    width = heads * HEAD_DIM
    left = base == 0
    edge_segs = edge_segments(seg_row, far_ref, left)
    for step in range(HALO):
        block = step + base
        own = block + HALO
        from_q = slice(block * TILE, (block + 1) * TILE)
        here = slice(step * TILE, (step + 1) * TILE)
        m_ref[...] = m_in[:, here]
        l_ref[...] = l_in[:, here]
        acc_ref[...] = acc_in[:, here]
        seg_q = seg_row[:, from_q]
        for h in range(HALO):
            segs, first, last = edge_segs[h]
            if abs((h if left else h + blocks + HALO) - own) > HALO:
                continue

            @pl.when(meet(first, last, bound_sm[2 * block], bound_sm[2 * block + 1]))
            def _():
                ks = rows_of(h)
                values_t = far_ref[ks, width : 2 * width].T
                forward_tile(
                    heads, False, allowed_of(seg_column(segs, 0), seg_q),
                    lambda head: far_ref[ks, pair_cols(head)], lambda hd: values_t[hd, :],
                    q_ref.at[from_q, :], m_ref, l_ref, acc_ref,
                )

        for head in range(heads):
            row, hd = slice(head, head + 1), head_rows(head)
            total = l_ref[row, :]
            acc_ref[hd, :] = acc_ref[hd, :] * (1.0 / total)
            lse_ref[row, here] = m_ref[row, :] + jnp.log2(total)
        att = acc_ref[...].T.astype(BF16)
        att_ref[here, :] = att

        @pl.when(position()[0] == step)
        def _():
            mine_ref[...] = att

        @pl.when(position()[0] != step)
        def _():
            other_ref[...] = att

    for copy in copies:
        copy.wait()


def attention_edge(order, chunk, bounds, seg, q, local, far, others=()):
    rows, width = q.shape
    heads, blocks = width // HEAD_DIM, rows // TILE
    square = ((TILE, width), BF16)
    att, lse, mine, other, *held = call(
        order, "edge",
        functools.partial(attn_edge_kernel, heads, blocks, chunk * HALO, len(others)),
        [((MAXDOC, width), BF16), ((heads, MAXDOC), F32), square, square]
        + [(p.shape, p.dtype) for p in others],
        (bounds, seg, q, *local, far, *in_hbm(others)),
        scratch=[
            pltpu.VMEM((heads, TILE), F32), pltpu.VMEM((heads, TILE), F32), pltpu.VMEM((width, TILE), F32),
            pltpu.SemaphoreType.DMA((max(1, len(others)),)),
        ],
        specs=[SMEM] + [VMEM] * 6 + [HBM] * len(others),
    )
    return att, lse, (mine, other), held


def per_head_sums(heads, d, a):
    width = heads * HEAD_DIM
    col = lax.broadcasted_iota(jnp.int32, (8, width), 1) // HEAD_DIM
    row = lax.broadcasted_iota(jnp.int32, (8, width), 0)
    return lax.dot_general(
        (col == row).astype(F32), d.astype(F32) * a.astype(F32), (((1,), (1,)), ((), ())),
        preferred_element_type=F32, precision=lax.Precision.HIGHEST,
    )


def backward_tile(heads, allowed, k_of, v_of, kt, q_of, d_of, lse, delta, dq_add, dkv_add):
    each = range(heads)
    scores = [dot_nt(head_mask(k_of(h), h), q_of(h)) for h in each]
    grads = [dot_nt(head_mask(v_of(h), h), d_of(h)) for h in each]
    probs = [jnp.where(allowed, jnp.exp2(s * SCORE - lse[h : h + 1, :]), 0.0) for h, s in enumerate(scores)]
    ds = [(p * (g - delta[h : h + 1, :])).astype(BF16) for h, (p, g) in enumerate(zip(probs, grads))]
    if dkv_add is not None:
        dk = [dot_nn(ds[h], q_of(h)) for h in each]
        dv = [dot_nn(probs[h].astype(BF16), d_of(h)) for h in each]
    if dq_add is not None:
        dq = [dot_nn(kt[head_rows(h), :], ds[h]) for h in each]
    for h in each:
        if dkv_add is not None:
            dkv_add(h, dk[h], dv[h])
        if dq_add is not None:
            dq_add(h, dq[h])


def merge_pairs(heads, acc):
    lane = lax.broadcasted_iota(jnp.int32, (TILE, 128), 1)
    pieces = [jnp.where(lane < HEAD_DIM, acc[h], acc[h + 1]) for h in range(0, heads, 2)]
    return jnp.concatenate(pieces, axis=1)


def back_local_kernel(
    heads, blocks,
    bound_sm, seg_row, q_ref, kv_ref, lse0, lse1, delta0, delta1, d0, d1,
    dqt_ref, dk_ref, dv_ref,
    dx, lx, delta, dk_acc, dv_acc,
):
    width = heads * HEAD_DIM
    for i, (d, lse, own_delta) in enumerate(((d0, lse0, delta0), (d1, lse1, delta1))):
        part = slice(i * MAXDOC, (i + 1) * MAXDOC)
        dx[part, :] = d[:MAXDOC, :]
        lx[:, part] = lse[...]
        delta[:, part] = own_delta[...]
    dqt_ref[...] = jnp.zeros_like(dqt_ref)

    def block(kb, carry):
        dk_acc[...] = jnp.zeros_like(dk_acc)
        dv_acc[...] = jnp.zeros_like(dv_acc)
        ks = rows_of(kb)
        seg_k = seg_column(seg_row, kb)
        kt = kv_ref[ks, :width].T

        def tile(qb):
            qs = rows_of(qb)

            def dq_add(head, value):
                dqt_ref[head_rows(head), qs] += value

            def dkv_add(head, dk, dv):
                dk_acc[head] += dk
                dv_acc[head] += dv

            backward_tile(
                heads, allowed_of(seg_k, seg_row[:, qs]),
                lambda h: kv_ref[ks, pair_cols(h)], lambda h: kv_ref[ks, pair_cols(h, width)], kt,
                lambda h: q_ref[qs, pair_cols(h)], lambda h: dx[qs, pair_cols(h)],
                lx[:, qs], delta[:, qs], dq_add, dkv_add,
            )

        def other(i, inner):
            qb = kb + i - HALO
            safe = jnp.clip(qb, 0, blocks - 1)

            @pl.when(jnp.logical_and(qb == safe, blocks_meet(bound_sm, safe, kb)))
            def _():
                tile(safe)

            return inner

        lax.fori_loop(0, 2 * HALO + 1, other, 0)
        dk_ref[ks, :] = merge_pairs(heads, dk_acc)
        dv_ref[ks, :] = merge_pairs(heads, dv_acc)
        return carry

    lax.fori_loop(0, blocks, block, 0)


def attention_back_local(order, bounds, seg, q, kv, d_parts, lse_parts, delta_parts):
    rows, width = q.shape
    heads, blocks = width // HEAD_DIM, rows // TILE
    out = ((rows, width), F32)
    return call(
        order, "back_local",
        functools.partial(back_local_kernel, heads, blocks),
        [((width, rows), F32), out, out],
        (bounds, seg, q, kv, *lse_parts, *delta_parts, *d_parts),
        scratch=[
            pltpu.VMEM((rows, width), BF16),
            pltpu.VMEM((heads, rows), F32),
            pltpu.VMEM((heads, rows), F32),
            pltpu.VMEM((heads, TILE, 128), F32),
            pltpu.VMEM((heads, TILE, 128), F32),
        ],
        specs=[SMEM] + [VMEM] * 9,
    )


def digits_of(value):
    rows = []
    for _ in range(3):
        part = value.astype(BF16)
        rows += [part.astype(F32)[:, b * TILE : (b + 1) * TILE] for b in range(HALO)]
        value = value - part.astype(F32)
    return jnp.concatenate(rows, axis=0)


def of_digits(heads, rows):
    digits = [rows[n * HALO * heads : (n + 1) * HALO * heads] for n in range(3)]
    total = digits[0] + digits[1] + digits[2]
    return jnp.concatenate([total[b * heads : (b + 1) * heads] for b in range(HALO)], axis=1)


STATS = 48


def back_edge_kernel(
    heads, blocks,
    bound_sm, seg_row, q_ref, kv_ref, lse0, lse1, delta0, delta1, d0, d1,
    kv_low, kv_high, q_low, q_high, dqt_in, dk_in, dv_in, d_low, d_high, *refs,
):
    count = (len(refs) - 8) // 2
    sources, (dq_ref, dk_ref, dv_ref), refs = refs[:count], refs[count : count + 3], refs[count + 3 :]
    copies = [pltpu.make_async_copy(a, b, refs[-1].at[n]) for n, (a, b) in enumerate(zip(sources, refs))]
    dqt, dk_acc, dv_acc, stats = refs[count:-1]
    for copy in copies:
        copy.start()
    width = heads * HEAD_DIM
    edge_segs = edge_segments(seg_row, kv_low, True) + edge_segments(seg_row, kv_high, False)
    low_meets = edge_segs[HALO - 1][2] >= bound_sm[0]
    high_meets = edge_segs[HALO][1] <= bound_sm[2 * blocks - 1]
    for n, (meets, d) in enumerate(((low_meets, d_low), (high_meets, d_high))):

        @pl.when(meets)
        def _():
            rows = d[MAXDOC : MAXDOC + STATS, :].astype(F32)
            stats[n, :heads, :] = of_digits(heads, rows[: STATS // 2])
            stats[n, 8 : 8 + heads, :] = of_digits(heads, rows[STATS // 2 :])

    for step in range(blocks):
        here = slice(step * TILE, (step + 1) * TILE)
        inner = slice((step % HALO) * TILE, (step % HALO + 1) * TILE)
        lse_own, delta_own, d_own = (lse0, delta0, d0) if step < HALO else (lse1, delta1, d1)
        dqt[...] = dqt_in[:, here]
        dk_acc[...] = jnp.zeros_like(dk_acc)
        dv_acc[...] = jnp.zeros_like(dv_acc)

        def dq_add(head, value):
            dqt[head_rows(head), :] += value

        def dkv_add(head, dk, dv):
            dk_acc[head] += dk
            dv_acc[head] += dv

        for h in range(2 * HALO):
            far = h if h < HALO else blocks + h
            if abs(far - step - HALO) > HALO:
                continue
            kv_far, q_far, d_far = (kv_low, q_low, d_low) if h < HALO else (kv_high, q_high, d_high)
            at = slice((h % HALO) * TILE, (h % HALO + 1) * TILE)
            segs, first, last = edge_segs[h]

            @pl.when(meet(first, last, bound_sm[2 * step], bound_sm[2 * step + 1]))
            def _():
                backward_tile(
                    heads, allowed_of(seg_column(segs, 0), seg_row[:, here]),
                    lambda hd: kv_far[at, pair_cols(hd)], lambda hd: kv_far[at, pair_cols(hd, width)],
                    kv_far[at, :width].T,
                    lambda hd: q_ref[here, pair_cols(hd)], lambda hd: d_own[inner, pair_cols(hd)],
                    lse_own[:, inner], delta_own[:, inner], dq_add, None,
                )
                side = h // HALO
                backward_tile(
                    heads, allowed_of(seg_column(seg_row, step), segs),
                    lambda hd: kv_ref[here, pair_cols(hd)], lambda hd: kv_ref[here, pair_cols(hd, width)], None,
                    lambda hd: q_far[at, pair_cols(hd)], lambda hd: d_far[at, pair_cols(hd)],
                    stats[side, :heads, at], stats[side, 8:, at], None, dkv_add,
                )

        dq_ref[here, :] = (dqt[...] * SCALE).T.astype(BF16)
        dk_ref[here, :] = ((dk_in[here, :] + merge_pairs(heads, dk_acc)) * SCALE).astype(BF16)
        dv_ref[here, :] = (dv_in[here, :] + merge_pairs(heads, dv_acc)).astype(BF16)
    for copy in copies:
        copy.wait()


def attention_back_edge(order, bounds, seg, q, kv, d_parts, lse_parts, delta_parts, kv_far, q_far, d_far, local, others):
    rows, width = q.shape
    heads, blocks = width // HEAD_DIM, rows // TILE
    return call(
        order, "back_edge",
        functools.partial(back_edge_kernel, heads, blocks),
        [((rows, width), BF16)] * 3 + [(p.shape, p.dtype) for p in others],
        (bounds, seg, q, kv, *lse_parts, *delta_parts, *d_parts, *kv_far, *q_far, *local, *d_far, *in_hbm(others)),
        scratch=[
            pltpu.VMEM((width, TILE), F32),
            pltpu.VMEM((heads, TILE, 128), F32),
            pltpu.VMEM((heads, TILE, 128), F32),
            pltpu.VMEM((2, 16, MAXDOC), F32),
            pltpu.SemaphoreType.DMA((len(others),)),
        ],
        specs=[SMEM] + [VMEM] * 18 + [HBM] * len(others),
    )


def moments(value):
    average = jnp.mean(value, axis=-1, keepdims=True)
    centred = value - average
    variance = jnp.mean(centred * centred, axis=-1, keepdims=True)
    scale = lax.rsqrt(variance + 1e-12)
    return centred * scale, scale


def norm_back(grad, normal, scale):
    return scale * (
        grad
        - jnp.mean(grad, axis=-1, keepdims=True)
        - normal * jnp.mean(grad * normal, axis=-1, keepdims=True)
    )


def gelu_both(value):
    half = 0.5 * (1.0 + lax.erf(value * 0.7071067811865476))
    slope = half + value * jnp.exp(-0.5 * value * value) * 0.3989422804014327
    return value * half, slope


PARTS = tuple((sum(SPLITS[:n]), rows) for n, rows in enumerate(SPLITS))
PIECES = len(PARTS)


def pieces_of(width):
    return [((count, width), BF16) for _, count in PARTS]


def swap_pieces(pieces):
    return tuple(swap(piece, WT, 1) for piece in pieces)


def gather(rows, refs):
    if len(refs) == 1:
        rows[...] = refs[0][...]
        return
    start = 0
    for ref in refs:
        rows[start : start + ref.shape[0], :] = ref[...]
        start += ref.shape[0]


def scatter(refs, value):
    for (start, count), ref in zip(PARTS, refs):
        ref[...] = value[start : start + count, :].astype(ref.dtype)


def by_pieces(one):
    for i, (start, count) in enumerate(PARTS):
        one(i, slice(start, start + count))


def add_sums(ref, first, rows):
    for i, value in enumerate(rows, first):
        ref[i : i + 1, :] += jnp.sum(value, axis=0, keepdims=True)


SPLIT = 128


def pick_kernel(value, *outs):
    for i, out in enumerate(outs):
        out[...] = value[i * SPLIT : (i + 1) * SPLIT, :]


def mix_kernel(chunk, tok, w_own, w_core, w_far, w_diag, bias, gain, shift, a_own, a_core, a_far, *refs):
    core, side = position()[:2]
    if chunk:
        pieces, (normal_ref, scale_ref, rows_ref, total, a_diag) = refs[:-5], refs[-5:]
        for i, ref in enumerate(pieces):
            a_diag[i * SPLIT : (i + 1) * SPLIT, :] = ref[...]
    else:
        a_diag, normal_ref, scale_ref, *low_refs, total = refs

    for group in range(1 + chunk):
        at = rows_of(core if group == 0 else 1 - core)
        here = slice(group * TILE, (group + 1) * TILE)
        core_part, far_part, diag_part = (ref[at, :] if chunk else ref[...] for ref in (a_core, a_far, a_diag))
        chip = ((a_own[at, :], w_own), (core_part, w_core))
        far = ((far_part, w_far), (diag_part, w_diag))

        def add_up(pairs):
            total[here, :] = dot_nt(pairs[0][0], pairs[0][1][...])
            for left, right in pairs[1:]:
                total[here, :] += dot_nt(left, right[...])

        @pl.when(side == 0)
        def _():
            add_up(chip + far)

        @pl.when(side != 0)
        def _():
            add_up(far + chip)

        first = (2 * chunk + (core if group == 0 else 1 - core)) * TILE
        for i, (start, rows) in enumerate(PARTS):
            piece = slice(group * TILE + start, group * TILE + start + rows)
            there = pl.ds(pl.multiple_of(first + start, 16), rows)
            normal, scale = moments(tok[there, :].astype(F32) + total[piece, :] + bias[...])
            low = (normal * gain[...] + shift[...]).astype(BF16)
            if group == 0:
                normal_ref[piece, :] = normal
                scale_ref[piece, :] = jnp.broadcast_to(scale, (rows, 128))
            if chunk:
                rows_ref[piece, :] = low
            else:
                low_refs[i][...] = low


def mix(order, chunk, tokens, att, weights, bias, gain, shift):
    rows, width = tokens.shape
    cols = weights[0].shape[1]
    tall = (1 + chunk) * TILE
    normal, scale, *low = call(
        order, "mix",
        functools.partial(mix_kernel, chunk),
        [((TILE, width), F32), ((TILE, 128), F32)]
        + ([((2 * TILE, width), BF16)] if chunk else pieces_of(width)),
        (tokens, *weights, bias, gain, shift, *att),
        scratch=[pltpu.VMEM((tall, width), F32)] + ([pltpu.VMEM((2 * TILE, cols), BF16)] if chunk else []),
    )
    return normal, scale, low


STRIP = 256


def strips(width, one):
    def step(i, carry):
        one(i, pl.ds(pl.multiple_of(i * STRIP, STRIP), STRIP))
        return carry

    lax.fori_loop(0, width // STRIP, step, 0)


def up_down_kernel(count, w_up, w_down, bias, *refs):
    given, refs = refs[:count], refs[count:]
    hidden_ref, slope_ref, part_mine = refs[:3]
    if count == 1:
        (rows,), part_refs = given, refs[3:]
    else:
        rows, part_refs = refs[3], refs[4:]
        gather(rows.at[:TILE, :], given[:PIECES])
        gather(rows.at[TILE:, :], given[PIECES:])

    def one(i, cols):
        active, slope = gelu_both(dot_nn(rows[...], w_up[:, cols]) + bias[:, cols])
        hidden_ref[:, cols] = active.astype(BF16)
        slope_ref[:, cols] = slope.astype(BF16)

    strips(w_up.shape[1], one)
    scatter(part_refs, dot_nt(hidden_ref[TILE:, :], w_down[...]))
    part_mine[...] = dot_nt(hidden_ref[:TILE, :], w_down[...])


def up_down(order, chunk, given, w_up, w_down, bias, waits=()):
    width, hidden = w_up.shape
    both = ((2 * TILE, hidden), BF16)
    collected = [] if len(given) == 1 else [((2 * TILE, width), BF16)]
    hidden, slope, part, *parts = call(
        order, "up_down", functools.partial(up_down_kernel, len(given)),
        [both, both, ((TILE, width), F32)] + collected + pieces_of(width),
        (w_up, w_down, bias, *given),
        waits=waits,
    )
    rows = parts.pop(0) if collected else given[0]
    return hidden, slope, rows, part, parts


def down_up_kernel(count, w_down, w_up, slope_ref, *refs):
    given, refs = refs[:count], refs[count:]
    inner_ref, sums, part_mine = refs[:3]
    if count == 1:
        (rows,), part_refs = given, refs[3:]
    else:
        rows, part_refs = refs[3], refs[4:]
        gather(rows.at[:TILE, :], given[:PIECES])
        gather(rows.at[TILE:, :], given[PIECES:])

    def one(i, cols):
        d_inner = (dot_nn(rows[...], w_down[:, cols]) * slope_ref[:, cols].astype(F32)).astype(BF16)
        inner_ref[:, cols] = d_inner
        sums[:, cols] = jnp.sum(d_inner.astype(F32), axis=0, keepdims=True)

    strips(w_down.shape[1], one)
    scatter(part_refs, dot_nt(inner_ref[TILE:, :], w_up[...]))
    part_mine[...] = dot_nt(inner_ref[:TILE, :], w_up[...])


def down_up_rows(order, chunk, rows, w_down, w_up, slope):
    width, hidden = w_up.shape
    inner, sums, part, *parts = call(
        order, "down_up", functools.partial(down_up_kernel, 1),
        [((2 * TILE, hidden), BF16), ((1, hidden), F32), ((TILE, width), F32)] + pieces_of(width),
        (w_down, w_up, slope, rows),
    )
    return inner, sums, part, parts


def down_up(order, chunk, mine, other, w_down, w_up, slope):
    width, hidden = w_up.shape
    inner, sums, part, rows, *parts = call(
        order, "down_up", functools.partial(down_up_kernel, 2 * PIECES),
        [((2 * TILE, hidden), BF16), ((1, hidden), F32), ((TILE, width), F32), ((2 * TILE, width), BF16)]
        + pieces_of(width),
        (w_down, w_up, slope, *mine, *other),
    )
    return inner, sums, rows, part, parts


def chip_sum_kernel(mine, *refs):
    out = refs[-1]
    for i, ref in enumerate(refs[:-1]):
        here = slice(PARTS[i][0], sum(PARTS[i]))
        out[here, :] = (mine[here, :] + ref[...].astype(F32)).astype(BF16)


def chip_sum(order, name, mine, parts, waits=()):
    return call(order, name, chip_sum_kernel, [(mine.shape, BF16)], (mine, *swap_pieces(parts)), waits=waits)[0]


def end_kernel(chunk, normal, chip, cot, mid_gain, mid_bias, bias, gain, shift, *refs):
    before, refs = (refs[:2], refs[2:]) if chunk else ((), refs)
    far, out_ref, d_ref, sums = refs[:4]
    low_refs = refs[4:]
    core, side = position()[:2]
    sums[...] = before[1][...] if before else jnp.zeros_like(sums)
    first = (2 * chunk + core) * TILE

    def one(i, here):
        there = pl.ds(pl.multiple_of(first + PARTS[i][0], 16), PARTS[i][1])
        both = chip[here, :].astype(F32) + far[here, :].astype(F32)
        second = (normal[here, :] * mid_gain[...] + mid_bias[...]) + both + bias[...]
        unit, scale = moments(second)
        value = (unit * gain[...] + shift[...]).astype(BF16)
        if before:
            value = jnp.where(side == chunk, value, before[0][here, :])
        out_ref[here, :] = value
        upstream = cot[there, :].astype(F32)
        d_second = norm_back(upstream * gain[...], unit, scale)
        low = d_second.astype(BF16)
        d_ref[here, :] = d_second
        low_refs[i][...] = low
        add_sums(sums, 0, (upstream * unit, upstream, low.astype(F32)))

    by_pieces(one)


def end(order, chunk, normal, chip, far, cotangent, vectors, before, waits=()):
    rows, width = normal.shape
    out, d, sums, *low = call(
        order, "end",
        functools.partial(end_kernel, chunk),
        [((rows, width), BF16), ((rows, width), F32), ((8, width), F32)] + pieces_of(width),
        (normal, chip, cotangent, *vectors, *before, far),
        waits=waits,
    )
    return out, d, sums, low


def mid_kernel(d_second, chip, normal, scale, gain, before, far, d_ref, sums, *low_refs):
    sums[...] = before[...]

    def one(i, here):
        d_first = d_second[here, :] + (chip[here, :].astype(F32) + far[here, :].astype(F32))
        unit = normal[here, :]
        d_sum = norm_back(d_first * gain[...], unit, scale[here, 0:1])
        low = d_sum.astype(BF16)
        d_ref[here, :] = d_sum
        if len(low_refs) == len(PARTS):
            low_refs[i][...] = low
        else:
            low_refs[0][here, :] = low
        add_sums(sums, 3, (d_first * unit, d_first, low.astype(F32)))

    by_pieces(one)


def mid(order, chunk, d_second, chip, far, normal, scale, gain, before, waits=()):
    rows, width = normal.shape
    d, sums, *low = call(
        order, "mid", mid_kernel,
        [((rows, width), F32), ((8, width), F32)] + ([((rows, width), BF16)] if chunk and LAST_SPLITS == (256,) else pieces_of(width)),
        (d_second, chip, normal, scale, gain, before, far),
        waits=waits,
    )
    return d, sums, low


def d_att_kernel(heads, w_out, att, lse, *refs):
    count = (len(refs) - 3) // 2
    mine, other, (out, rows, delta_ref) = refs[:count], refs[count : 2 * count], refs[2 * count :]
    core = position()[0]
    here = pl.ds(pl.multiple_of(core * TILE, TILE), TILE)
    there = pl.ds(pl.multiple_of((1 - core) * TILE, TILE), TILE)
    gather(rows.at[here, :], mine)
    gather(rows.at[there, :], other)
    d = dot_nn(rows[...], w_out[...]).astype(BF16)
    out[:MAXDOC, :] = d
    delta = per_head_sums(heads, d, att[...])[:heads]
    delta_ref[...] = delta
    out[MAXDOC:, :] = jnp.concatenate([digits_of(lse[...]), digits_of(delta)], axis=0).astype(BF16)


def d_att(order, chunk, mine, other, w_out, att, lse):
    width, cols = w_out.shape
    heads = cols // HEAD_DIM
    return call(
        order, "d_att", functools.partial(d_att_kernel, heads),
        [((MAXDOC + STATS, cols), BF16), ((2 * TILE, width), BF16), ((heads, MAXDOC), F32)],
        (w_out, att, lse, *mine, *other),
    )


def part_of(refs, weights, block):
    rows = pl.ds(pl.multiple_of(block * TILE, TILE), TILE)
    total = None
    for ref, weight in zip(refs, weights):
        part = dot_nt(ref[rows, :], weight[...])
        total = part if total is None else total + part
    return total


def input_other_kernel(wq, wk, wv, dq, dk, dv, *others):
    for j in range(2):
        block = 2 * j + 1 - position()[0]
        part = part_of((dq, dk, dv), (wq, wk, wv), block).astype(BF16)
        each = len(others) // 2
        for n, ref in enumerate(others[j * each : (j + 1) * each] if each else others):
            rows = slice(n * ref.shape[0], (n + 1) * ref.shape[0]) if each else slice(0, TILE)
            (ref if each else ref.at[j * TILE : (j + 1) * TILE, :])[...] = part[rows]


def input_mine_kernel(wq, wk, wv, dq, dk, dv, d0, d1, *refs):
    got, (here, away) = refs[:-2], refs[-2:]
    core, side = position()[:2]

    def chip(j):
        each = len(got) // 2
        if each:
            far = jnp.concatenate([ref[...].astype(F32) for ref in got[j * each : (j + 1) * each]], axis=0)
        else:
            far = got[0][j * TILE : (j + 1) * TILE, :].astype(F32)
        return part_of((dq, dk, dv), (wq, wk, wv), 2 * j + core) + far

    for mine, d in ((0, d0), (1, d1)):

        @pl.when(side == mine)
        def _():
            here[...] = chip(mine) + d[...]

        @pl.when(side != mine)
        def _():
            away[...] = chip(mine).astype(BF16)


def input_sum_kernel(here, got, out):
    out[...] = here[...] + got[...].astype(F32)


def halves(tall, bit, rows):
    size = (1 << bit[0]) * rows
    mine = (position()[2] >> bit[1]) & 1
    for n in range(tall // (2 * size)):
        for own, side in ((True, mine), (False, 1 - mine)):
            yield own, pl.ds(pl.multiple_of((2 * n + side) * size, size), size), slice(n * size, (n + 1) * size)


def transpose_halves(ref, out, at, bit, rows):
    here = slice(at, at + ref.shape[0])
    half = ref.shape[1] // 2
    size = (1 << bit[0]) * rows
    if size % 128:
        split = ref[...].T.reshape(half // size, 2, size, ref.shape[0])
        zero, one = split[:, 0].reshape(half, ref.shape[0]), split[:, 1].reshape(half, ref.shape[0])
        own = ((position()[2] >> bit[1]) & 1) == 0
        out[:half, here] = jnp.where(own, zero, one)
        out[half:, here] = jnp.where(own, one, zero)
        return
    for own, source, target in halves(ref.shape[1], bit, rows):
        first = target.start + (0 if own else half)
        size = target.stop - target.start
        out[first : first + size, here] = ref[:, source].T


def weight_grad_kernel(bit, rows, count, *refs):
    lefts, rights = refs[:count], refs[count : 2 * count]
    keep_ref, give_ref, left_t = refs[2 * count :]
    at = 0
    for ref in lefts:
        transpose_halves(ref, left_t, at, bit, rows)
        at += ref.shape[0]
    half = left_t.shape[0] // 2
    for first in range(0, keep_ref.shape[1], 256):
        cols = slice(first, first + 256)
        for out, side in ((keep_ref, slice(0, half)), (give_ref, slice(half, 2 * half))):
            total, at = None, 0
            for ref in rights:
                part = dot_nn(left_t[side, at : at + ref.shape[0]], ref[:, cols])
                total = part if total is None else total + part
                at += ref.shape[0]
            out[:, cols] = total.astype(BF16)


def weight_grad(order, name, lefts, rights, bit, ctx_count, waits=()):
    width, cols = lefts[0].shape[1], rights[0].shape[1]
    tall = sum(left.shape[0] for left in lefts)
    return call(
        order, name,
        functools.partial(weight_grad_kernel, (bit, bit), width // ctx_count, len(lefts)),
        [((width // 2, cols), BF16)] * 2, (*lefts, *rights),
        scratch=[pltpu.VMEM((width, tall), BF16)],
        waits=waits,
    )


SMALL = 8


def two_digits(small, width):
    flat = [small[:, at : at + width] for at in range(0, small.shape[1], width)]
    value = jnp.concatenate(flat, axis=0)
    upper = value.astype(BF16)
    return jnp.concatenate([upper, (value - upper.astype(F32)).astype(BF16)], axis=0)


def from_digits(rows, width):
    half = rows.shape[0] // 2
    value = rows[:half].astype(F32) + rows[half:].astype(F32)
    return jnp.concatenate([value[at : at + SMALL] for at in range(0, half, SMALL)], axis=1)


def groups_of(width):
    cuts = (0, *CUTS, 3 * width)
    return list(zip(cuts[:-1], cuts[1:]))


def small_width(group):
    return 512 if group >= 512 else 256


def small_rows(width, group):
    return 2 * SMALL * (width // small_width(group))


def qkv_grad_kernel(bits, rows, tokens, sums_own, sums_far, up_0, up_1, dq, dk, dv, *refs):
    width = dq.shape[1]
    groups = groups_of(width)
    outs, (small_ref, tok_t, *more) = refs[: 2 * len(groups)], refs[2 * len(groups) :]
    lefts = {bits[0]: tok_t}
    for bit in bits:
        if bit not in lefts:
            lefts[bit] = more[0]
    for bit, ref in lefts.items():
        transpose_halves(tokens, ref, 0, (bit, bit), rows)
    half = tok_t.shape[0] // 2
    small_ref[0:6, :] = sums_own[0:6, :] + sums_far[0:6, :]
    small_ref[6:7, :] = up_0[...] + up_1[...]
    small_ref[7:8, :] = jnp.zeros_like(small_ref[7:8, :])
    small_ref[7:8, :width] = jnp.sum(dq[...].astype(F32), axis=0, keepdims=True)
    small_ref[7:8, width : 2 * width] = jnp.sum(dv[...].astype(F32), axis=0, keepdims=True)
    put_small(outs[1], small_ref[...], half)
    for n, (low, high) in enumerate(groups):
        keep, give, left = outs[2 * n], outs[2 * n + 1], lefts[bits[n]]
        for which, ref in enumerate((dq, dk, dv)):
            first, last = max(low, which * width), min(high, (which + 1) * width)
            if first < last:
                right = ref[:, first - which * width : last - which * width]
                here = slice(first - low, last - low)
                give[:half, here] = dot_nn(left[half:, :], right).astype(BF16)
                keep[:, here] = dot_nn(left[:half, :], right).astype(BF16)


def put_small(give, small, tall):
    width = small_width(give.shape[1])
    give[tall:, :width] = two_digits(small, width)
    if give.shape[1] > width:
        give[tall:, width:] = jnp.zeros((give.shape[0] - tall, give.shape[1] - width), BF16)


def qkv_grad(order, tokens, sums, dq, dk, dv, bits, ctx_count):
    width, cols = tokens.shape[1], dq.shape[1]
    half = width // 2
    outs = []
    for n, (low, high) in enumerate(groups_of(cols)):
        extra = 0 if n else small_rows(width, high - low)
        outs += [((half, high - low), BF16), ((half + extra, high - low), BF16)]
    return call(
        order, "grad_qkv",
        functools.partial(qkv_grad_kernel, bits, width // ctx_count),
        outs + [((SMALL, width), F32)], (tokens, *sums, dq, dk, dv),
        scratch=[pltpu.VMEM(tokens.shape[::-1], BF16)] * len(set(bits)),
    )


def fold_rows(keep, got, bit, rows, keep_ref, give_ref):
    for own, source, target in halves(keep.shape[0], bit, rows):
        total = keep[source, :].astype(F32) + got[source, :].astype(F32)
        (keep_ref if own else give_ref)[target, :] = total.astype(BF16)


def small_sum(small, got, tall):
    width = small_width(got.shape[1])
    own = from_digits(two_digits(small[...], width), width)
    return own + from_digits(got[tall:, :width], width)


def fold_small_kernel(bit, rows, keep, small, got, keep_ref, give_ref, small_ref):
    tall = keep.shape[0]
    fold_rows(keep, got, bit, rows, keep_ref, give_ref)
    value = small_sum(small, got, tall)
    small_ref[...] = value
    put_small(give_ref, value, tall // 2)


def last_small_kernel(small, *refs):
    count = len(CUTS) + 1
    keeps, gots, outs, rows = refs[:count], refs[count : 2 * count], refs[2 * count : 2 * count + 3], refs[2 * count + 3 :]
    tall, width = outs[0].shape
    for n, (low, high) in enumerate(groups_of(width)):
        value = keeps[n][...].astype(F32) + gots[n][:tall, :].astype(F32)
        for which, out in enumerate(outs):
            first, last = max(low, which * width), min(high, (which + 1) * width)
            if first < last:
                out[:, first - which * width : last - which * width] = value[:, first - low : last - low]
    value = small_sum(small, gots[0], tall)
    for n, row in enumerate(rows[:7]):
        row[...] = value[n : n + 1, :]
    for n, row in enumerate(rows[7:]):
        row[...] = value[7:8, n * width : (n + 1) * width]


def fold_kernel(bit, rows, keep, got, keep_ref, give_ref):
    fold_rows(keep, got, bit, rows, keep_ref, give_ref)


def last_kernel(keep, got, out):
    out[...] = keep[...].astype(F32) + got[...].astype(F32)


class ScatterSum:
    def __init__(self, order, name, keep, give, bits, ctx_count, small=None):
        self.order, self.name, self.bits, self.small = order, name, bits, small
        self.left = list(range(ctx_count.bit_length() - 1))
        self.keep, self.give, self.done = keep, give, 0
        self.rows = keep.shape[0] * 2 // ctx_count

    def send(self):
        self.got = swap(self.give, CTX, 1 << self.bits[self.done])
        return self

    def rest(self):
        while self.done < len(self.bits) - 1:
            self.fold()
        return self

    def fold(self, waits=()):
        self.left.remove(self.bits[self.done])
        self.done += 1
        tall, width = self.keep.shape
        bit = self.bits[self.done]
        half = ((tall // 2, width), BF16)
        if self.small is not None:
            extra = self.got.shape[0] - tall
            self.keep, self.give, self.small = call(
                self.order, self.name,
                functools.partial(fold_small_kernel, (self.left.index(bit), bit), self.rows),
                [half, ((tall // 2 + extra, width), BF16), (self.small.shape, F32)],
                (self.keep, self.small, self.got), waits=waits,
            )
            return self.send()
        self.keep, self.give = call(
            self.order, self.name,
            functools.partial(fold_kernel, (self.left.index(bit), bit), self.rows),
            [half, half], (self.keep, self.got), waits=waits,
        )
        return self.send()

    def last(self):
        return call(
            self.order, self.name, last_kernel, [(self.keep.shape, F32)], (self.keep, self.got)
        )[0]


def swap(value, axis, mask):
    return lax.ppermute(value, axis, [(i, i ^ mask) for i in range(lax.axis_size(axis))])


def from_left(value, axis):
    return lax.ppermute(value, axis, [(i, i + 1) for i in range(lax.axis_size(axis) - 1)])


def from_right(value, axis):
    return lax.ppermute(value, axis, [(i + 1, i) for i in range(lax.axis_size(axis) - 1)])


def body(
    tokens, flags, w_query, w_key, w_value, w_out, w_up, w_down, bias_query, bias_value, bias_out,
    mid_gain, mid_bias, bias_up, bias_down, end_gain, end_bias, cotangent,
):
    rows, width = tokens.shape
    assert rows == 4 * TILE == 2 * MAXDOC
    ctx_count = lax.axis_size(CTX)
    bits = list(range(ctx_count.bit_length() - 1))
    turned = bits[1:] + bits[:1]
    order = Order()
    biases = [v[None] for v in (bias_out, mid_gain, mid_bias, bias_up, bias_down, end_gain, end_bias)]

    tokens, kv, to_left, to_right, seg, bounds = project_keys(
        order, tokens, w_key, w_value, bias_value[None], flags[None]
    )
    kv_low = from_left(to_right, CTX)
    queries, q_to_left, q_to_right = project_queries(order, tokens, w_query, bias_query[None])
    queries, w_out = lax.optimization_barrier((queries, w_out))
    w_far = swap(w_out, WT, 2)
    order.hold(tokens, kv, queries)
    local_0, shared = attention_local(order, 0, bounds, seg, queries, kv)
    order.hold(*local_0)
    local_1, _ = attention_local(order, 1, bounds, seg, queries, kv, shared)
    kv_low, to_left, *local_1 = lax.optimization_barrier((kv_low, to_left, *local_1))
    kv_high = from_right(to_left, CTX)
    order.hold(*local_1)
    w_diag = swap(w_far, WT, 1)

    att_0, lse_0, (mine, other), held = attention_edge(
        order, 0, bounds, seg, queries, local_0, kv_low, (w_out, w_up, w_down, cotangent, *biases)
    )
    order.free(*local_0)
    w_out, w_up, w_down, cotangent, bias_out, mid_gain, mid_bias, bias_up, bias_down, end_gain, end_bias = held
    w_core = swap(w_out, WT, 1)
    weights = (w_out, w_core, w_far, w_diag)
    order.hold(w_out, w_up, w_down, cotangent, att_0)
    pieces = (att_0, swap(other, WT, 1), swap(mine, WT, 2), swap(other, WT, 3))
    n_0, s_0, lo = mix(order, 0, tokens, pieces, weights, bias_out, mid_gain, mid_bias)
    order.hold(n_0, s_0)
    att_1, lse_1, _, _ = attention_edge(order, 1, bounds, seg, queries, local_1, kv_high)
    order.free(*local_1)
    order.hold(att_1)
    att_1, q_to_left, q_to_right = lax.optimization_barrier((att_1, q_to_left, q_to_right))
    q_low, q_high = from_left(q_to_right, CTX), from_right(q_to_left, CTX)
    att_far = swap(att_1, WT, 2)
    h_0, sl_0, low_0, part, parts = up_down(
        order, 0, (*lo, *swap_pieces(lo)), w_up, w_down, bias_up
    )
    order.hold(h_0, sl_0, low_0)
    picked = call(order, "far", pick_kernel, [((SPLIT, att_1.shape[1]), BF16)] * 4, (att_far,))
    chip_0 = chip_sum(order, "chip", part, parts, (q_low,))
    far_0 = swap(chip_0, WT, 2)
    pieces = (att_1, swap(att_1, WT, 1), att_far, *swap_pieces(picked))
    n_1, s_1, lo = mix(order, 1, tokens, pieces, weights, bias_out, mid_gain, mid_bias)
    h_1, sl_1, low_1, part, parts = up_down(order, 1, lo, w_up, w_down, bias_up)
    order.hold(n_1, s_1, h_1, sl_1, low_1)
    chip_1 = chip_sum(order, "chip", part, parts, (q_high,))
    far_1 = swap(chip_1, WT, 2)
    att, lse, normal, scale = (att_0, att_1), (lse_0, lse_1), (n_0, n_1), (s_0, s_1)
    hidden, slope, low, chip, far = (h_0, h_1), (sl_0, sl_1), (low_0, low_1), (chip_0, chip_1), (far_0, far_1)

    vectors = (mid_gain, mid_bias, bias_down, end_gain, end_bias)
    out, d_second_0, sums, lo = end(order, 0, normal[0], chip[0], far[0], cotangent, vectors, ())
    d_inner_0, up_sums_0, down_0, *part = down_up(order, 0, lo, swap_pieces(lo), w_down, w_up, slope[0])
    order.hold(d_second_0, d_inner_0, down_0)
    d_chip_0 = chip_sum(order, "chip", *part, (far[1],))
    d_far_0 = swap(d_chip_0, WT, 2)
    layer_out, d_second_1, end_sums, lo = end(
        order, 1, normal[1], chip[1], far[1], cotangent, vectors, (out, sums)
    )
    d_inner_1, up_sums_1, down_1, part, parts = down_up(
        order, 1, lo, swap_pieces(lo), w_down, w_up, slope[1]
    )
    order.hold(d_second_1, d_inner_1, down_1)
    order.free(w_up, w_down, *slope, cotangent)
    v = types.SimpleNamespace(d_sum=[], d=[], mixed=[], delta=[], lo=[])
    up_sums = (up_sums_0, up_sums_1)

    def first_1():
        v.d_chip = chip_sum(order, "chip", part, parts)
        v.d_far = swap(v.d_chip, WT, 2)

    def grad_down():
        way = turned if DOWN_TURNED else bits
        keep, give = weight_grad(order, "grad_down", (down_0, down_1), hidden, way[0], ctx_count)
        order.free(*hidden, down_0, down_1)
        v.down = ScatterSum(order, "fold_down", keep, give, way, ctx_count).send()

    def grad_up():
        way = turned if UP_TURNED else bits
        keep, give = weight_grad(order, "grad_up", low, (d_inner_0, d_inner_1), way[0], ctx_count)
        order.free(*low, d_inner_0, d_inner_1)
        v.up = ScatterSum(order, "fold_up", keep, give, way, ctx_count).send()

    def mid_0():
        d_sum, v.sums, lo = mid(
            order, 0, d_second_0, d_chip_0, d_far_0, normal[0], scale[0], mid_gain, end_sums
        )
        v.d_sum.append(d_sum)
        v.lo.append(lo)
        order.hold(d_sum)
        order.free(d_second_0, normal[0], scale[0])

    def mid_1():
        d_sum, v.sums, lo = mid(
            order, 1, d_second_1, v.d_chip, v.d_far, normal[1], scale[1], mid_gain, v.sums
        )
        v.d_sum.append(d_sum)
        v.lo.append(lo)
        order.hold(d_sum)
        order.free(d_second_1, normal[1], scale[1])

    def d_att_of(j):
        d, mixed, delta = d_att(order, j, v.lo[j], swap_pieces(v.lo[j]), w_out, att[j], lse[j])
        v.d.append(d)
        v.mixed.append(mixed)
        v.delta.append(delta)
        order.hold(d, mixed)
        if j == 0:
            v.d_high = from_right(d, CTX)
        else:
            v.d_low = from_left(d, CTX)

    def back_local():
        v.local = attention_back_local(order, bounds, seg, queries, kv, v.d, lse, v.delta)

    def grad_out(waits=()):
        way = turned if OUT_TURNED else bits
        keep, give = weight_grad(order, "grad_out", v.mixed, att, way[0], ctx_count, waits)
        order.free(*v.mixed, *att, w_out)
        v.out = ScatterSum(order, "fold_out", keep, give, way, ctx_count).send()

    def back_edge():
        *v.grads, v.wq, v.wk, v.wv = attention_back_edge(
            order, bounds, seg, queries, kv, v.d, lse, v.delta,
            (kv_low, kv_high), (q_low, q_high), (v.d_low, v.d_high), v.local, (w_query, w_key, w_value),
        )
        order.free(queries, kv, *v.d)
        order.hold(*v.grads, v.wq, v.wk, v.wv)

    def grad_qkv():
        sums = (v.sums, swap(v.sums, WT, 1), *up_sums)
        ways = [turned if t else bits for t in QKV_TURNED]
        *parts, small = qkv_grad(order, tokens, sums, *v.grads, tuple(way[0] for way in ways), ctx_count)
        order.free(tokens)
        order.hold(*parts[::2])
        v.qkv = [
            ScatterSum(order, "fold_qkv", keep, give, way, ctx_count, None if n else small).send()
            for n, (keep, give, way) in enumerate(zip(parts[::2], parts[1::2], ways))
        ]

    def input_other():
        parts = call(
            order, "input", input_other_kernel, [((rows, width), BF16) for rows in INPUT_SPLITS],
            (v.wq, v.wk, v.wv, *v.grads),
        )
        v.input_far = [swap(part, WT, 1) for part in parts]

    def input_mine():
        v.here, v.away = call(
            order, "input", input_mine_kernel, [((TILE, width), F32), ((TILE, width), BF16)],
            (v.wq, v.wk, v.wv, *v.grads, *v.d_sum, *v.input_far),
        )
        order.free(*v.grads, v.wq, v.wk, v.wv, *v.d_sum)
        order.hold(v.here)
        v.arriving = swap(v.away, WT, 2)

    def last_down():
        v.summed_down = v.down.rest().last()

    def last_out():
        v.summed_out = v.out.rest().last()

    def last_up():
        v.summed_up = v.up.rest().last()

    def input_last():
        (v.input_grad,) = call(order, "input", input_sum_kernel, [((TILE, width), F32)], (v.here, v.arriving))

    grad_down()
    grad_up()
    first_1()
    mid_0()
    d_att_of(0)
    mid_1()
    d_att_of(1)
    back_local()
    v.up.fold()
    v.down.fold()
    grad_out((v.d_low, v.d_high))
    back_edge()
    grad_qkv()
    v.out.fold()
    v.down.fold()
    input_other()
    v.up.fold()
    input_mine()
    v.out.fold()
    v.qkv[0].fold()
    v.qkv[1].fold()
    last_down()
    v.qkv[0].fold()
    v.qkv[1].fold()
    input_last()
    last_out()
    last_up()
    for part in v.qkv:
        part.rest()
    piece = (v.qkv[0].keep.shape[0], queries.shape[1])
    wide, narrow = ((1, width), F32), ((1, queries.shape[1]), F32)
    *summed, g_end_gain, g_end_bias, g_down, g_mid_gain, g_mid_bias, g_out, g_up, g_query, g_value = call(
        order, "sum", last_small_kernel, [(piece, F32)] * 3 + [wide] * 7 + [narrow] * 2,
        (v.qkv[0].small, *(part.keep for part in v.qkv), *(part.got for part in v.qkv)),
    )
    vectors = (g_query, g_value, g_out, g_mid_gain, g_mid_bias, g_up, g_down, g_end_gain, g_end_bias)
    return (
        layer_out, v.input_grad, *summed, v.summed_out, v.summed_up, v.summed_down, *(v.reshape(-1) for v in vectors)
    )


def solution(mesh):
    wt = P(None, WT)
    in_specs = (
        P(CTX, None), P(CTX), wt, wt, wt, wt, wt, wt, P(WT), P(WT),
        P(), P(), P(), P(WT), P(), P(), P(), P(CTX, None),
    )
    rows = P((CTX, WT), None)
    both = P(CTX, WT)
    out_specs = (
        rows, rows, both, both, both, both, both, both, P(WT), P(WT),
        P(), P(), P(), P(WT), P(), P(), P(),
    )
    return jax.shard_map(body, mesh=mesh, in_specs=in_specs, out_specs=out_specs, check_vma=False)
```
